32 devices in a mesh: section: 4 (over y, x), dp: 8 (over z, core).
Axes of the slice: x: 2, y: 2, z: 4, core: 2. Of those that a mesh axis runs over, the one named last changes fastest.
Arguments:
- frames: bfloat16 [32, 4, 128, 512], P('dp', 'section'), may hold values from -6 to 6
- lengths: int32 [32], P('dp'), may hold values from 1 to 4, as said below
- decay: float32 [2, 96], replicated, may hold values from 0.9 to 0.99
- read_gain: bfloat16 [2, 512], replicated, may hold values from 0.5 to 1.5
- read_weight: bfloat16 [2, 512, 16], replicated, may hold values from -0.25 to 0.25
- norm_attn: bfloat16 [2, 2, 512], replicated, may hold values from 0.5 to 1.5
- w_qkv: bfloat16 [2, 2, 512, 1536], replicated, may hold values from -0.25 to 0.25
- w_out: bfloat16 [2, 2, 512, 512], replicated, may hold values from -0.5 to 0.5
- norm_mlp: bfloat16 [2, 2, 512], replicated, may hold values from 0.5 to 1.5
- w_up: bfloat16 [2, 2, 512, 2048], replicated, may hold values from -0.25 to 0.25
- w_down: bfloat16 [2, 2, 2048, 512], replicated, may hold values from -0.125 to 0.125
- write_gain: bfloat16 [2, 512], replicated, may hold values from 0.5 to 1.5
- write_weight: bfloat16 [2, 512, 96], replicated, may hold values from -0.25 to 0.25
- cotangent: bfloat16 [32, 4, 16, 512], P('dp', 'section'), may hold values from -6 to 6
Outputs:
- result: bfloat16 [32, 4, 16, 512], P('dp', 'section')
- frames_grad: bfloat16 [32, 4, 128, 512], P('dp', 'section')
- read_gain_grad: float32 [2, 512], P(None, ('section', 'dp'))
- read_weight_grad: float32 [2, 512, 16], P(None, ('section', 'dp'))
- norm_attn_grad: float32 [2, 2, 512], P(None, None, ('section', 'dp'))
- w_qkv_grad: float32 [2, 2, 512, 1536], P(None, None, ('section', 'dp'))
- w_out_grad: float32 [2, 2, 512, 512], P(None, None, ('section', 'dp'))
- norm_mlp_grad: float32 [2, 2, 512], P(None, None, ('section', 'dp'))
- w_up_grad: float32 [2, 2, 512, 2048], P(None, None, ('section', 'dp'))
- w_down_grad: float32 [2, 2, 2048, 512], P(None, None, ('section', 'dp'))
- write_gain_grad: float32 [2, 512], P(None, ('section', 'dp'))
- write_weight_grad: float32 [2, 512, 96], P(None, ('section', 'dp'))
The draws below stay inside these ranges and needn't reach their ends.
Inputs may be any that keep to these rules, and one draw needn't show every extreme that they name: `lengths`: every index of dp holds, among its 4 clips, one clip of all 4 frames.
All inputs are finite; a program needn't handle non-finite values.
Results may differ from the reference program's by a relative error of at most 0.028.
Values may be sent and summed in bfloat16 or wider, within the bound.
A program may use at most 1 GiB of HBM per device.

```python
import jax
import jax.numpy as jnp
from jax import lax

D = 512
HEADS = 8
HEAD = 64
FF = 2048
MEM = 96
READ = 16
BLOCKS = 2
LAYERS = 2
TOK_FRAME = 128
CLIP_DEV = 4
CLIPS = 32
FRAMES = 4


def draw_lengths(key, part):
    key = jax.random.fold_in(key, 7)
    length_key, pick_key = jax.random.split(key)
    drawn_lengths = jax.random.randint(length_key, (CLIPS,), 1, FRAMES + 1)
    chosen_slot = jax.random.randint(pick_key, (CLIPS // CLIP_DEV,), 0, CLIP_DEV)
    slot_index = jnp.arange(CLIPS) % CLIP_DEV
    owner_index = jnp.arange(CLIPS) // CLIP_DEV
    full_clip = slot_index == chosen_slot[owner_index]
    return jnp.where(full_clip, FRAMES, drawn_lengths).astype(jnp.int32)


def steps_of(rng, dims, pieces, least, largest):
    level = 1.0
    for axis_at, blocks in pieces:
        heights = jax.random.uniform(jax.random.fold_in(jax.random.fold_in(rng, 6), axis_at), (blocks,), jnp.float32, least / len(pieces), largest / len(pieces))
        level = level * jnp.repeat(jnp.exp(heights), dims[axis_at] // blocks).reshape((-1,) + (1,) * (len(dims) - 1 - axis_at))
    return level


def noise(own_key, extent, scale, limit, cuts=(), kind=jnp.bfloat16):
    factor_of = steps_of(own_key, extent, cuts, -0.22, 0.18) if cuts else 1.0
    drawn = jax.random.normal(own_key, extent, jnp.float32) * scale * factor_of
    return jnp.minimum(jnp.maximum(drawn, -limit), limit).astype(kind)


def setup_inputs(seed: int = 0) -> dict:
    key_of = jax.random.split(jax.random.key(seed), 15)
    return {
        "frames": noise(key_of[0], (CLIPS, FRAMES, TOK_FRAME, D), 1.0, 6.0, ((0, 8), (1, 4))),
        "lengths": draw_lengths(jax.random.fold_in(key_of[14], 71), 0),
        "decay": jnp.clip(jax.random.uniform(key_of[2], (LAYERS, MEM), jnp.float32, 0.9, 0.99), 0.9, 0.99),
        "read_gain": jnp.clip(1.0 + 0.1 * jax.random.normal(key_of[3], (LAYERS, D), jnp.float32), 0.5, 1.5).astype(jnp.bfloat16),
        "read_weight": noise(key_of[4], (LAYERS, D, READ), D ** -0.5, 0.25),
        "norm_attn": jnp.clip(1.0 + 0.1 * jax.random.normal(key_of[5], (LAYERS, BLOCKS, D), jnp.float32), 0.5, 1.5).astype(jnp.bfloat16),
        "w_qkv": noise(key_of[6], (LAYERS, BLOCKS, D, 3 * D), D ** -0.5, 0.25),
        "w_out": noise(key_of[7], (LAYERS, BLOCKS, D, D), (D // 4) ** -0.5, 0.5),
        "norm_mlp": jnp.clip(1.0 + 0.1 * jax.random.normal(key_of[8], (LAYERS, BLOCKS, D), jnp.float32), 0.5, 1.5).astype(jnp.bfloat16),
        "w_up": noise(key_of[9], (LAYERS, BLOCKS, D, FF), D ** -0.5, 0.25),
        "w_down": noise(key_of[10], (LAYERS, BLOCKS, FF, D), FF ** -0.5, 0.125),
        "write_gain": jnp.clip(1.0 + 0.1 * jax.random.normal(key_of[11], (LAYERS, D), jnp.float32), 0.5, 1.5).astype(jnp.bfloat16),
        "write_weight": noise(key_of[12], (LAYERS, D, MEM), D ** -0.5, 0.25),
        "cotangent": noise(key_of[13], (CLIPS, FRAMES, READ, D), 1.0, 6.0, ((0, 8), (1, 4))),
    }


@jax.custom_vjp
def low(v):
    return lax.optimization_barrier(v.astype(jnp.bfloat16)).astype(jnp.float32)

@jax.custom_vjp
def low_back(v):
    return v

def low_keep(v):
    return (low(v), None)

def low_pass(kept, grad):
    return (grad,)

def back_keep(v):
    return (v, None)

def back_low(kept, grad):
    return (low(grad),)
low.defvjp(low_keep, low_pass)
low_back.defvjp(back_keep, back_low)

def rounded(values):
    return low_back(low(values))

def product(form, left, right):
    return jnp.einsum(form, left, right, precision=lax.Precision.HIGHEST)

def layer_norm(values, gain):
    centred = values - lax.optimization_barrier(jnp.mean(values, axis=-1, keepdims=True))
    spread = lax.optimization_barrier(jnp.mean(centred * centred, axis=-1, keepdims=True))
    return centred * lax.rsqrt(spread + 1e-05) * gain

def processor(weights, layer_index, tokens):
    norm_attn, w_qkv, w_out, norm_mlp, w_up, w_down = weights[2:8]
    clip_count, token_count, width = tokens.shape
    hidden_state = tokens
    for block_index in range(BLOCKS):
        normed = rounded(layer_norm(hidden_state, norm_attn[layer_index, block_index]))
        joined = rounded(product('brd,de->bre', normed, w_qkv[layer_index, block_index]))
        joined = joined.reshape(clip_count, token_count, 3, HEADS, HEAD)
        queries, keys_all, values_all = (joined[:, :, 0], joined[:, :, 1], joined[:, :, 2])
        scores = product('bqhe,bkhe->bhqk', queries, keys_all) * HEAD ** (-0.5)
        soft_weights = rounded(jax.nn.softmax(scores, axis=-1))
        attended = product('bhqk,bkhe->bqhe', soft_weights, values_all).reshape(clip_count, token_count, width)
        hidden_state = hidden_state + product('brd,de->bre', rounded(attended), w_out[layer_index, block_index])
        normed = rounded(layer_norm(hidden_state, norm_mlp[layer_index, block_index]))
        lifted = rounded(jax.nn.gelu(product('brd,df->brf', normed, w_up[layer_index, block_index]), approximate=True))
        hidden_state = hidden_state + product('brf,fd->brd', lifted, w_down[layer_index, block_index])
    return hidden_state

def layer_step(weights, layer_index, decay, memory, inputs_low, live_mask):
    read_gain, read_weight = (weights[0], weights[1])
    write_gain, write_weight = (weights[8], weights[9])
    memory_low = rounded(memory)
    gathered = jnp.concatenate([memory_low, inputs_low], axis=1)
    normed = rounded(layer_norm(gathered, read_gain[layer_index]))
    read_soft = rounded(jax.nn.softmax(product('bnd,dr->bnr', normed, read_weight[layer_index]), axis=1))
    summary = product('bnr,bnd->brd', read_soft, gathered)
    result_low = rounded(processor(weights, layer_index, summary))
    pooled = jnp.concatenate([memory_low, result_low, inputs_low], axis=1)
    normed_pool = rounded(layer_norm(pooled, write_gain[layer_index]))
    write_soft = rounded(jax.nn.softmax(product('bnd,dm->bnm', normed_pool, write_weight[layer_index]), axis=1))
    written = product('bnm,bnd->bmd', write_soft, pooled)
    rate = decay[layer_index][None, :, None]
    updated = rate * memory_low + (1.0 - rate) * written
    keep = live_mask[:, None, None]
    return (keep * updated + (1.0 - keep) * memory, keep * result_low)

def run_frames(weights, decay, memory, frame_values, live_mask):

    def frame_step(carry, sliced):
        tokens, alive_now = sliced
        current = rounded(tokens)
        new_memory = []
        for layer_index in range(LAYERS):
            updated, current = layer_step(weights, layer_index, decay, carry[layer_index], current, alive_now)
            new_memory.append(updated)
        return (jnp.stack(new_memory), current)
    final, outputs = lax.scan(jax.checkpoint(frame_step), memory, (jnp.swapaxes(frame_values, 0, 1), jnp.swapaxes(live_mask, 0, 1)))
    return (jnp.swapaxes(outputs, 0, 1), final)

def reference(frames, lengths, decay, read_gain, read_weight, norm_attn, w_qkv, w_out, norm_mlp, w_up, w_down, write_gain, write_weight, cotangent):
    weights_full = tuple((w.astype(jnp.float32) for w in (read_gain, read_weight, norm_attn, w_qkv, w_out, norm_mlp, w_up, w_down, write_gain, write_weight)))
    frame_index = jnp.arange(FRAMES, dtype=jnp.int32)
    groups = CLIPS // CLIP_DEV

    def group_step(totals, sliced):
        group_frames, group_lengths, group_cot = sliced
        live_mask = (frame_index[None, :] < group_lengths[:, None]).astype(jnp.float32)
        start = jnp.zeros((LAYERS, group_frames.shape[0], MEM, D), jnp.float32)

        def forward(weight_tuple, frame_values):
            return run_frames(weight_tuple, decay, start, frame_values, live_mask)[0]
        outputs, pullback = jax.vjp(forward, weights_full, group_frames.astype(jnp.float32))
        weight_grads, frame_grads = pullback(group_cot.astype(jnp.float32))
        totals = jax.tree.map(jnp.add, totals, weight_grads)
        return (totals, (outputs.astype(jnp.bfloat16), frame_grads.astype(jnp.bfloat16)))
    zeros_tuple = tuple((jnp.zeros_like(w) for w in weights_full))
    totals, (outputs, frame_grads) = lax.scan(group_step, zeros_tuple, (frames.reshape(groups, CLIP_DEV, FRAMES, TOK_FRAME, D), lengths.reshape(groups, CLIP_DEV), cotangent.reshape(groups, CLIP_DEV, FRAMES, READ, D)))
    return (outputs.reshape(CLIPS, FRAMES, READ, D), frame_grads.reshape(CLIPS, FRAMES, TOK_FRAME, D), totals[0], totals[1], totals[2], totals[3], totals[4], totals[5], totals[6], totals[7], totals[8], totals[9])
```

```python
import jax
import jax.numpy as jnp
from jax import lax
from jax.experimental import pallas as pl
from jax.experimental.pallas import tpu as pltpu
from jax.sharding import PartitionSpec as P

HEADS = 8
HEAD = 64
MEM = 96
READ = 16
BLOCKS = 2
LAYERS = 2
EPS = 1e-05
BF = jnp.bfloat16
F32 = jnp.float32


def nn(a, b):
    return lax.dot_general(a, b, (((1,), (0,)), ((), ())), preferred_element_type=F32)


def nt(a, b):
    return lax.dot_general(a, b, (((1,), (1,)), ((), ())), preferred_element_type=F32)


def tn(a, b):
    return lax.dot_general(a, b, (((0,), (0,)), ((), ())), preferred_element_type=F32)


def normalize(v):
    centred = v - jnp.mean(v, axis=-1, keepdims=True)
    spread = jnp.mean(centred * centred, axis=-1, keepdims=True)
    r = lax.rsqrt(spread + EPS)
    return centred * r, r


def normalize_back(dx, xh, r):
    return r * (dx - jnp.mean(dx, axis=-1, keepdims=True) - xh * jnp.mean(dx * xh, axis=-1, keepdims=True))


def softmax_lanes(v):
    e = jnp.exp(v - jnp.max(v, axis=1, keepdims=True))
    return e / jnp.sum(e, axis=1, keepdims=True)


def softmax_lanes_back(p, dp):
    return p * (dp - jnp.sum(p * dp, axis=1, keepdims=True))


def chain_kernel(
    len_ref, frames_ref, cot_ref, dec_ref, gain_ref, small_ref, wqkv_hbm, wout_hbm, wup_hbm, wdown_hbm,
    res_ref, fgrad_ref, fa_g, fa_qkv, fa_o, fa_h1, fa_u, fa_up, fa_lift, fa_h2, dgain_ref, dsmall_ref,
    wqkv, wout, wup, wdown, z0, z1, xh0, xh1, rs0, rs1, at0, at1, bt0, bt1,
    mem, dmem, dout, xa, ra, xm, rm, gp, qkv, pt, mask_ref, sems,
):
    frames, tok, width = frames_ref.shape

    def weight_copies(lb):
        pairs = ((wqkv_hbm, wqkv), (wout_hbm, wout), (wup_hbm, wup), (wdown_hbm, wdown))
        return [pltpu.make_async_copy(s.at[lb], d.at[lb], sems.at[lb, i]) for i, (s, d) in enumerate(pairs)]

    for lb in range(LAYERS * BLOCKS):
        for c in weight_copies(lb):
            c.start()

    row = lax.broadcasted_iota(jnp.int32, (HEADS * READ, width), 0) // READ
    col = lax.broadcasted_iota(jnp.int32, (HEADS * READ, width), 1) // HEAD
    mask_ref[...] = jnp.where(row == col, 1.0, 0.0).astype(BF)
    dgain_ref[...] = jnp.zeros_like(dgain_ref)
    dsmall_ref[...] = jnp.zeros_like(dsmall_ref)

    def spread_heads(v):
        return jnp.concatenate([v] * HEADS, axis=0) * mask_ref[...]

    def gather_heads(v):
        return jnp.sum((v * mask_ref[...].astype(F32)).reshape(HEADS, READ, width), axis=0)

    def live_at(f):
        return jnp.where(f < len_ref[0], 1.0, 0.0).astype(F32)

    def gain(i):
        return gain_ref[i:i + 1, :]

    def block_forward(lb, f, h):
        xh, r = normalize(h)
        xa[lb, f], ra[lb, f] = xh, r
        g = (xh * gain(2 + lb)).astype(BF)
        fa_g[lb, f] = g
        joined = nn(g, wqkv[lb]).astype(BF)
        qkv[lb, f] = joined
        q, k, v = joined[:, :width], joined[:, width:2 * width], joined[:, 2 * width:]
        s = nt(k, spread_heads(q)) * HEAD ** (-0.5)
        e = jnp.exp(s - jnp.max(s, axis=0, keepdims=True))
        p = e / jnp.sum(e, axis=0, keepdims=True)
        pt[lb, f] = p
        o = gather_heads(tn(p.astype(BF), v)).astype(BF)
        fa_o[lb, f] = o
        h = h + nn(o, wout[lb])
        xh, r = normalize(h)
        xm[lb, f], rm[lb, f] = xh, r
        u = (xh * gain(6 + lb)).astype(BF)
        fa_u[lb, f] = u
        x = nn(u, wup[lb])
        c0, c1 = 0.7978845608028654, 0.044715
        x2 = x * x
        t = jnp.tanh(c0 * x * (1.0 + c1 * x2))
        lift = (0.5 * x * (1.0 + t)).astype(BF)
        gp[lb, f] = 0.5 * (1.0 + t) + 0.5 * x * (1.0 - t * t) * c0 * (1.0 + 3.0 * c1 * x2)
        fa_lift[lb, f] = lift
        return h + nn(lift, wdown[lb])

    def block_backward(lb, f, dh):
        dhb = dh.astype(BF)
        fa_h2[lb, f] = dhb
        dup = (nt(dhb, wdown[lb]) * gp[lb, f]).astype(BF)
        fa_up[lb, f] = dup
        du = nt(dup, wup[lb])
        xh = xm[lb, f]
        dgain_ref[6 + lb:7 + lb, :] += jnp.sum(du * xh, axis=0, keepdims=True)
        dh = dh + normalize_back(du * gain(6 + lb), xh, rm[lb, f])
        dhb = dh.astype(BF)
        fa_h1[lb, f] = dhb
        do = spread_heads(nt(dhb, wout[lb]).astype(BF))
        joined = qkv[lb, f]
        q, k, v = joined[:, :width], joined[:, width:2 * width], joined[:, 2 * width:]
        p = pt[lb, f]
        dp = nt(v, do)
        ds = (p * (dp - jnp.sum(p * dp, axis=0, keepdims=True)) * HEAD ** (-0.5)).astype(BF)
        dv = nn(p.astype(BF), do)
        dk = nn(ds, spread_heads(q))
        dq = gather_heads(tn(ds, k))
        dj = jnp.concatenate([dq, dk, dv], axis=1).astype(BF)
        fa_qkv[lb, f] = dj
        dg = nt(dj, wqkv[lb])
        xh = xa[lb, f]
        dgain_ref[2 + lb:3 + lb, :] += jnp.sum(dg * xh, axis=0, keepdims=True)
        return dh + normalize_back(dg * gain(2 + lb), xh, ra[lb, f])

    def layer_forward(l, f, z, xh_ref, rs_ref, at, bt, inputs):
        live = live_at(f)
        m = mem[...]
        rows = z.shape[1] - READ
        n_in = rows - MEM
        z[f, :n_in] = inputs
        z[f, n_in:rows] = m.astype(BF)
        zz = z[f, :rows]
        xh, r = normalize(zz.astype(F32))
        xh_ref[f, :rows], rs_ref[f, :rows] = xh, r
        n = (xh * gain(l)).astype(BF)
        a = softmax_lanes(nt(small_ref[l, :READ], n))
        at[f] = a
        h = nn(a.astype(BF), zz)
        for b in range(BLOCKS):
            h = block_forward(l * BLOCKS + b, f, h)
        y = h.astype(BF)
        z[f, rows:] = y
        xh, r = normalize(y.astype(F32))
        xh_ref[f, rows:], rs_ref[f, rows:] = xh, r
        n = (xh_ref[f] * gain(10 + l)).astype(BF)
        b = softmax_lanes(nt(small_ref[l, READ:], n))
        bt[f] = b
        written = nn(b.astype(BF), z[f])
        rate = dec_ref[l]
        updated = rate * z[f, n_in:rows].astype(F32) + (1.0 - rate) * written
        mem[...] = live * updated + (1.0 - live) * m
        return (live * y.astype(F32)).astype(BF)

    def layer_backward(l, f, z, xh_ref, rs_ref, at, bt, dy_out):
        live = live_at(f)
        rows = z.shape[1] - READ
        n_in = rows - MEM
        dm = dmem[...]
        rate = dec_ref[l]
        dt = ((live * (1.0 - rate)) * dm).astype(BF)
        zf = z[f]
        b = bt[f]
        dl = softmax_lanes_back(b, nt(dt, zf)).astype(BF)
        dz = tn(b.astype(BF), dt)
        dn = tn(dl, small_ref[l, READ:])
        xh = xh_ref[f]
        dsmall_ref[l, READ:] += nn(dl, (xh * gain(10 + l)).astype(BF))
        dgain_ref[10 + l:11 + l, :] += jnp.sum(dn * xh, axis=0, keepdims=True)
        dx = dn * gain(10 + l)
        dy = dz[rows:] + normalize_back(dx[rows:], xh[rows:], rs_ref[f, rows:]) + live * dy_out
        dh = dy.astype(BF).astype(F32)
        for bb in range(BLOCKS - 1, -1, -1):
            dh = block_backward(l * BLOCKS + bb, f, dh)
        ds = dh.astype(BF)
        xh = xh[:rows]
        a = at[f]
        dl = softmax_lanes_back(a, nt(ds, zf[:rows])).astype(BF)
        dz = dz[:rows] + tn(a.astype(BF), ds)
        dn = tn(dl, small_ref[l, :READ])
        dsmall_ref[l, :READ] += nn(dl, (xh * gain(l)).astype(BF))
        dgain_ref[l:l + 1, :] += jnp.sum(dn * xh, axis=0, keepdims=True)
        dz = dz + normalize_back(dx[:rows] + dn * gain(l), xh, rs_ref[f, :rows])
        dmq = (dz[n_in:] + (live * rate) * dm).astype(BF).astype(F32)
        dmem[...] = dmq + (1.0 - live) * dm
        return dz[:n_in].astype(BF)

    kept0 = (z0, xh0, rs0, at0, bt0)
    kept1 = (z1, xh1, rs1, at1, bt1)

    def wait_layer(l):
        for b in range(BLOCKS):
            for c in weight_copies(l * BLOCKS + b):
                c.wait()

    wait_layer(0)
    mem[...] = jnp.zeros_like(mem)

    def forward0(f, carry):
        dout[f] = layer_forward(0, f, *kept0, frames_ref[f])
        return carry

    lax.fori_loop(0, frames, forward0, 0)
    wait_layer(1)
    mem[...] = jnp.zeros_like(mem)

    def forward1(f, carry):
        res_ref[f] = layer_forward(1, f, *kept1, dout[f])
        return carry

    lax.fori_loop(0, frames, forward1, 0)
    dmem[...] = jnp.zeros_like(dmem)

    def backward1(i, carry):
        f = frames - 1 - i
        dout[f] = layer_backward(1, f, *kept1, cot_ref[f].astype(F32))
        return carry

    lax.fori_loop(0, frames, backward1, 0)
    dmem[...] = jnp.zeros_like(dmem)

    def backward0(i, carry):
        f = frames - 1 - i
        fgrad_ref[f] = layer_backward(0, f, *kept0, dout[f].astype(F32))
        return carry

    lax.fori_loop(0, frames, backward0, 0)


def run_chain(length, frames, cot, decay, gains, small, wqkv, wout, wup, wdown):
    count, tok, width = frames.shape
    lbs = LAYERS * BLOCKS
    ff = wup.shape[-1]
    vm, anym = pl.BlockSpec(memory_space=pltpu.VMEM), pl.BlockSpec(memory_space=pl.ANY)

    def per(cols, dtype):
        return (lbs, count, READ, cols), dtype

    def sds(shape, dtype):
        return jax.ShapeDtypeStruct(shape, dtype)

    factor_cols = (width, 3 * width, width, width, width, ff, ff, width)
    out_shape = [sds((count, READ, width), BF), sds((count, tok, width), BF)]
    out_shape += [sds(*per(c, BF)) for c in factor_cols]
    out_shape += [sds(gains.shape, F32), sds(small.shape, F32)]
    rows0, rows1 = tok + MEM, READ + MEM
    v = pltpu.VMEM
    scratch = [v(w.shape, BF) for w in (wqkv, wout, wup, wdown)]
    scratch += [v((count, r + READ, width), BF) for r in (rows0, rows1)]
    scratch += [v((count, r + READ, width), F32) for r in (rows0, rows1)]
    scratch += [v((count, r + READ, 1), F32) for r in (rows0, rows1)]
    scratch += [v((count, READ, r), F32) for r in (rows0, rows1)]
    scratch += [v((count, MEM, r + READ), F32) for r in (rows0, rows1)]
    scratch += [v((MEM, width), F32), v((MEM, width), F32), v((count, READ, width), BF)]
    scratch += [v(*per(width, F32)), v(*per(1, F32)), v(*per(width, F32)), v(*per(1, F32))]
    scratch += [v(*per(ff, F32)), v(*per(3 * width, BF)), v(*per(HEADS * READ, F32))]
    scratch += [v((HEADS * READ, width), BF), pltpu.SemaphoreType.DMA((lbs, 4))]
    return pl.pallas_call(
        chain_kernel,
        out_shape=out_shape,
        in_specs=[pl.BlockSpec(memory_space=pltpu.SMEM)] + [vm] * 5 + [anym] * 4,
        out_specs=[vm] * len(out_shape),
        scratch_shapes=scratch,
        compiler_params=pltpu.CompilerParams(vmem_limit_bytes=60 * 2**20),
    )(length, frames, cot, decay, gains, small, wqkv, wout, wup, wdown)


def local(
    frames, lengths, decay, read_gain, read_weight, norm_attn, w_qkv, w_out, norm_mlp, w_up, w_down,
    write_gain, write_weight, cotangent,
):
    sections = lax.axis_size("section")
    clip_dev, span, tok, width = frames.shape
    lbs = LAYERS * BLOCKS
    assert clip_dev == sections and span == 1
    both = jnp.concatenate([frames[:, 0], cotangent[:, 0]], axis=1)
    both = lax.all_to_all(both, "section", 0, 0, tiled=True)
    length = lax.dynamic_slice_in_dim(lengths, lax.axis_index("section"), 1, 0)
    gains = jnp.concatenate(
        [read_gain, norm_attn.reshape(lbs, width), norm_mlp.reshape(lbs, width), write_gain], axis=0
    ).astype(F32)
    small = jnp.swapaxes(jnp.concatenate([read_weight, write_weight], axis=2), 1, 2)
    weights = [w.reshape(lbs, *w.shape[2:]) for w in (w_qkv, w_out, w_up, w_down)]
    res, fgrad, g, dqkv, o, dh1, u, dup, lift, dh2, dgain, dsmall = run_chain(
        length, both[:, :tok], both[:, tok:], decay[:, :, None], gains, small, *weights
    )
    back = lax.all_to_all(jnp.concatenate([fgrad, res], axis=1), "section", 0, 0, tiled=True)

    def weight_grad(left, right):
        a = left.reshape(lbs, -1, left.shape[-1])
        b = right.reshape(lbs, -1, right.shape[-1])
        grad = jnp.einsum("lrd,lre->lde", a, b, preferred_element_type=F32).astype(BF)
        return grad.reshape(LAYERS, BLOCKS, *grad.shape[1:])

    def summed(v, axis):
        out = lax.psum_scatter(v, ("section", "dp"), scatter_dimension=axis, tiled=True)
        return out.astype(F32)

    dgain = summed(dgain, 1)
    dsmall = jnp.swapaxes(summed(dsmall, 2), 1, 2)
    return (
        back[:, None, tok:],
        back[:, None, :tok],
        dgain[:2],
        dsmall[:, :, :READ],
        dgain[2:6].reshape(LAYERS, BLOCKS, -1),
        summed(weight_grad(g, dqkv), 2),
        summed(weight_grad(o, dh1), 2),
        dgain[6:10].reshape(LAYERS, BLOCKS, -1),
        summed(weight_grad(u, dup), 2),
        summed(weight_grad(lift, dh2), 2),
        dgain[10:],
        dsmall[:, :, READ:],
    )


def solution(mesh):
    both = ("section", "dp")
    split = P("dp", "section", None, None)
    return jax.shard_map(
        local,
        mesh=mesh,
        in_specs=(split, P("dp")) + (P(),) * 11 + (split,),
        out_specs=(
            split, split, P(None, both), P(None, both, None), P(None, None, both), P(None, None, both, None),
            P(None, None, both, None), P(None, None, both), P(None, None, both, None),
            P(None, None, both, None), P(None, both), P(None, both, None),
        ),
        check_vma=False,
    )
```

```python
import functools

import jax
import jax.numpy as jnp
from jax import lax
from jax.experimental import pallas as pl
from jax.experimental.pallas import tpu as pltpu
from jax.sharding import PartitionSpec as P

HEADS = 8
HEAD = 64
MEM = 96
READ = 16
BLOCKS = 2
LAYERS = 2
EPS = 1e-05
SMALL = 128
TILE = 16
BF = jnp.bfloat16
F32 = jnp.float32


def nn(a, b):
    return lax.dot_general(a, b, (((1,), (0,)), ((), ())), preferred_element_type=F32)


def nt(a, b):
    return lax.dot_general(a, b, (((1,), (1,)), ((), ())), preferred_element_type=F32)


def tn(a, b):
    return lax.dot_general(a, b, (((0,), (0,)), ((), ())), preferred_element_type=F32)


def normalize(v):
    centred = v - jnp.mean(v, axis=-1, keepdims=True)
    spread = jnp.mean(centred * centred, axis=-1, keepdims=True)
    r = lax.rsqrt(spread + EPS)
    return centred * r, r


def normalize_back(dx, xh, r):
    return r * (dx - jnp.mean(dx, axis=-1, keepdims=True) - xh * jnp.mean(dx * xh, axis=-1, keepdims=True))


def softmax_lanes(v):
    e = jnp.exp(v - jnp.max(v, axis=1, keepdims=True))
    return e / jnp.sum(e, axis=1, keepdims=True)


def softmax_lanes_back(p, dp):
    return p * (dp - jnp.sum(p * dp, axis=1, keepdims=True))


def chain_kernel(
    len_ref, frames_ref, cot_ref, dec_ref, gain_ref, small_ref, wqkv_hbm, wout_hbm, wup_hbm, wdown_hbm,
    res_ref, fgrad_ref, gath_f, slice_f, gath_b, slice_b, dsm_ref,
    wqkv, wout, wup, wdown, z0, z1, xh0, xh1, rs0, rs1, at0, at1, bt0, bt1,
    mem, dmem, dout, xa, ra, xm, rm, gp, qkv, pt, mask_ref, sems,
):
    frames, tok, width = frames_ref.shape

    def weight_copies(lb):
        pairs = ((wqkv_hbm, wqkv), (wout_hbm, wout), (wup_hbm, wup), (wdown_hbm, wdown))
        return [pltpu.make_async_copy(s.at[lb], d.at[lb], sems.at[lb, i]) for i, (s, d) in enumerate(pairs)]

    for lb in range(LAYERS * BLOCKS):
        for c in weight_copies(lb):
            c.start()

    row = lax.broadcasted_iota(jnp.int32, (HEADS * READ, width), 0) // READ
    col = lax.broadcasted_iota(jnp.int32, (HEADS * READ, width), 1) // HEAD
    mask_ref[...] = jnp.where(row == col, 1.0, 0.0).astype(BF)
    dsm_ref[...] = jnp.zeros_like(dsm_ref)
    parts = slice_f.shape[1]

    def spread_heads(v):
        return jnp.concatenate([v] * HEADS, axis=0) * mask_ref[...]

    def gather_heads(v):
        return jnp.sum((v * mask_ref[...].astype(F32)).reshape(HEADS, READ, width), axis=0)

    def live_at(f):
        return jnp.where(f < len_ref[0], 1.0, 0.0).astype(F32)

    def keep_slices(ref, lb, f, first, v):
        cols = v.shape[1] // parts
        for s in range(parts):
            ref[lb, s, f, :, first:first + cols] = v[:, s * cols:(s + 1) * cols]

    def add_gain_grad(l, i, v):
        dsm_ref[l, READ + MEM + i:READ + MEM + i + 1, :] += jnp.sum(v, axis=0, keepdims=True)

    def gain(i):
        return gain_ref[i:i + 1, :]

    def block_forward(lb, f, h):
        xh, r = normalize(h)
        xa[lb, f], ra[lb, f] = xh, r
        g = (xh * gain(2 + lb)).astype(BF)
        gath_f[lb, f, :, :width] = g
        joined = nn(g, wqkv[lb]).astype(BF)
        qkv[lb, f] = joined
        q, k, v = joined[:, :width], joined[:, width:2 * width], joined[:, 2 * width:]
        s = nt(k, spread_heads(q)) * HEAD ** (-0.5)
        e = jnp.exp(s - jnp.max(s, axis=0, keepdims=True))
        p = e / jnp.sum(e, axis=0, keepdims=True)
        pt[lb, f] = p
        o = gather_heads(tn(p.astype(BF), v)).astype(BF)
        gath_f[lb, f, :, width:2 * width] = o
        h = h + nn(o, wout[lb])
        xh, r = normalize(h)
        xm[lb, f], rm[lb, f] = xh, r
        u = (xh * gain(6 + lb)).astype(BF)
        gath_f[lb, f, :, 2 * width:] = u
        x = nn(u, wup[lb])
        c0, c1 = 0.7978845608028654, 0.044715
        x2 = x * x
        t = jnp.tanh(c0 * x * (1.0 + c1 * x2))
        lift = (0.5 * x * (1.0 + t)).astype(BF)
        gp[lb, f] = 0.5 * (1.0 + t) + 0.5 * x * (1.0 - t * t) * c0 * (1.0 + 3.0 * c1 * x2)
        keep_slices(slice_f, lb, f, 0, lift)
        return h + nn(lift, wdown[lb])

    def block_backward(lb, f, dh):
        dhb = dh.astype(BF)
        gath_b[lb, f] = dhb
        dup = (nt(dhb, wdown[lb]) * gp[lb, f]).astype(BF)
        keep_slices(slice_b, lb, f, width, dup)
        du = nt(dup, wup[lb])
        xh = xm[lb, f]
        add_gain_grad(lb // BLOCKS, 3 + lb % BLOCKS, du * xh)
        dh = dh + normalize_back(du * gain(6 + lb), xh, rm[lb, f])
        dhb = dh.astype(BF)
        keep_slices(slice_b, lb, f, 3 * width // parts, dhb)
        do = spread_heads(nt(dhb, wout[lb]).astype(BF))
        joined = qkv[lb, f]
        q, k, v = joined[:, :width], joined[:, width:2 * width], joined[:, 2 * width:]
        p = pt[lb, f]
        dp = nt(v, do)
        ds = (p * (dp - jnp.sum(p * dp, axis=0, keepdims=True)) * HEAD ** (-0.5)).astype(BF)
        dv = nn(p.astype(BF), do)
        dk = nn(ds, spread_heads(q))
        dq = gather_heads(tn(ds, k))
        dj = jnp.concatenate([dq, dk, dv], axis=1).astype(BF)
        keep_slices(slice_b, lb, f, 0, dj)
        dg = nt(dj, wqkv[lb])
        xh = xa[lb, f]
        add_gain_grad(lb // BLOCKS, 1 + lb % BLOCKS, dg * xh)
        return dh + normalize_back(dg * gain(2 + lb), xh, ra[lb, f])

    def layer_forward(l, f, z, xh_ref, rs_ref, at, bt, inputs):
        live = live_at(f)
        m = mem[...]
        rows = z.shape[1] - READ
        n_in = rows - MEM
        z[f, :n_in] = inputs
        z[f, n_in:rows] = m.astype(BF)
        zz = z[f, :rows]
        xh, r = normalize(zz.astype(F32))
        xh_ref[f, :rows], rs_ref[f, :rows] = xh, r
        n = (xh * gain(l)).astype(BF)
        a = softmax_lanes(nt(small_ref[l, :READ], n))
        at[f] = a
        h = nn(a.astype(BF), zz)
        for b in range(BLOCKS):
            h = block_forward(l * BLOCKS + b, f, h)
        y = h.astype(BF)
        z[f, rows:] = y
        xh, r = normalize(y.astype(F32))
        xh_ref[f, rows:], rs_ref[f, rows:] = xh, r
        n = (xh_ref[f] * gain(10 + l)).astype(BF)
        b = softmax_lanes(nt(small_ref[l, READ:], n))
        bt[f] = b
        written = nn(b.astype(BF), z[f])
        rate = dec_ref[l]
        updated = rate * z[f, n_in:rows].astype(F32) + (1.0 - rate) * written
        mem[...] = live * updated + (1.0 - live) * m
        return (live * y.astype(F32)).astype(BF)

    def layer_backward(l, f, z, xh_ref, rs_ref, at, bt, dy_out):
        live = live_at(f)
        rows = z.shape[1] - READ
        n_in = rows - MEM
        dm = dmem[...]
        rate = dec_ref[l]
        dt = ((live * (1.0 - rate)) * dm).astype(BF)
        zf = z[f]
        b = bt[f]
        dl = softmax_lanes_back(b, nt(dt, zf)).astype(BF)
        dz = tn(b.astype(BF), dt)
        dn = tn(dl, small_ref[l, READ:])
        xh = xh_ref[f]
        dsm_ref[l, READ:READ + MEM] += nn(dl, (xh * gain(10 + l)).astype(BF))
        add_gain_grad(l, 5, dn * xh)
        dx = dn * gain(10 + l)
        dy = dz[rows:] + normalize_back(dx[rows:], xh[rows:], rs_ref[f, rows:]) + live * dy_out
        dh = dy.astype(BF).astype(F32)
        for bb in range(BLOCKS - 1, -1, -1):
            dh = block_backward(l * BLOCKS + bb, f, dh)
        ds = dh.astype(BF)
        xh = xh[:rows]
        a = at[f]
        dl = softmax_lanes_back(a, nt(ds, zf[:rows])).astype(BF)
        dz = dz[:rows] + tn(a.astype(BF), ds)
        dn = tn(dl, small_ref[l, :READ])
        dsm_ref[l, :READ] += nn(dl, (xh * gain(l)).astype(BF))
        add_gain_grad(l, 0, dn * xh)
        dz = dz + normalize_back(dx[:rows] + dn * gain(l), xh, rs_ref[f, :rows])
        dmq = (dz[n_in:] + (live * rate) * dm).astype(BF).astype(F32)
        dmem[...] = dmq + (1.0 - live) * dm
        return dz[:n_in].astype(BF)

    kept0 = (z0, xh0, rs0, at0, bt0)
    kept1 = (z1, xh1, rs1, at1, bt1)

    def wait_layer(l):
        for b in range(BLOCKS):
            for c in weight_copies(l * BLOCKS + b):
                c.wait()

    wait_layer(0)
    mem[...] = jnp.zeros_like(mem)

    def forward0(f, carry):
        dout[f] = layer_forward(0, f, *kept0, frames_ref[f])
        return carry

    lax.fori_loop(0, frames, forward0, 0)
    wait_layer(1)
    mem[...] = jnp.zeros_like(mem)

    def forward1(f, carry):
        res_ref[f] = layer_forward(1, f, *kept1, dout[f])
        return carry

    lax.fori_loop(0, frames, forward1, 0)
    dmem[...] = jnp.zeros_like(dmem)

    def backward1(i, carry):
        f = frames - 1 - i
        dout[f] = layer_backward(1, f, *kept1, cot_ref[f].astype(F32))
        return carry

    lax.fori_loop(0, frames, backward1, 0)
    dmem[...] = jnp.zeros_like(dmem)

    def backward0(i, carry):
        f = frames - 1 - i
        fgrad_ref[f] = layer_backward(0, f, *kept0, dout[f].astype(F32))
        return carry

    lax.fori_loop(0, frames, backward0, 0)


def run_chain(parts, length, frames, cot, decay, gains, small, wqkv, wout, wup, wdown):
    count, tok, width = frames.shape
    lbs = LAYERS * BLOCKS
    ff = wup.shape[-1]
    vm, anym = pl.BlockSpec(memory_space=pltpu.VMEM), pl.BlockSpec(memory_space=pl.ANY)

    def per(cols, dtype):
        return (lbs, count, READ, cols), dtype

    def sds(shape, dtype):
        return jax.ShapeDtypeStruct(shape, dtype)

    out_shape = [sds((count, READ, width), BF), sds((count, tok, width), BF)]
    out_shape += [sds(*per(3 * width, BF)), sds((lbs, parts, count, READ, ff // parts), BF)]
    out_shape += [sds(*per(width, BF)), sds((lbs, parts, count, READ, (4 * width + ff) // parts), BF)]
    out_shape += [sds((LAYERS, SMALL, width), F32)]
    rows0, rows1 = tok + MEM, READ + MEM
    v = pltpu.VMEM
    scratch = [v(w.shape, BF) for w in (wqkv, wout, wup, wdown)]
    scratch += [v((count, r + READ, width), BF) for r in (rows0, rows1)]
    scratch += [v((count, r + READ, width), F32) for r in (rows0, rows1)]
    scratch += [v((count, r + READ, 1), F32) for r in (rows0, rows1)]
    scratch += [v((count, READ, r), F32) for r in (rows0, rows1)]
    scratch += [v((count, MEM, r + READ), F32) for r in (rows0, rows1)]
    scratch += [v((MEM, width), F32), v((MEM, width), F32), v((count, READ, width), BF)]
    scratch += [v(*per(width, F32)), v(*per(1, F32)), v(*per(width, F32)), v(*per(1, F32))]
    scratch += [v(*per(ff, F32)), v(*per(3 * width, BF)), v(*per(HEADS * READ, F32))]
    scratch += [v((HEADS * READ, width), BF), pltpu.SemaphoreType.DMA((lbs, 4))]
    return pl.pallas_call(
        chain_kernel,
        out_shape=out_shape,
        in_specs=[pl.BlockSpec(memory_space=pltpu.SMEM)] + [vm] * 5 + [anym] * 4,
        out_specs=[vm] * len(out_shape),
        scratch_shapes=scratch,
        compiler_params=pltpu.CompilerParams(vmem_limit_bytes=60 * 2**20),
    )(length, frames, cot, decay, gains, small, wqkv, wout, wup, wdown)


def comm_kernel(
    hi, lo, gath_f, slice_f, gath_b, slice_b, dsm_ref, rows_ref, down_ref, small_ref,
    all_f, part_f, all_b, part_b, wgrad, into, small_t, small_in, small_sum, small_into,
    a_send, a_recv, a_own, c_send, c_recv, s_send, s_recv, t_send, t_recv, d_send, d_recv, d_own,
):
    lbs, sections = all_f.shape[:2]
    width = gath_b.shape[-1]
    me, dp_at = lax.axis_index("section"), lax.axis_index("dp")
    bits = hi.bit_length() - 1
    own_bits = [(dp_at // (lo << k)) % 2 for k in range(bits)]
    partners = [dp_at + (1 - 2 * b) * (lo << k) for k, b in enumerate(own_bits)]
    peers = [(me + k) % sections for k in range(1, sections)]

    barrier = pltpu.get_barrier_semaphore()
    for p in peers:
        pl.semaphore_signal(barrier, inc=1, device_id={"section": p}, device_id_type=pl.DeviceIdType.MESH)
    for p in partners:
        pl.semaphore_signal(barrier, inc=1, device_id={"dp": p}, device_id_type=pl.DeviceIdType.MESH)
    pl.semaphore_wait(barrier, len(peers) + len(partners))

    def remote(src, dst, send, recv, device):
        return pltpu.make_async_remote_copy(
            src_ref=src, dst_ref=dst, send_sem=send, recv_sem=recv, device_id=device, device_id_type=pl.DeviceIdType.MESH
        )

    def factor_copies(u):
        out = []
        for k, p in enumerate(peers):
            pairs = (
                (gath_f.at[u], all_f.at[u, me]), (gath_b.at[u], all_b.at[u, me]),
                (slice_f.at[u, p], part_f.at[u, me]), (slice_b.at[u, p], part_b.at[u, me]),
            )
            out += [remote(s, t, a_send.at[u, k, i], a_recv.at[u, k, i], {"section": p}) for i, (s, t) in enumerate(pairs)]
        return out

    def own_copies(u):
        pairs = (
            (gath_f.at[u], all_f.at[u, me]), (gath_b.at[u], all_b.at[u, me]),
            (slice_f.at[u, me], part_f.at[u, me]), (slice_b.at[u, me], part_b.at[u, me]),
        )
        return [pltpu.make_async_copy(s, t, a_own.at[u, i]) for i, (s, t) in enumerate(pairs)]

    def small_copies(l):
        return [
            remote(small_t.at[l, p], small_in.at[l, me], s_send.at[l, k], s_recv.at[l, k], {"section": p})
            for k, p in enumerate(peers)
        ]

    def halves(ref, lead, k, other):
        b = own_bits[k]
        at = lead + (slice(None),) * (bits - 1 - k) + ((1 - b) if other else b,) + tuple(own_bits[k - 1::-1] if k else ())
        return at

    def halving_copy(u, k):
        src = wgrad.at[halves(wgrad, (u,), k, True)]
        return remote(src, into[k].at[u], c_send.at[u, k], c_recv.at[u, k], {"dp": partners[k]})

    def small_halving_copy(l, k):
        src = small_sum.at[halves(small_sum, (l,), k, True)]
        return remote(src, small_into[k].at[l], t_send.at[l, k], t_recv.at[l, k], {"dp": partners[k]})

    own_at = tuple(own_bits[::-1])
    cols = part_b.shape[-1]

    def row_copies(u):
        return [
            remote(
                wgrad.at[(u,) + own_at + (pl.ds(pl.multiple_of(p * TILE, TILE), TILE), pl.ds(0, cols))],
                rows_ref.at[u, me], d_send.at[u, k], d_recv.at[u, k], {"section": p},
            )
            for k, p in enumerate(peers)
        ]

    def final_copies(u):
        here = wgrad.at[(u,) + own_at + (pl.ds(pl.multiple_of(me * TILE, TILE), TILE), pl.ds(0, cols))]
        down = wgrad.at[(u,) + own_at + (slice(None), pl.ds(cols, width))]
        return [
            pltpu.make_async_copy(here, rows_ref.at[u, me], d_own.at[u, 0]),
            pltpu.make_async_copy(down, down_ref.at[u], d_own.at[u, 1]),
        ]

    def store_rows(u, first, v):
        c = v.shape[1]
        v = v.astype(BF).reshape(sections, hi, TILE, c)
        for s in range(sections):
            for h in range(hi):
                at = tuple((h >> k) & 1 for k in range(bits - 1, -1, -1))
                wgrad[(u,) + at + (slice(s * TILE, (s + 1) * TILE), slice(first, first + c))] = v[s, h]

    def store_down(u, first, v):
        c = v.shape[1]
        v = v.astype(BF).reshape(hi, sections * TILE, c)
        for h in range(hi):
            at = tuple((h >> k) & 1 for k in range(bits - 1, -1, -1))
            wgrad[(u,) + at + (slice(None), slice(first, first + c))] = v[h]

    def form(u):
        for c in own_copies(u):
            c.wait()
        for c in factor_copies(u):
            c.wait_recv()
        tokens = all_b.shape[1] * all_b.shape[2] * all_b.shape[3]
        q, o = 3 * width // sections, 4 * width // sections

        def flat(ref, a, b):
            return ref[u, :, :, :, a:b].reshape(tokens, b - a)

        store_rows(u, 0, tn(flat(all_f, 0, width), flat(part_b, 0, q)))
        store_rows(u, q, tn(flat(all_f, width, 2 * width), flat(part_b, q, o)))
        store_rows(u, o, tn(flat(all_f, 2 * width, 3 * width), flat(part_b, o, cols)))
        store_down(u, cols, tn(flat(part_f, 0, part_f.shape[-1]), flat(all_b, 0, width)))
        halving_copy(u, 0).start()
        if u % BLOCKS == 0:
            l = u // BLOCKS
            for c in small_copies(l):
                c.wait_recv()
            total = small_t[l, me]
            for k in range(1, sections):
                total = total + small_in[l, (me + k) % sections]
            total = total.reshape(hi, TILE, SMALL)
            for h in range(hi):
                at = tuple((h >> k) & 1 for k in range(bits - 1, -1, -1))
                small_sum[(l,) + at] = total[h]
            small_halving_copy(l, 0).start()

    def halve(u, k):
        halving_copy(u, k).wait_recv()
        at = halves(wgrad, (u,), k, False)
        wgrad[at] = wgrad[at] + into[k][u]
        if k + 1 < bits:
            halving_copy(u, k + 1).start()
        else:
            for c in row_copies(u) + final_copies(u):
                c.start()
        if u % BLOCKS == 0:
            l = u // BLOCKS
            small_halving_copy(l, k).wait_recv()
            at = halves(small_sum, (l,), k, False)
            small_sum[at] = small_sum[at] + small_into[k][l]
            if k + 1 < bits:
                small_halving_copy(l, k + 1).start()
            else:
                small_ref[l] = small_sum[(l,) + own_at]

    def finish(u):
        for c in final_copies(u):
            c.wait()
        for c in row_copies(u):
            c.wait()
        for c in factor_copies(u):
            c.wait_send()
        for k in range(bits):
            halving_copy(u, k).wait_send()
        if u % BLOCKS == 0:
            l = u // BLOCKS
            for c in small_copies(l):
                c.wait_send()
            for k in range(bits):
                small_halving_copy(l, k).wait_send()

    order = list(range(lbs - 1, -1, -1))
    for u in order:
        for c in factor_copies(u) + own_copies(u):
            c.start()
        if u % BLOCKS == 0:
            l = u // BLOCKS
            small_t[l] = jnp.transpose(dsm_ref[l]).reshape(small_t.shape[1:])
            for c in small_copies(l):
                c.start()
    stages = [form] + [lambda u, k=k: halve(u, k) for k in range(bits)] + [finish]
    for t in range(lbs + len(stages) - 1):
        for i in range(len(stages) - 1, -1, -1):
            if 0 <= t - i < lbs:
                stages[i](order[t - i])


def sum_over_devices(sections, hi, lo, gath_f, slice_f, gath_b, slice_b, dsm):
    lbs, count, rows, width = gath_b.shape
    cols = slice_b.shape[-1]
    all_cols = cols + width
    bits = hi.bit_length() - 1
    chunk = sections * TILE
    peers = sections - 1
    vm = pl.BlockSpec(memory_space=pltpu.VMEM)
    v, dma = pltpu.VMEM, pltpu.SemaphoreType.DMA

    def with_sources(a):
        return v((lbs, sections) + a.shape[-3:], a.dtype)

    scratch = [with_sources(a) for a in (gath_f, slice_f, gath_b, slice_b)]
    scratch += [v((lbs,) + (2,) * bits + (chunk, all_cols), BF)]
    scratch += [[v((lbs,) + (2,) * (bits - 1 - k) + (chunk, all_cols), BF) for k in range(bits)]]
    scratch += [v((LAYERS, sections, width // sections, SMALL), F32)] * 2
    scratch += [v((LAYERS,) + (2,) * bits + (TILE, SMALL), F32)]
    scratch += [[v((LAYERS,) + (2,) * (bits - 1 - k) + (TILE, SMALL), F32) for k in range(bits)]]
    scratch += [dma((lbs, peers, 4)), dma((lbs, peers, 4)), dma((lbs, 4)), dma((lbs, bits)), dma((lbs, bits))]
    scratch += [dma((LAYERS, peers)), dma((LAYERS, peers)), dma((LAYERS, bits)), dma((LAYERS, bits))]
    scratch += [dma((lbs, peers)), dma((lbs, peers)), dma((lbs, 2))]
    return pl.pallas_call(
        functools.partial(comm_kernel, hi, lo),
        out_shape=[
            jax.ShapeDtypeStruct((lbs, sections, TILE, cols), BF),
            jax.ShapeDtypeStruct((lbs, chunk, width), BF),
            jax.ShapeDtypeStruct((LAYERS, TILE, SMALL), F32),
        ],
        in_specs=[vm] * 5,
        out_specs=[vm] * 3,
        scratch_shapes=scratch,
        compiler_params=pltpu.CompilerParams(
            collective_id=0, has_side_effects=True, vmem_limit_bytes=60 * 2**20
        ),
    )(gath_f, slice_f, gath_b, slice_b, dsm)


def widen_kernel(rows_ref, down_ref, qkv_ref, out_ref, up_ref, down_out):
    lbs, sections, _, _ = rows_ref.shape
    cols = [ref.shape[-1] // sections for ref in (qkv_ref, out_ref, up_ref)]
    for s in range(sections):
        first = 0
        for ref, c in zip((qkv_ref, out_ref, up_ref), cols):
            ref[:, :, s * c:(s + 1) * c] = rows_ref[:, s, :, first:first + c].astype(F32)
            first += c
    down_out[...] = down_ref[...].astype(F32)


def widen(rows, down):
    lbs, sections, tile, cols = rows.shape
    width = down.shape[-1]
    vm = pl.BlockSpec(memory_space=pltpu.VMEM)
    shapes = [(lbs, tile, 3 * width), (lbs, tile, width), (lbs, tile, sections * cols - 4 * width), down.shape]
    return pl.pallas_call(
        widen_kernel,
        out_shape=[jax.ShapeDtypeStruct(s, F32) for s in shapes],
        in_specs=[vm] * 2,
        out_specs=[vm] * 4,
    )(rows, down)


def local(
    frames, lengths, decay, read_gain, read_weight, norm_attn, w_qkv, w_out, norm_mlp, w_up, w_down,
    write_gain, write_weight, cotangent,
):
    sections, dp = lax.axis_size("section"), lax.axis_size("dp")
    clip_dev, span, tok, width = frames.shape
    lbs = LAYERS * BLOCKS
    hi = width // (sections * TILE)
    lo = dp // hi
    assert clip_dev == sections and span == 1 and hi * lo == dp
    both = jnp.concatenate([frames[:, 0], cotangent[:, 0]], axis=1)
    both = lax.all_to_all(both, "section", 0, 0, tiled=True)
    length = lax.dynamic_slice_in_dim(lengths, lax.axis_index("section"), 1, 0)
    gains = jnp.concatenate(
        [read_gain, norm_attn.reshape(lbs, width), norm_mlp.reshape(lbs, width), write_gain], axis=0
    ).astype(F32)
    small = jnp.swapaxes(jnp.concatenate([read_weight, write_weight], axis=2), 1, 2)
    weights = [w.reshape(lbs, *w.shape[2:]) for w in (w_qkv, w_out, w_up, w_down)]
    res, fgrad, *factors = run_chain(
        sections, length, both[:, :tok], both[:, tok:], decay[:, :, None], gains, small, *weights
    )
    back = lax.all_to_all(jnp.concatenate([fgrad, res], axis=1), "section", 0, 0, tiled=True)
    rows, down, sm = sum_over_devices(sections, hi, lo, *factors)
    grads = [g.reshape(LAYERS, BLOCKS, *g.shape[1:]) for g in widen(rows, down)]
    if lo > 1:
        groups = [[h * lo + k for k in range(lo)] for h in range(hi)]
        grads = [lax.psum_scatter(g, "dp", scatter_dimension=2, axis_index_groups=groups, tiled=True) for g in grads]
        sm = lax.psum_scatter(sm, "dp", scatter_dimension=1, axis_index_groups=groups, tiled=True)
    gain_grads = jnp.swapaxes(sm[:, :, READ + MEM:], 1, 2)
    return (
        back[:, None, tok:],
        back[:, None, :tok],
        gain_grads[:, 0],
        sm[:, :, :READ],
        gain_grads[:, 1:1 + BLOCKS],
        grads[0],
        grads[1],
        gain_grads[:, 1 + BLOCKS:1 + 2 * BLOCKS],
        grads[2],
        grads[3],
        gain_grads[:, 1 + 2 * BLOCKS],
        sm[:, :, READ:READ + MEM],
    )


def solution(mesh):
    both = ("section", "dp")
    split = P("dp", "section", None, None)
    return jax.shard_map(
        local,
        mesh=mesh,
        in_specs=(split, P("dp")) + (P(),) * 11 + (split,),
        out_specs=(
            split, split, P(None, both), P(None, both, None), P(None, None, both), P(None, None, both, None),
            P(None, None, both, None), P(None, None, both), P(None, None, both, None),
            P(None, None, both, None), P(None, both), P(None, both, None),
        ),
        check_vma=False,
    )
```

```python
import functools

import jax
import jax.numpy as jnp
from jax import lax
from jax.experimental import pallas as pl
from jax.experimental.pallas import tpu as pltpu
from jax.sharding import PartitionSpec as P

HEADS = 8
HEAD = 64
MEM = 96
READ = 16
BLOCKS = 2
LAYERS = 2
EPS = 1e-05
SMALL = 128
TILE = 16
BF = jnp.bfloat16
F32 = jnp.float32


def nn(a, b):
    return lax.dot_general(a, b, (((1,), (0,)), ((), ())), preferred_element_type=F32)


def nt(a, b):
    return lax.dot_general(a, b, (((1,), (1,)), ((), ())), preferred_element_type=F32)


def tn(a, b):
    return lax.dot_general(a, b, (((0,), (0,)), ((), ())), preferred_element_type=F32)


def normalize(v):
    centred = v - jnp.mean(v, axis=-1, keepdims=True)
    spread = jnp.mean(centred * centred, axis=-1, keepdims=True)
    r = lax.rsqrt(spread + EPS)
    return centred * r, r


def normalize_back(dx, xh, r):
    return r * (dx - jnp.mean(dx, axis=-1, keepdims=True) - xh * jnp.mean(dx * xh, axis=-1, keepdims=True))


def softmax_lanes(v):
    e = jnp.exp(v - jnp.max(v, axis=1, keepdims=True))
    return e / jnp.sum(e, axis=1, keepdims=True)


def softmax_lanes_back(p, dp):
    return p * (dp - jnp.sum(p * dp, axis=1, keepdims=True))


def fused_kernel(
    hi, lo, len_ref, decay_ref, rg_ref, na_ref, nm_ref, wg_ref, rw_ref, ww_ref, frames_hbm, cot_hbm,
    wqkv_hbm, wout_hbm, wup_hbm, wdown_hbm, res_out, fgrad_out, rows_ref, down_ref, small_ref, scratch,
):
    (
        wqkv, wout, wup, wdown, frames_v, cot_v, res_v, fgrad_v, z0, z1, xh0, xh1, rs0, rs1, at0, at1, bt0, bt1,
        mem, dmem, dout, xa, ra, xm, rm, gp, qkv, pt, mask_ref, gains, dec_col, dsm_ref,
        slice_f, slice_b, all_f, part_f, all_b, part_b, wgrad, into, small_t, small_in, small_sum, small_into,
        w_sem, f_send, f_recv, f_own, o_send, o_recv, o_own,
        a_send, a_recv, a_own, c_send, c_recv, s_send, s_recv, t_send, t_recv, d_send, d_recv, d_own,
    ) = scratch
    sections, frames, _, width = all_b.shape[1:]
    parts = sections
    lbs = LAYERS * BLOCKS
    me, dp_at = lax.axis_index("section"), lax.axis_index("dp")
    bits = hi.bit_length() - 1
    own_bits = [(dp_at // (lo << k)) % 2 for k in range(bits)]
    partners = [dp_at + (1 - 2 * b) * (lo << k) for k, b in enumerate(own_bits)]
    peers = [(me + k) % sections for k in range(1, sections)]

    def weight_copies(lb):
        at = (lb // BLOCKS, lb % BLOCKS)
        pairs = ((wqkv_hbm, wqkv), (wout_hbm, wout), (wup_hbm, wup), (wdown_hbm, wdown))
        return [pltpu.make_async_copy(s.at[at], d.at[lb], w_sem.at[lb, i]) for i, (s, d) in enumerate(pairs)]

    barrier = pltpu.get_barrier_semaphore()
    for p in peers:
        pl.semaphore_signal(barrier, inc=1, device_id={"section": p}, device_id_type=pl.DeviceIdType.MESH)
    for p in partners:
        pl.semaphore_signal(barrier, inc=1, device_id={"dp": p}, device_id_type=pl.DeviceIdType.MESH)

    def remote(src, dst, send, recv, device):
        return pltpu.make_async_remote_copy(
            src_ref=src, dst_ref=dst, send_sem=send, recv_sem=recv, device_id=device, device_id_type=pl.DeviceIdType.MESH
        )

    def forward_copies(u):
        return [
            remote(src, dst, a_send.at[u, k, i], a_recv.at[u, k, i], {"section": p})
            for k, p in enumerate(peers)
            for i, (src, dst) in enumerate(
                ((all_f.at[u, me], all_f.at[u, me]), (slice_f.at[u, p], part_f.at[u, me]))
            )
        ]

    def backward_copies(u, first, count):
        at = pl.ds(first, count)
        return [
            remote(src, dst, a_send.at[u, k, 2 + i], a_recv.at[u, k, 2 + i], {"section": p})
            for k, p in enumerate(peers)
            for i, (src, dst) in enumerate(
                ((all_b.at[u, me, at], all_b.at[u, me, at]), (slice_b.at[u, p, at], part_b.at[u, me, at]))
            )
        ]

    def own_forward(u):
        return pltpu.make_async_copy(slice_f.at[u, me], part_f.at[u, me], a_own.at[u, 0])

    def own_backward(u, first, count):
        at = pl.ds(first, count)
        return pltpu.make_async_copy(slice_b.at[u, me, at], part_b.at[u, me, at], a_own.at[u, 1])

    def factor_copies(u):
        return forward_copies(u) + backward_copies(u, 0, frames)

    def start_forward(l):
        for u in range(l * BLOCKS + BLOCKS - 1, l * BLOCKS - 1, -1):
            for c in forward_copies(u) + [own_forward(u)]:
                c.start()

    def start_backward(l, first, count):
        for u in range(l * BLOCKS + BLOCKS - 1, l * BLOCKS - 1, -1):
            for c in backward_copies(u, first, count) + [own_backward(u, first, count)]:
                c.start()

    def start_small(l):
        small_t[l] = jnp.transpose(dsm_ref[l]).reshape(small_t.shape[1:])
        for c in small_copies(l):
            c.start()

    def small_copies(l):
        return [
            remote(small_t.at[l, p], small_in.at[l, me], s_send.at[l, k], s_recv.at[l, k], {"section": p})
            for k, p in enumerate(peers)
        ]

    def halves(ref, lead, k, other):
        b = own_bits[k]
        at = lead + (slice(None),) * (bits - 1 - k) + ((1 - b) if other else b,) + tuple(own_bits[k - 1::-1] if k else ())
        return at

    def halving_copy(u, k):
        src = wgrad.at[halves(wgrad, (u,), k, True)]
        return remote(src, into[k].at[u], c_send.at[u, k], c_recv.at[u, k], {"dp": partners[k]})

    def small_halving_copy(l, k):
        src = small_sum.at[halves(small_sum, (l,), k, True)]
        return remote(src, small_into[k].at[l], t_send.at[l, k], t_recv.at[l, k], {"dp": partners[k]})

    own_at = tuple(own_bits[::-1])
    cols = part_b.shape[-1]

    def row_copies(u):
        return [
            remote(
                wgrad.at[(u,) + own_at + (pl.ds(pl.multiple_of(p * TILE, TILE), TILE), pl.ds(0, cols))],
                rows_ref.at[u, me], d_send.at[u, k], d_recv.at[u, k], {"section": p},
            )
            for k, p in enumerate(peers)
        ]

    def final_copies(u):
        here = wgrad.at[(u,) + own_at + (pl.ds(pl.multiple_of(me * TILE, TILE), TILE), pl.ds(0, cols))]
        down = wgrad.at[(u,) + own_at + (slice(None), pl.ds(cols, width))]
        return [
            pltpu.make_async_copy(here, rows_ref.at[u, me], d_own.at[u, 0]),
            pltpu.make_async_copy(down, down_ref.at[u], d_own.at[u, 1]),
        ]

    def store_rows(u, first, v):
        c = v.shape[1]
        v = v.astype(BF).reshape(sections, hi, TILE, c)
        for s in range(sections):
            for h in range(hi):
                at = tuple((h >> k) & 1 for k in range(bits - 1, -1, -1))
                wgrad[(u,) + at + (slice(s * TILE, (s + 1) * TILE), slice(first, first + c))] = v[s, h]

    def store_down(u, first, v):
        c = v.shape[1]
        v = v.astype(BF).reshape(hi, sections * TILE, c)
        for h in range(hi):
            at = tuple((h >> k) & 1 for k in range(bits - 1, -1, -1))
            wgrad[(u,) + at + (slice(None), slice(first, first + c))] = v[h]

    def form(u):
        own_forward(u).wait()
        own_backward(u, 0, frames).wait()
        for c in factor_copies(u):
            c.wait_recv()
        tokens = all_b.shape[1] * all_b.shape[2] * all_b.shape[3]
        q, o = 3 * width // sections, 4 * width // sections

        def flat(ref, a, b):
            return ref[u, :, :, :, a:b].reshape(tokens, b - a)

        store_rows(u, 0, tn(flat(all_f, 0, width), flat(part_b, 0, q)))
        store_rows(u, q, tn(flat(all_f, width, 2 * width), flat(part_b, q, o)))
        store_rows(u, o, tn(flat(all_f, 2 * width, 3 * width), flat(part_b, o, cols)))
        store_down(u, cols, tn(flat(part_f, 0, part_f.shape[-1]), flat(all_b, 0, width)))
        halving_copy(u, 0).start()
        if u % BLOCKS == 0:
            l = u // BLOCKS
            for c in small_copies(l):
                c.wait_recv()
            total = small_t[l, me]
            for k in range(1, sections):
                total = total + small_in[l, (me + k) % sections]
            total = total.reshape(hi, TILE, SMALL)
            for h in range(hi):
                at = tuple((h >> k) & 1 for k in range(bits - 1, -1, -1))
                small_sum[(l,) + at] = total[h]
            small_halving_copy(l, 0).start()

    def halve(u, k):
        halving_copy(u, k).wait_recv()
        at = halves(wgrad, (u,), k, False)
        wgrad[at] = wgrad[at] + into[k][u]
        if k + 1 < bits:
            halving_copy(u, k + 1).start()
        else:
            for c in row_copies(u) + final_copies(u):
                c.start()
        if u % BLOCKS == 0:
            l = u // BLOCKS
            small_halving_copy(l, k).wait_recv()
            at = halves(small_sum, (l,), k, False)
            small_sum[at] = small_sum[at] + small_into[k][l]
            if k + 1 < bits:
                small_halving_copy(l, k + 1).start()
            else:
                small_ref[l] = small_sum[(l,) + own_at]

    def finish(u):
        for c in final_copies(u):
            c.wait()
        for c in row_copies(u):
            c.wait()
        for c in factor_copies(u):
            c.wait_send()
        for k in range(bits):
            halving_copy(u, k).wait_send()
        if u % BLOCKS == 0:
            l = u // BLOCKS
            for c in small_copies(l):
                c.wait_send()
            for k in range(bits):
                small_halving_copy(l, k).wait_send()

    def frame_copies():
        return [
            remote(src.at[p, 0], dst.at[me], f_send.at[k, i], f_recv.at[k, i], {"section": p})
            for k, p in enumerate(peers)
            for i, (src, dst) in enumerate(((frames_hbm, frames_v), (cot_hbm, cot_v)))
        ]

    def own_frames():
        return [
            pltpu.make_async_copy(src.at[me, 0], dst.at[me], f_own.at[i])
            for i, (src, dst) in enumerate(((frames_hbm, frames_v), (cot_hbm, cot_v)))
        ]

    def output_copies(i, src, dst):
        copies = [
            remote(src.at[p], dst.at[me], o_send.at[k, i], o_recv.at[k, i], {"section": p}) for k, p in enumerate(peers)
        ]
        return copies, pltpu.make_async_copy(src.at[me], dst.at[me], o_own.at[i])

    def start_output(i, src, dst):
        copies, own = output_copies(i, src, dst)
        for c in copies + [own]:
            c.start()

    def spread_heads(v):
        return jnp.concatenate([v] * HEADS, axis=0) * mask_ref[...]

    def gather_heads(v):
        return jnp.sum((v * mask_ref[...].astype(F32)).reshape(HEADS, READ, width), axis=0)

    def live_at(f):
        return jnp.where(f < len_ref[me], 1.0, 0.0).astype(F32)

    def keep_slices(ref, lb, f, first, v):
        cols = v.shape[1] // parts
        for s in range(parts):
            ref[lb, s, f, :, first:first + cols] = v[:, s * cols:(s + 1) * cols]

    def add_gain_grad(l, i, v):
        dsm_ref[l, READ + MEM + i:READ + MEM + i + 1, :] += jnp.sum(v, axis=0, keepdims=True)

    def gain(i):
        return gains[i:i + 1, :]

    def block_forward(lb, f, h):
        xh, r = normalize(h)
        xa[lb, f], ra[lb, f] = xh, r
        g = (xh * gain(2 + lb)).astype(BF)
        all_f[lb, me, f, :, :width] = g
        joined = nn(g, wqkv[lb]).astype(BF)
        qkv[lb, f] = joined
        q, k, v = joined[:, :width], joined[:, width:2 * width], joined[:, 2 * width:]
        s = nt(k, spread_heads(q)) * HEAD ** (-0.5)
        e = jnp.exp(s - jnp.max(s, axis=0, keepdims=True))
        p = e / jnp.sum(e, axis=0, keepdims=True)
        pt[lb, f] = p
        o = gather_heads(tn(p.astype(BF), v)).astype(BF)
        all_f[lb, me, f, :, width:2 * width] = o
        h = h + nn(o, wout[lb])
        xh, r = normalize(h)
        xm[lb, f], rm[lb, f] = xh, r
        u = (xh * gain(6 + lb)).astype(BF)
        all_f[lb, me, f, :, 2 * width:] = u
        x = nn(u, wup[lb])
        c0, c1 = 0.7978845608028654, 0.044715
        x2 = x * x
        t = jnp.tanh(c0 * x * (1.0 + c1 * x2))
        lift = (0.5 * x * (1.0 + t)).astype(BF)
        gp[lb, f] = 0.5 * (1.0 + t) + 0.5 * x * (1.0 - t * t) * c0 * (1.0 + 3.0 * c1 * x2)
        keep_slices(slice_f, lb, f, 0, lift)
        return h + nn(lift, wdown[lb])

    def block_backward(lb, f, dh):
        dhb = dh.astype(BF)
        all_b[lb, me, f] = dhb
        dup = (nt(dhb, wdown[lb]) * gp[lb, f]).astype(BF)
        keep_slices(slice_b, lb, f, width, dup)
        du = nt(dup, wup[lb])
        xh = xm[lb, f]
        add_gain_grad(lb // BLOCKS, 3 + lb % BLOCKS, du * xh)
        dh = dh + normalize_back(du * gain(6 + lb), xh, rm[lb, f])
        dhb = dh.astype(BF)
        keep_slices(slice_b, lb, f, 3 * width // parts, dhb)
        do = spread_heads(nt(dhb, wout[lb]).astype(BF))
        joined = qkv[lb, f]
        q, k, v = joined[:, :width], joined[:, width:2 * width], joined[:, 2 * width:]
        p = pt[lb, f]
        dp = nt(v, do)
        ds = (p * (dp - jnp.sum(p * dp, axis=0, keepdims=True)) * HEAD ** (-0.5)).astype(BF)
        dv = nn(p.astype(BF), do)
        dk = nn(ds, spread_heads(q))
        dq = gather_heads(tn(ds, k))
        dj = jnp.concatenate([dq, dk, dv], axis=1).astype(BF)
        keep_slices(slice_b, lb, f, 0, dj)
        dg = nt(dj, wqkv[lb])
        xh = xa[lb, f]
        add_gain_grad(lb // BLOCKS, 1 + lb % BLOCKS, dg * xh)
        return dh + normalize_back(dg * gain(2 + lb), xh, ra[lb, f])

    def layer_forward(l, f, z, xh_ref, rs_ref, at, bt, inputs):
        live = live_at(f)
        m = mem[...]
        rows = z.shape[1] - READ
        n_in = rows - MEM
        z[f, :n_in] = inputs
        z[f, n_in:rows] = m.astype(BF)
        zz = z[f, :rows]
        xh, r = normalize(zz.astype(F32))
        xh_ref[f, :rows], rs_ref[f, :rows] = xh, r
        n = (xh * gain(l)).astype(BF)
        a = softmax_lanes(nt(rw_ref[l], n))
        at[f] = a
        h = nn(a.astype(BF), zz)
        for b in range(BLOCKS):
            h = block_forward(l * BLOCKS + b, f, h)
        y = h.astype(BF)
        z[f, rows:] = y
        xh, r = normalize(y.astype(F32))
        xh_ref[f, rows:], rs_ref[f, rows:] = xh, r
        n = (xh_ref[f] * gain(10 + l)).astype(BF)
        b = softmax_lanes(nt(ww_ref[l], n))
        bt[f] = b
        written = nn(b.astype(BF), z[f])
        rate = dec_col[l]
        updated = rate * z[f, n_in:rows].astype(F32) + (1.0 - rate) * written
        mem[...] = live * updated + (1.0 - live) * m
        return (live * y.astype(F32)).astype(BF)

    def layer_backward(l, f, z, xh_ref, rs_ref, at, bt, dy_out):
        live = live_at(f)
        rows = z.shape[1] - READ
        n_in = rows - MEM
        dm = dmem[...]
        rate = dec_col[l]
        dt = ((live * (1.0 - rate)) * dm).astype(BF)
        zf = z[f]
        b = bt[f]
        dl = softmax_lanes_back(b, nt(dt, zf)).astype(BF)
        dz = tn(b.astype(BF), dt)
        dn = tn(dl, ww_ref[l])
        xh = xh_ref[f]
        dsm_ref[l, READ:READ + MEM] += nn(dl, (xh * gain(10 + l)).astype(BF))
        add_gain_grad(l, 5, dn * xh)
        dx = dn * gain(10 + l)
        dy = dz[rows:] + normalize_back(dx[rows:], xh[rows:], rs_ref[f, rows:]) + live * dy_out
        dh = dy.astype(BF).astype(F32)
        for bb in range(BLOCKS - 1, -1, -1):
            dh = block_backward(l * BLOCKS + bb, f, dh)
        ds = dh.astype(BF)
        xh = xh[:rows]
        a = at[f]
        dl = softmax_lanes_back(a, nt(ds, zf[:rows])).astype(BF)
        dz = dz[:rows] + tn(a.astype(BF), ds)
        dn = tn(dl, rw_ref[l])
        dsm_ref[l, :READ] += nn(dl, (xh * gain(l)).astype(BF))
        add_gain_grad(l, 0, dn * xh)
        dz = dz + normalize_back(dx[:rows] + dn * gain(l), xh, rs_ref[f, :rows])
        dmq = (dz[n_in:] + (live * rate) * dm).astype(BF).astype(F32)
        dmem[...] = dmq + (1.0 - live) * dm
        return dz[:n_in].astype(BF)

    for c in own_frames():
        c.start()
    for lb in range(lbs):
        for c in weight_copies(lb):
            c.start()
    row = lax.broadcasted_iota(jnp.int32, (HEADS * READ, width), 0) // READ
    col = lax.broadcasted_iota(jnp.int32, (HEADS * READ, width), 1) // HEAD
    mask_ref[...] = jnp.where(row == col, 1.0, 0.0).astype(BF)
    dsm_ref[...] = jnp.zeros_like(dsm_ref)
    for l in range(LAYERS):
        gains[l:l + 1] = rg_ref[...].astype(F32)[l:l + 1]
        gains[10 + l:11 + l] = wg_ref[...].astype(F32)[l:l + 1]
        for b in range(BLOCKS):
            lb = l * BLOCKS + b
            gains[2 + lb:3 + lb] = na_ref[l].astype(F32)[b:b + 1]
            gains[6 + lb:7 + lb] = nm_ref[l].astype(F32)[b:b + 1]
        spread = jnp.broadcast_to(decay_ref[l:l + 1], (MEM, MEM))
        diagonal = lax.broadcasted_iota(jnp.int32, (MEM, MEM), 0) == lax.broadcasted_iota(jnp.int32, (MEM, MEM), 1)
        dec_col[l] = jnp.sum(jnp.where(diagonal, spread, 0.0), axis=1, keepdims=True)

    pl.semaphore_wait(barrier, len(peers) + len(partners))
    for c in frame_copies():
        c.start()

    kept0 = (z0, xh0, rs0, at0, bt0)
    kept1 = (z1, xh1, rs1, at1, bt1)

    def wait_layer(l):
        for b in range(BLOCKS):
            for c in weight_copies(l * BLOCKS + b):
                c.wait()

    wait_layer(0)
    for c in own_frames():
        c.wait()
    for c in frame_copies():
        c.wait_recv()
    mem[...] = jnp.zeros_like(mem)

    def forward0(f, carry):
        dout[f] = layer_forward(0, f, *kept0, frames_v[f])
        return carry

    lax.fori_loop(0, frames, forward0, 0)
    start_forward(0)
    wait_layer(1)
    mem[...] = jnp.zeros_like(mem)

    def forward1(f, carry):
        res_v[f] = layer_forward(1, f, *kept1, dout[f])
        return carry

    lax.fori_loop(0, frames, forward1, 0)
    start_forward(1)
    start_output(0, res_v, res_out)
    dmem[...] = jnp.zeros_like(dmem)

    def backward1(i, carry):
        f = frames - 1 - i
        dout[f] = layer_backward(1, f, *kept1, cot_v[f].astype(F32))
        return carry

    lax.fori_loop(0, frames, backward1, 0)
    start_backward(1, 0, frames)
    start_small(1)
    dmem[...] = jnp.zeros_like(dmem)

    def backward0(i, carry):
        f = frames - 1 - i
        fgrad_v[f] = layer_backward(0, f, *kept0, dout[f].astype(F32))

        @pl.when(i == 0)
        def _():
            form(3)
            form(2)

        @pl.when(i == 1)
        def _():
            halve(3, 0)
            halve(2, 0)

        @pl.when(i == 2)
        def _():
            start_backward(0, 1, frames - 1)
            halve(3, 1)

        return carry

    lax.fori_loop(0, frames, backward0, 0)
    start_backward(0, 0, 1)
    start_small(0)
    start_output(1, fgrad_v, fgrad_out)
    halve(2, 1)
    halve(3, 2)
    form(1)
    form(0)
    halve(2, 2)
    halve(1, 0)
    halve(0, 0)
    halve(1, 1)
    halve(0, 1)
    halve(1, 2)
    halve(0, 2)
    for u in range(lbs - 1, -1, -1):
        finish(u)
    for i, (src, dst) in enumerate(((res_v, res_out), (fgrad_v, fgrad_out))):
        copies, own = output_copies(i, src, dst)
        for c in copies + [own]:
            c.wait()
    for c in frame_copies():
        c.wait_send()


def run_fused(sections, hi, lo, lengths, decay, gains, small, frames, cot, weights):
    count, _, tok, width = frames.shape
    lbs = LAYERS * BLOCKS
    ff = weights[2].shape[-1]
    cols = (4 * width + ff) // sections
    all_cols = cols + width
    bits = hi.bit_length() - 1
    chunk = sections * TILE
    peers = sections - 1
    vm, anym = pl.BlockSpec(memory_space=pltpu.VMEM), pl.BlockSpec(memory_space=pl.ANY)
    v, dma = pltpu.VMEM, pltpu.SemaphoreType.DMA

    def sds(shape, dtype):
        return jax.ShapeDtypeStruct(shape, dtype)

    def per(c, dtype):
        return v((lbs, count, READ, c), dtype)

    def by_section(c):
        return v((lbs, sections, count, READ, c), BF)

    rows0, rows1 = tok + MEM, READ + MEM
    scratch = [v((lbs,) + w.shape[2:], BF) for w in weights]
    scratch += [v((count, tok, width), BF), v((count, READ, width), BF)]
    scratch += [v((count, READ, width), BF), v((count, tok, width), BF)]
    scratch += [v((count, r + READ, width), BF) for r in (rows0, rows1)]
    scratch += [v((count, r + READ, width), F32) for r in (rows0, rows1)]
    scratch += [v((count, r + READ, 1), F32) for r in (rows0, rows1)]
    scratch += [v((count, READ, r), F32) for r in (rows0, rows1)]
    scratch += [v((count, MEM, r + READ), F32) for r in (rows0, rows1)]
    scratch += [v((MEM, width), F32), v((MEM, width), F32), v((count, READ, width), BF)]
    scratch += [per(width, F32), per(1, F32), per(width, F32), per(1, F32)]
    scratch += [per(ff, F32), per(3 * width, BF), per(HEADS * READ, F32)]
    scratch += [v((HEADS * READ, width), BF), v((12, width), F32), v((LAYERS, MEM, 1), F32)]
    scratch += [v((LAYERS, SMALL, width), F32)]
    scratch += [by_section(ff // sections), by_section(cols), by_section(3 * width), by_section(ff // sections)]
    scratch += [by_section(width), by_section(cols)]
    scratch += [v((lbs,) + (2,) * bits + (chunk, all_cols), BF)]
    scratch += [[v((lbs,) + (2,) * (bits - 1 - k) + (chunk, all_cols), BF) for k in range(bits)]]
    scratch += [v((LAYERS, sections, width // sections, SMALL), F32)] * 2
    scratch += [v((LAYERS,) + (2,) * bits + (TILE, SMALL), F32)]
    scratch += [[v((LAYERS,) + (2,) * (bits - 1 - k) + (TILE, SMALL), F32) for k in range(bits)]]
    scratch += [dma((lbs, 4)), dma((peers, 2)), dma((peers, 2)), dma((2,)), dma((peers, 2)), dma((peers, 2)), dma((2,))]
    scratch += [dma((lbs, peers, 4)), dma((lbs, peers, 4)), dma((lbs, 2)), dma((lbs, bits)), dma((lbs, bits))]
    scratch += [dma((LAYERS, peers)), dma((LAYERS, peers)), dma((LAYERS, bits)), dma((LAYERS, bits))]
    scratch += [dma((lbs, peers)), dma((lbs, peers)), dma((lbs, 2))]
    return pl.pallas_call(
        functools.partial(fused_kernel, hi, lo),
        out_shape=[
            sds((count, READ, width), BF),
            sds((count, tok, width), BF),
            sds((lbs, sections, TILE, cols), BF),
            sds((lbs, chunk, width), BF),
            sds((LAYERS, TILE, SMALL), F32),
        ],
        in_specs=[pl.BlockSpec(memory_space=pltpu.SMEM)] + [vm] * 7 + [anym] * 6,
        out_specs=[vm] * 5,
        scratch_shapes=[scratch],
        compiler_params=pltpu.CompilerParams(
            collective_id=0, has_side_effects=True, vmem_limit_bytes=64 * 2**20 - 2**16
        ),
    )(lengths, decay, *gains, *small, frames, cot, *weights)


def widen_kernel(rows_ref, down_ref, res_ref, fgrad_ref, qkv_ref, out_ref, up_ref, down_out, res_out, fgrad_out):
    lbs, sections, _, _ = rows_ref.shape
    cols = [ref.shape[-1] // sections for ref in (qkv_ref, out_ref, up_ref)]
    for s in range(sections):
        first = 0
        for ref, c in zip((qkv_ref, out_ref, up_ref), cols):
            ref[:, :, s * c:(s + 1) * c] = rows_ref[:, s, :, first:first + c].astype(F32)
            first += c
    down_out[...] = down_ref[...].astype(F32)
    res_out[...] = res_ref[...]
    fgrad_out[...] = fgrad_ref[...]


def widen(rows, down, res, fgrad):
    lbs, sections, tile, cols = rows.shape
    width = down.shape[-1]
    vm = pl.BlockSpec(memory_space=pltpu.VMEM)
    shapes = [(lbs, tile, 3 * width), (lbs, tile, width), (lbs, tile, sections * cols - 4 * width), down.shape]
    return pl.pallas_call(
        widen_kernel,
        out_shape=[jax.ShapeDtypeStruct(s, F32) for s in shapes]
        + [jax.ShapeDtypeStruct(a.shape, a.dtype) for a in (res, fgrad)],
        in_specs=[vm] * 4,
        out_specs=[vm] * 6,
    )(rows, down, res, fgrad)


def local(
    frames, lengths, decay, read_gain, read_weight, norm_attn, w_qkv, w_out, norm_mlp, w_up, w_down,
    write_gain, write_weight, cotangent,
):
    sections, dp = lax.axis_size("section"), lax.axis_size("dp")
    clip_dev, span, tok, width = frames.shape
    hi = width // (sections * TILE)
    lo = dp // hi
    assert clip_dev == sections and span == 1 and hi * lo == dp
    res, fgrad, rows, down, sm = run_fused(
        sections, hi, lo, lengths, decay, (read_gain, norm_attn, norm_mlp, write_gain),
        [jnp.swapaxes(w, 1, 2) for w in (read_weight, write_weight)], frames, cotangent, (w_qkv, w_out, w_up, w_down),
    )
    *grads, res, fgrad = widen(rows, down, res, fgrad)
    grads = [g.reshape(LAYERS, BLOCKS, *g.shape[1:]) for g in grads]
    if lo > 1:
        groups = [[h * lo + k for k in range(lo)] for h in range(hi)]
        grads = [lax.psum_scatter(g, "dp", scatter_dimension=2, axis_index_groups=groups, tiled=True) for g in grads]
        sm = lax.psum_scatter(sm, "dp", scatter_dimension=1, axis_index_groups=groups, tiled=True)
    gain_grads = jnp.swapaxes(sm[:, :, READ + MEM:], 1, 2)
    return (
        res[:, None],
        fgrad[:, None],
        gain_grads[:, 0],
        sm[:, :, :READ],
        gain_grads[:, 1:1 + BLOCKS],
        grads[0],
        grads[1],
        gain_grads[:, 1 + BLOCKS:1 + 2 * BLOCKS],
        grads[2],
        grads[3],
        gain_grads[:, 1 + 2 * BLOCKS],
        sm[:, :, READ:READ + MEM],
    )


def solution(mesh):
    both = ("section", "dp")
    split = P("dp", "section", None, None)
    return jax.shard_map(
        local,
        mesh=mesh,
        in_specs=(split, P("dp")) + (P(),) * 11 + (split,),
        out_specs=(
            split, split, P(None, both), P(None, both, None), P(None, None, both), P(None, None, both, None),
            P(None, None, both, None), P(None, None, both), P(None, None, both, None),
            P(None, None, both, None), P(None, both), P(None, both, None),
        ),
        check_vma=False,
    )
```

```python
import functools

import jax
import jax.numpy as jnp
from jax import lax
from jax.experimental import pallas as pl
from jax.experimental.pallas import tpu as pltpu
from jax.sharding import PartitionSpec as P

HEADS = 8
HEAD = 64
MEM = 96
READ = 16
BLOCKS = 2
LAYERS = 2
EPS = 1e-05
SMALL = 128
TILE = 16
BF = jnp.bfloat16
F32 = jnp.float32


def nn(a, b):
    return lax.dot_general(a, b, (((1,), (0,)), ((), ())), preferred_element_type=F32)


def nt(a, b):
    return lax.dot_general(a, b, (((1,), (1,)), ((), ())), preferred_element_type=F32)


def tn(a, b):
    return lax.dot_general(a, b, (((0,), (0,)), ((), ())), preferred_element_type=F32)


def normalize(v):
    centred = v - jnp.mean(v, axis=-1, keepdims=True)
    spread = jnp.mean(centred * centred, axis=-1, keepdims=True)
    r = lax.rsqrt(spread + EPS)
    return centred * r, r


def normalize_back(dx, xh, r):
    return r * (dx - jnp.mean(dx, axis=-1, keepdims=True) - xh * jnp.mean(dx * xh, axis=-1, keepdims=True))


def gelu_and_slope(x):
    c0, c1 = 0.7978845608028654, 0.044715
    x2 = x * x
    t = jnp.tanh(c0 * x * (1.0 + c1 * x2))
    return 0.5 * x * (1.0 + t), 0.5 * (1.0 + t) + 0.5 * x * (1.0 - t * t) * c0 * (1.0 + 3.0 * c1 * x2)


def softmax_lanes(v):
    e = jnp.exp(v - jnp.max(v, axis=1, keepdims=True))
    return e / jnp.sum(e, axis=1, keepdims=True)


def softmax_lanes_back(p, dp):
    return p * (dp - jnp.sum(p * dp, axis=1, keepdims=True))


def fused_kernel(
    hi, lo, len_ref, decay_ref, rg_ref, na_ref, nm_ref, wg_ref, rw_ref, ww_ref, frames_hbm, cot_hbm,
    wqkv_hbm, wout_hbm, wup_hbm, wdown_hbm, res_out, fgrad_out, rows_ref, down_ref, small_ref, scratch,
):
    (
        wqkv, wout, wup, wdown, frames_v, cot_v, res_v, fgrad_v, z0, z1, xh0, xh1, rs0, rs1, at0, at1, bt0, bt1,
        mem, dmem, dout, xa, ra, xm, rm, gp, qkv, pt, mask_ref, gains, dec_col, dsm_ref,
        slice_b, all_f, part_b, wgrad, into, small_t, small_in, small_sum, small_into,
        w_sem, f_send, f_recv, f_own, o_send, o_recv, o_own,
        a_send, a_recv, a_own, c_send, c_recv, s_send, s_recv, t_send, t_recv, d_send, d_recv, d_own,
    ) = scratch
    sections, frames = all_f.shape[1:3]
    width = dsm_ref.shape[-1]
    lbs = LAYERS * BLOCKS
    me, dp_at = lax.axis_index("section"), lax.axis_index("dp")
    bits = hi.bit_length() - 1
    own_bits = [(dp_at // (lo << k)) % 2 for k in range(bits)]
    partners = [dp_at + (1 - 2 * b) * (lo << k) for k, b in enumerate(own_bits)]
    peers = [(me + k) % sections for k in range(1, sections)]

    def weight_copies(lb):
        at = (lb // BLOCKS, lb % BLOCKS)
        pairs = ((wqkv_hbm, wqkv), (wout_hbm, wout), (wup_hbm, wup), (wdown_hbm, wdown))
        return [pltpu.make_async_copy(s.at[at], d.at[lb], w_sem.at[lb, i]) for i, (s, d) in enumerate(pairs)]

    barrier = pltpu.get_barrier_semaphore()
    for p in peers:
        pl.semaphore_signal(barrier, inc=1, device_id={"section": p}, device_id_type=pl.DeviceIdType.MESH)
    for p in partners:
        pl.semaphore_signal(barrier, inc=1, device_id={"dp": p}, device_id_type=pl.DeviceIdType.MESH)

    def remote(src, dst, send, recv, device):
        return pltpu.make_async_remote_copy(
            src_ref=src, dst_ref=dst, send_sem=send, recv_sem=recv, device_id=device, device_id_type=pl.DeviceIdType.MESH
        )

    def forward_copies(l, first, count):
        at = pl.ds(first, count)
        return [
            remote(all_f.at[l, me, at], all_f.at[l, me, at], a_send.at[l, k, 0], a_recv.at[l, k, 0], {"section": p})
            for k, p in enumerate(peers)
        ]

    def backward_copies(l, first, count):
        at = pl.ds(first, count)
        return [
            remote(slice_b.at[l, p, at], part_b.at[l, me, at], a_send.at[l, k, 1], a_recv.at[l, k, 1], {"section": p})
            for k, p in enumerate(peers)
        ]

    def own_backward(l, first, count):
        at = pl.ds(first, count)
        return pltpu.make_async_copy(slice_b.at[l, me, at], part_b.at[l, me, at], a_own.at[l])

    def start_forward(l, f):
        for c in forward_copies(l, f, 1):
            c.start()

    def start_backward(l, f):
        for c in backward_copies(l, f, 1) + [own_backward(l, f, 1)]:
            c.start()

    def wait_factors(l):
        own_backward(l, 0, frames).wait()
        for c in forward_copies(l, 0, frames) + backward_copies(l, 0, frames):
            c.wait_recv()

    def start_small(l):
        small_t[l] = jnp.transpose(dsm_ref[l]).reshape(small_t.shape[1:])
        for c in small_copies(l):
            c.start()

    def small_copies(l):
        return [
            remote(small_t.at[l, p], small_in.at[l, me], s_send.at[l, k], s_recv.at[l, k], {"section": p})
            for k, p in enumerate(peers)
        ]

    def halves(ref, lead, k, other):
        b = own_bits[k]
        at = lead + (slice(None),) * (bits - 1 - k) + ((1 - b) if other else b,) + tuple(own_bits[k - 1::-1] if k else ())
        return at

    def halving_copy(u, k):
        src = wgrad.at[halves(wgrad, (u,), k, True)]
        return remote(src, into[k].at[u], c_send.at[u, k], c_recv.at[u, k], {"dp": partners[k]})

    def small_halving_copy(l, k):
        src = small_sum.at[halves(small_sum, (l,), k, True)]
        return remote(src, small_into[k].at[l], t_send.at[l, k], t_recv.at[l, k], {"dp": partners[k]})

    own_at = tuple(own_bits[::-1])
    cols = wgrad.shape[-1] - width

    def row_copies(u):
        return [
            remote(
                wgrad.at[(u,) + own_at + (pl.ds(pl.multiple_of(p * TILE, TILE), TILE), pl.ds(0, cols))],
                rows_ref.at[u, me], d_send.at[u, k], d_recv.at[u, k], {"section": p},
            )
            for k, p in enumerate(peers)
        ]

    def final_copies(u):
        here = wgrad.at[(u,) + own_at + (pl.ds(pl.multiple_of(me * TILE, TILE), TILE), pl.ds(0, cols))]
        down = wgrad.at[(u,) + own_at + (slice(None), pl.ds(cols, width))]
        return [
            pltpu.make_async_copy(here, rows_ref.at[u, me], d_own.at[u, 0]),
            pltpu.make_async_copy(down, down_ref.at[u], d_own.at[u, 1]),
        ]

    def store_rows(u, first, v):
        c = v.shape[1]
        v = v.astype(BF).reshape(sections, hi, TILE, c)
        for s in range(sections):
            for h in range(hi):
                at = tuple((h >> k) & 1 for k in range(bits - 1, -1, -1))
                wgrad[(u,) + at + (slice(s * TILE, (s + 1) * TILE), slice(first, first + c))] = v[s, h]

    def store_down(u, first, v):
        c = v.shape[1]
        v = v.astype(BF).reshape(hi, sections * TILE, c)
        for h in range(hi):
            at = tuple((h >> k) & 1 for k in range(bits - 1, -1, -1))
            wgrad[(u,) + at + (slice(None), slice(first, first + c))] = v[h]

    def form(u):
        l, b = u // BLOCKS, u % BLOCKS
        q, o = 3 * width // sections, 4 * width // sections
        ff = wup.shape[-1] // sections

        def flat(ref, first, count):
            v = ref[l, :, :, b, :, first:first + count]
            return v.reshape(sections * frames * READ, count)

        own_ff = pl.ds(pl.multiple_of(me * ff, ff), ff)
        u_all, dh_all = flat(all_f, 2 * width, width), flat(part_b, o, width)
        lift, slope = gelu_and_slope(nn(u_all, wup[u, :, own_ff]))
        dup = (nt(dh_all, wdown[u, own_ff, :]) * slope).astype(BF)
        store_rows(u, 0, tn(flat(all_f, 0, width), flat(part_b, 0, q)))
        store_rows(u, q, tn(flat(all_f, width, width), flat(part_b, q, o - q)))
        store_rows(u, o, tn(u_all, dup))
        store_down(u, cols, tn(lift.astype(BF), dh_all))
        halving_copy(u, 0).start()
        if u % BLOCKS == 0:
            l = u // BLOCKS
            for c in small_copies(l):
                c.wait_recv()
            total = small_t[l, me]
            for k in range(1, sections):
                total = total + small_in[l, (me + k) % sections]
            total = total.reshape(hi, TILE, SMALL)
            for h in range(hi):
                at = tuple((h >> k) & 1 for k in range(bits - 1, -1, -1))
                small_sum[(l,) + at] = total[h]
            small_halving_copy(l, 0).start()

    def halve(u, k):
        halving_copy(u, k).wait_recv()
        at = halves(wgrad, (u,), k, False)
        wgrad[at] = wgrad[at] + into[k][u]
        if k + 1 < bits:
            halving_copy(u, k + 1).start()
        else:
            for c in row_copies(u) + final_copies(u):
                c.start()
        if u % BLOCKS == 0:
            l = u // BLOCKS
            small_halving_copy(l, k).wait_recv()
            at = halves(small_sum, (l,), k, False)
            small_sum[at] = small_sum[at] + small_into[k][l]
            if k + 1 < bits:
                small_halving_copy(l, k + 1).start()
            else:
                small_ref[l] = small_sum[(l,) + own_at]

    def finish(u):
        for c in final_copies(u):
            c.wait()
        for c in row_copies(u):
            c.wait()
        for k in range(bits):
            halving_copy(u, k).wait_send()
        if u % BLOCKS == 0:
            l = u // BLOCKS
            for c in forward_copies(l, 0, frames) + backward_copies(l, 0, frames):
                c.wait_send()
            for c in small_copies(l):
                c.wait_send()
            for k in range(bits):
                small_halving_copy(l, k).wait_send()

    def frame_copies():
        return [
            remote(src.at[p, 0], dst.at[me], f_send.at[k, i], f_recv.at[k, i], {"section": p})
            for k, p in enumerate(peers)
            for i, (src, dst) in enumerate(((frames_hbm, frames_v), (cot_hbm, cot_v)))
        ]

    def own_frames():
        return [
            pltpu.make_async_copy(src.at[me, 0], dst.at[me], f_own.at[i])
            for i, (src, dst) in enumerate(((frames_hbm, frames_v), (cot_hbm, cot_v)))
        ]

    def output_copies(i, src, dst):
        copies = [
            remote(src.at[p], dst.at[me], o_send.at[k, i], o_recv.at[k, i], {"section": p}) for k, p in enumerate(peers)
        ]
        return copies, pltpu.make_async_copy(src.at[me], dst.at[me], o_own.at[i])

    def start_output(i, src, dst):
        copies, own = output_copies(i, src, dst)
        for c in copies + [own]:
            c.start()

    def spread_heads(v):
        return jnp.concatenate([v] * HEADS, axis=0) * mask_ref[...]

    def gather_heads(v):
        return jnp.sum((v * mask_ref[...].astype(F32)).reshape(HEADS, READ, width), axis=0)

    def live_at(f):
        return jnp.where(f < len_ref[me], 1.0, 0.0).astype(F32)

    def keep_slices(lb, f, first, v):
        c = v.shape[1] // sections
        for s in range(sections):
            slice_b[lb // BLOCKS, s, f, lb % BLOCKS, :, first:first + c] = v[:, s * c:(s + 1) * c]

    def add_gain_grad(l, i, v):
        dsm_ref[l, READ + MEM + i:READ + MEM + i + 1, :] += jnp.sum(v, axis=0, keepdims=True)

    def gain(i):
        return gains[i:i + 1, :]

    def block_forward(lb, f, h):
        xh, r = normalize(h)
        xa[lb, f], ra[lb, f] = xh, r
        g = (xh * gain(2 + lb)).astype(BF)
        all_f[lb // BLOCKS, me, f, lb % BLOCKS, :, :width] = g
        joined = nn(g, wqkv[lb]).astype(BF)
        qkv[lb, f] = joined
        q, k, v = joined[:, :width], joined[:, width:2 * width], joined[:, 2 * width:]
        s = nt(k, spread_heads(q)) * HEAD ** (-0.5)
        e = jnp.exp(s - jnp.max(s, axis=0, keepdims=True))
        p = e / jnp.sum(e, axis=0, keepdims=True)
        pt[lb, f] = p
        o = gather_heads(tn(p.astype(BF), v)).astype(BF)
        all_f[lb // BLOCKS, me, f, lb % BLOCKS, :, width:2 * width] = o
        h = h + nn(o, wout[lb])
        xh, r = normalize(h)
        xm[lb, f], rm[lb, f] = xh, r
        u = (xh * gain(6 + lb)).astype(BF)
        all_f[lb // BLOCKS, me, f, lb % BLOCKS, :, 2 * width:] = u
        x = nn(u, wup[lb])
        lift, gp[lb, f] = gelu_and_slope(x)
        lift = lift.astype(BF)
        return h + nn(lift, wdown[lb])

    def block_backward(lb, f, dh):
        dhb = dh.astype(BF)
        for s in range(sections):
            slice_b[lb // BLOCKS, s, f, lb % BLOCKS, :, 4 * width // sections:] = dhb
        dup = (nt(dhb, wdown[lb]) * gp[lb, f]).astype(BF)
        du = nt(dup, wup[lb])
        xh = xm[lb, f]
        add_gain_grad(lb // BLOCKS, 3 + lb % BLOCKS, du * xh)
        dh = dh + normalize_back(du * gain(6 + lb), xh, rm[lb, f])
        dhb = dh.astype(BF)
        keep_slices(lb, f, 3 * width // sections, dhb)
        do = spread_heads(nt(dhb, wout[lb]).astype(BF))
        joined = qkv[lb, f]
        q, k, v = joined[:, :width], joined[:, width:2 * width], joined[:, 2 * width:]
        p = pt[lb, f]
        dp = nt(v, do)
        ds = (p * (dp - jnp.sum(p * dp, axis=0, keepdims=True)) * HEAD ** (-0.5)).astype(BF)
        dv = nn(p.astype(BF), do)
        dk = nn(ds, spread_heads(q))
        dq = gather_heads(tn(ds, k))
        dj = jnp.concatenate([dq, dk, dv], axis=1).astype(BF)
        keep_slices(lb, f, 0, dj)
        dg = nt(dj, wqkv[lb])
        xh = xa[lb, f]
        add_gain_grad(lb // BLOCKS, 1 + lb % BLOCKS, dg * xh)
        return dh + normalize_back(dg * gain(2 + lb), xh, ra[lb, f])

    def layer_forward(l, f, z, xh_ref, rs_ref, at, bt, inputs):
        live = live_at(f)
        m = mem[...]
        rows = z.shape[1] - READ
        n_in = rows - MEM
        z[f, :n_in] = inputs
        z[f, n_in:rows] = m.astype(BF)
        zz = z[f, :rows]
        xh, r = normalize(zz.astype(F32))
        xh_ref[f, :rows], rs_ref[f, :rows] = xh, r
        n = (xh * gain(l)).astype(BF)
        a = softmax_lanes(nt(rw_ref[l], n))
        at[f] = a
        h = nn(a.astype(BF), zz)
        for b in range(BLOCKS):
            h = block_forward(l * BLOCKS + b, f, h)
        y = h.astype(BF)
        z[f, rows:] = y
        xh, r = normalize(y.astype(F32))
        xh_ref[f, rows:], rs_ref[f, rows:] = xh, r
        n = (xh_ref[f] * gain(10 + l)).astype(BF)
        b = softmax_lanes(nt(ww_ref[l], n))
        bt[f] = b
        written = nn(b.astype(BF), z[f])
        rate = dec_col[l]
        updated = rate * z[f, n_in:rows].astype(F32) + (1.0 - rate) * written
        mem[...] = live * updated + (1.0 - live) * m
        return (live * y.astype(F32)).astype(BF)

    def layer_backward(l, f, z, xh_ref, rs_ref, at, bt, dy_out):
        live = live_at(f)
        rows = z.shape[1] - READ
        n_in = rows - MEM
        dm = dmem[...]
        rate = dec_col[l]
        dt = ((live * (1.0 - rate)) * dm).astype(BF)
        zf = z[f]
        b = bt[f]
        dl = softmax_lanes_back(b, nt(dt, zf)).astype(BF)
        dz = tn(b.astype(BF), dt)
        dn = tn(dl, ww_ref[l])
        xh = xh_ref[f]
        dsm_ref[l, READ:READ + MEM] += nn(dl, (xh * gain(10 + l)).astype(BF))
        add_gain_grad(l, 5, dn * xh)
        dx = dn * gain(10 + l)
        dy = dz[rows:] + normalize_back(dx[rows:], xh[rows:], rs_ref[f, rows:]) + live * dy_out
        dh = dy.astype(BF).astype(F32)
        for bb in range(BLOCKS - 1, -1, -1):
            dh = block_backward(l * BLOCKS + bb, f, dh)
        ds = dh.astype(BF)
        xh = xh[:rows]
        a = at[f]
        dl = softmax_lanes_back(a, nt(ds, zf[:rows])).astype(BF)
        dz = dz[:rows] + tn(a.astype(BF), ds)
        dn = tn(dl, rw_ref[l])
        dsm_ref[l, :READ] += nn(dl, (xh * gain(l)).astype(BF))
        add_gain_grad(l, 0, dn * xh)
        dz = dz + normalize_back(dx[:rows] + dn * gain(l), xh, rs_ref[f, :rows])
        dmq = (dz[n_in:] + (live * rate) * dm).astype(BF).astype(F32)
        dmem[...] = dmq + (1.0 - live) * dm
        return dz[:n_in].astype(BF)

    for c in own_frames():
        c.start()
    for lb in range(lbs):
        for c in weight_copies(lb):
            c.start()
    row = lax.broadcasted_iota(jnp.int32, (HEADS * READ, width), 0) // READ
    col = lax.broadcasted_iota(jnp.int32, (HEADS * READ, width), 1) // HEAD
    mask_ref[...] = jnp.where(row == col, 1.0, 0.0).astype(BF)
    dsm_ref[...] = jnp.zeros_like(dsm_ref)
    for l in range(LAYERS):
        gains[l:l + 1] = rg_ref[...].astype(F32)[l:l + 1]
        gains[10 + l:11 + l] = wg_ref[...].astype(F32)[l:l + 1]
        for b in range(BLOCKS):
            lb = l * BLOCKS + b
            gains[2 + lb:3 + lb] = na_ref[l].astype(F32)[b:b + 1]
            gains[6 + lb:7 + lb] = nm_ref[l].astype(F32)[b:b + 1]
        spread = jnp.broadcast_to(decay_ref[l:l + 1], (MEM, MEM))
        diagonal = lax.broadcasted_iota(jnp.int32, (MEM, MEM), 0) == lax.broadcasted_iota(jnp.int32, (MEM, MEM), 1)
        dec_col[l] = jnp.sum(jnp.where(diagonal, spread, 0.0), axis=1, keepdims=True)

    pl.semaphore_wait(barrier, len(peers) + len(partners))
    for c in frame_copies():
        c.start()

    kept0 = (z0, xh0, rs0, at0, bt0)
    kept1 = (z1, xh1, rs1, at1, bt1)

    def wait_layer(l):
        for b in range(BLOCKS):
            for c in weight_copies(l * BLOCKS + b):
                c.wait()

    wait_layer(0)
    for c in own_frames():
        c.wait()
    for c in frame_copies():
        c.wait_recv()
    mem[...] = jnp.zeros_like(mem)

    def forward0(f, carry):
        dout[f] = layer_forward(0, f, *kept0, frames_v[f])
        start_forward(0, f)
        return carry

    lax.fori_loop(0, frames, forward0, 0)
    wait_layer(1)
    mem[...] = jnp.zeros_like(mem)

    def forward1(f, carry):
        res_v[f] = layer_forward(1, f, *kept1, dout[f])
        start_forward(1, f)
        return carry

    lax.fori_loop(0, frames, forward1, 0)
    start_output(0, res_v, res_out)
    dmem[...] = jnp.zeros_like(dmem)

    def backward1(i, carry):
        f = frames - 1 - i
        dout[f] = layer_backward(1, f, *kept1, cot_v[f].astype(F32))
        start_backward(1, f)
        return carry

    lax.fori_loop(0, frames, backward1, 0)
    start_small(1)
    dmem[...] = jnp.zeros_like(dmem)

    def backward0(i, carry):
        f = frames - 1 - i
        fgrad_v[f] = layer_backward(0, f, *kept0, dout[f].astype(F32))
        start_backward(0, f)

        @pl.when(i == 0)
        def _():
            wait_factors(1)
            form(3)
            form(2)
            halve(3, 0)

        @pl.when(i == 1)
        def _():
            halve(2, 0)

        @pl.when(i == 2)
        def _():
            halve(3, 1)

        return carry

    lax.fori_loop(0, frames, backward0, 0)
    start_small(0)
    start_output(1, fgrad_v, fgrad_out)
    halve(2, 1)
    wait_factors(0)
    form(1)
    form(0)
    halve(1, 0)
    halve(3, 2)
    halve(0, 0)
    halve(1, 1)
    halve(2, 2)
    halve(0, 1)
    halve(1, 2)
    halve(0, 2)
    for u in range(lbs - 1, -1, -1):
        finish(u)
    for i, (src, dst) in enumerate(((res_v, res_out), (fgrad_v, fgrad_out))):
        copies, own = output_copies(i, src, dst)
        for c in copies + [own]:
            c.wait()
    for c in frame_copies():
        c.wait_send()


def run_fused(sections, hi, lo, lengths, decay, gains, small, frames, cot, weights):
    count, _, tok, width = frames.shape
    lbs = LAYERS * BLOCKS
    ff = weights[2].shape[-1]
    cols = (4 * width + ff) // sections
    all_cols = cols + width
    bits = hi.bit_length() - 1
    chunk = sections * TILE
    peers = sections - 1
    vm, anym = pl.BlockSpec(memory_space=pltpu.VMEM), pl.BlockSpec(memory_space=pl.ANY)
    v, dma = pltpu.VMEM, pltpu.SemaphoreType.DMA

    def sds(shape, dtype):
        return jax.ShapeDtypeStruct(shape, dtype)

    def per(c, dtype):
        return v((lbs, count, READ, c), dtype)

    def by_section(c):
        return v((LAYERS, sections, count, BLOCKS, READ, c), BF)

    rows0, rows1 = tok + MEM, READ + MEM
    scratch = [v((lbs,) + w.shape[2:], BF) for w in weights]
    scratch += [v((count, tok, width), BF), v((count, READ, width), BF)]
    scratch += [v((count, READ, width), BF), v((count, tok, width), BF)]
    scratch += [v((count, r + READ, width), BF) for r in (rows0, rows1)]
    scratch += [v((count, r + READ, width), F32) for r in (rows0, rows1)]
    scratch += [v((count, r + READ, 1), F32) for r in (rows0, rows1)]
    scratch += [v((count, READ, r), F32) for r in (rows0, rows1)]
    scratch += [v((count, MEM, r + READ), F32) for r in (rows0, rows1)]
    scratch += [v((MEM, width), F32), v((MEM, width), F32), v((count, READ, width), BF)]
    scratch += [per(width, F32), per(1, F32), per(width, F32), per(1, F32)]
    scratch += [per(ff, F32), per(3 * width, BF), per(HEADS * READ, F32)]
    scratch += [v((HEADS * READ, width), BF), v((12, width), F32), v((LAYERS, MEM, 1), F32)]
    scratch += [v((LAYERS, SMALL, width), F32)]
    sliced = 4 * width // sections + width
    scratch += [by_section(sliced), by_section(3 * width), by_section(sliced)]
    scratch += [v((lbs,) + (2,) * bits + (chunk, all_cols), BF)]
    scratch += [[v((lbs,) + (2,) * (bits - 1 - k) + (chunk, all_cols), BF) for k in range(bits)]]
    scratch += [v((LAYERS, sections, width // sections, SMALL), F32)] * 2
    scratch += [v((LAYERS,) + (2,) * bits + (TILE, SMALL), F32)]
    scratch += [[v((LAYERS,) + (2,) * (bits - 1 - k) + (TILE, SMALL), F32) for k in range(bits)]]
    scratch += [dma((lbs, 4)), dma((peers, 2)), dma((peers, 2)), dma((2,)), dma((peers, 2)), dma((peers, 2)), dma((2,))]
    scratch += [dma((LAYERS, peers, 2)), dma((LAYERS, peers, 2)), dma((LAYERS,)), dma((lbs, bits)), dma((lbs, bits))]
    scratch += [dma((LAYERS, peers)), dma((LAYERS, peers)), dma((LAYERS, bits)), dma((LAYERS, bits))]
    scratch += [dma((lbs, peers)), dma((lbs, peers)), dma((lbs, 2))]
    return pl.pallas_call(
        functools.partial(fused_kernel, hi, lo),
        out_shape=[
            sds((count, READ, width), BF),
            sds((count, tok, width), BF),
            sds((lbs, sections, TILE, cols), BF),
            sds((lbs, chunk, width), BF),
            sds((LAYERS, TILE, SMALL), F32),
        ],
        in_specs=[pl.BlockSpec(memory_space=pltpu.SMEM)] + [vm] * 7 + [anym] * 6,
        out_specs=[vm] * 5,
        scratch_shapes=[scratch],
        compiler_params=pltpu.CompilerParams(
            collective_id=0, has_side_effects=True, vmem_limit_bytes=64 * 2**20 - 2**16
        ),
    )(lengths, decay, *gains, *small, frames, cot, *weights)


def widen_kernel(
    rows_ref, down_ref, small_ref, res_ref, fgrad_ref,
    res_out, fgrad_out, rg_out, rw_out, na_out, qkv_out, out_out, nm_out, up_out, down_out, wg_out, ww_out,
):
    sections, tile = rows_ref.shape[1:3]
    lbs = LAYERS * BLOCKS
    res_out[...] = res_ref[...]
    fgrad_out[...] = fgrad_ref[...]
    cols = [ref.shape[-1] // sections for ref in (qkv_out, out_out, up_out)]
    for u in range(lbs):
        l, b = u // BLOCKS, u % BLOCKS
        for s in range(sections):
            first = 0
            for ref, c in zip((qkv_out, out_out, up_out), cols):
                ref[l, b, :, s * c:(s + 1) * c] = rows_ref[u, s, :, first:first + c].astype(F32)
                first += c
        down_out[l, b] = down_ref[u].astype(F32)
    diagonal = lax.broadcasted_iota(jnp.int32, (tile, tile), 0) == lax.broadcasted_iota(jnp.int32, (tile, tile), 1)

    def as_row(l, i):
        column = jnp.broadcast_to(small_ref[l][:, READ + MEM + i:READ + MEM + i + 1], (tile, tile))
        return jnp.sum(jnp.where(diagonal, column, 0.0), axis=0, keepdims=True)

    for l in range(LAYERS):
        rw_out[l] = small_ref[l][:, :READ]
        ww_out[l] = small_ref[l][:, READ:READ + MEM]
        rg_out[l:l + 1] = as_row(l, 0)
        wg_out[l:l + 1] = as_row(l, 1 + 2 * BLOCKS)
        for b in range(BLOCKS):
            na_out[l, b:b + 1] = as_row(l, 1 + b)
            nm_out[l, b:b + 1] = as_row(l, 1 + BLOCKS + b)


def widen(rows, down, sm, res, fgrad):
    sections, tile, cols = rows.shape[1:]
    width = down.shape[-1]
    vm = pl.BlockSpec(memory_space=pltpu.VMEM)

    def f32(*shape):
        return jax.ShapeDtypeStruct((LAYERS,) + shape, F32)

    out_shape = [jax.ShapeDtypeStruct(a.shape, a.dtype) for a in (res, fgrad)] + [
        f32(tile), f32(tile, READ), f32(BLOCKS, tile), f32(BLOCKS, tile, 3 * width), f32(BLOCKS, tile, width),
        f32(BLOCKS, tile), f32(BLOCKS, tile, sections * cols - 4 * width), f32(BLOCKS, *down.shape[1:]),
        f32(tile), f32(tile, MEM),
    ]
    return pl.pallas_call(
        widen_kernel, out_shape=out_shape, in_specs=[vm] * 5, out_specs=[vm] * len(out_shape)
    )(rows, down, sm, res, fgrad)


def local(
    frames, lengths, decay, read_gain, read_weight, norm_attn, w_qkv, w_out, norm_mlp, w_up, w_down,
    write_gain, write_weight, cotangent,
):
    sections, dp = lax.axis_size("section"), lax.axis_size("dp")
    clip_dev, span, tok, width = frames.shape
    hi = width // (sections * TILE)
    lo = dp // hi
    assert clip_dev == sections and span == 1 and hi * lo == dp
    res, fgrad, rows, down, sm = run_fused(
        sections, hi, lo, lengths, decay, (read_gain, norm_attn, norm_mlp, write_gain),
        [jnp.swapaxes(w, 1, 2) for w in (read_weight, write_weight)], frames, cotangent, (w_qkv, w_out, w_up, w_down),
    )
    if lo > 1:
        groups = [[h * lo + k for k in range(lo)] for h in range(hi)]

        def over_rest(v, axis):
            return lax.psum_scatter(
                v.astype(F32), "dp", scatter_dimension=axis, axis_index_groups=groups, tiled=True
            )

        rows, down, sm = over_rest(rows, 2), over_rest(down, 1), over_rest(sm, 1)
    res, fgrad, *grads = widen(rows, down, sm, res, fgrad)
    return (res[:, None], fgrad[:, None], *grads)


def solution(mesh):
    both = ("section", "dp")
    split = P("dp", "section", None, None)
    return jax.shard_map(
        local,
        mesh=mesh,
        in_specs=(split, P("dp")) + (P(),) * 11 + (split,),
        out_specs=(
            split, split, P(None, both), P(None, both, None), P(None, None, both), P(None, None, both, None),
            P(None, None, both, None), P(None, None, both), P(None, None, both, None),
            P(None, None, both, None), P(None, both), P(None, both, None),
        ),
        check_vma=False,
    )
```

```python
import functools

import jax
import jax.numpy as jnp
from jax import lax
from jax.experimental import pallas as pl
from jax.experimental.pallas import tpu as pltpu
from jax.sharding import PartitionSpec as P

HEADS = 8
HEAD = 64
MEM = 96
READ = 16
BLOCKS = 2
LAYERS = 2
EPS = 1e-05
SMALL = 128
TILE = 16
PIECES = 2
S0, S1, D0, D1, D2 = ("section", 0), ("section", 1), ("dp", 0), ("dp", 1), ("dp", 2)
ROW_BITS = (S1, S0, D2, D1, D0)
GROUP = ((S0, D1), (S0, D1))
SUM = ((D0, S1, D2), (D0, S1, D2))


def free_bits(l):
    return tuple(b for b in ROW_BITS if b not in GROUP[l] and b != D0)


def run_start(bit, l, j, fixed):
    free = free_bits(l)
    value = {b: (j >> (len(free) - 1 - i)) & 1 for i, b in enumerate(free)} | fixed
    return sum(value[b] * (bit << (len(ROW_BITS) - 2 - i)) for i, b in enumerate(ROW_BITS[:-1]))
BF = jnp.bfloat16
F32 = jnp.float32


def nn(a, b):
    return lax.dot_general(a, b, (((1,), (0,)), ((), ())), preferred_element_type=F32)


def nt(a, b):
    return lax.dot_general(a, b, (((1,), (1,)), ((), ())), preferred_element_type=F32)


def tn(a, b):
    return lax.dot_general(a, b, (((0,), (0,)), ((), ())), preferred_element_type=F32)


def normalize(v):
    centred = v - jnp.mean(v, axis=-1, keepdims=True)
    spread = jnp.mean(centred * centred, axis=-1, keepdims=True)
    r = lax.rsqrt(spread + EPS)
    return centred * r, r


def normalize_back(dx, xh, r):
    return r * (dx - jnp.mean(dx, axis=-1, keepdims=True) - xh * jnp.mean(dx * xh, axis=-1, keepdims=True))


def gelu_and_slope(x):
    c0, c1 = 0.7978845608028654, 0.044715
    x2 = x * x
    t = jnp.tanh(c0 * x * (1.0 + c1 * x2))
    return 0.5 * x * (1.0 + t), 0.5 * (1.0 + t) + 0.5 * x * (1.0 - t * t) * c0 * (1.0 + 3.0 * c1 * x2)


def softmax_lanes(v):
    e = jnp.exp(v - jnp.max(v, axis=1, keepdims=True))
    return e / jnp.sum(e, axis=1, keepdims=True)


def softmax_lanes_back(p, dp):
    return p * (dp - jnp.sum(p * dp, axis=1, keepdims=True))


def fused_kernel(
    hi, lo, len_ref, decay_ref, rg_ref, na_ref, nm_ref, wg_ref, rw_ref, ww_ref, frames_hbm, cot_hbm,
    wqkv_hbm, wout_hbm, wup_hbm, wdown_hbm, res_out, fgrad_out, rows_ref, down_ref, small_ref,
    tq_hbm, to_hbm, tu_hbm, td_hbm, scratch,
):
    (
        wq, wo, wu, wd, cot_v, res_v, z0, z1, xh0, xh1, rs0, rs1, at0, at1, bt0, bt1,
        mem, dmem, dout, xa, ra, xm, rm, gp, qkv, pt, mask_ref, gains, dec_col, dsm_ref,
        slice_b, all_f, part_b, wgrad, into, small_t, small_in, small_sum, small_into,
        w_sem, v_sem, t_sem, f_send, f_recv, f_own, o_send, o_recv, o_own,
        a_send, a_recv, a_own, c_send, c_recv, s_send, s_recv, t_send, t_recv, d_send, d_recv, d_own,
    ) = scratch
    sections, frames = all_f.shape[1:3]
    tokens0 = pl.ds(0, frames_hbm.shape[2])
    width = dsm_ref.shape[-1]
    lbs = LAYERS * BLOCKS
    me, dp_at = lax.axis_index("section"), lax.axis_index("dp")
    bits = hi.bit_length() - 1
    peers = [(me + k) % sections for k in range(1, sections)]
    members = 1 << len(GROUP[0])
    own = {S0: me % 2, S1: (me // 2) % 2} | {("dp", k): (dp_at // (lo << k)) % 2 for k in range(bits)}
    assert sections == 4 and bits == 3

    def device(flips):
        s, d = me, dp_at
        for axis, k in flips:
            step = 1 - 2 * own[axis, k]
            s, d = (s + step * (1 << k), d) if axis == "section" else (s, d + step * (lo << k))
        return {"section": s, "dp": d}

    def flips_of(l, x):
        return tuple(b for j, b in enumerate(GROUP[l]) if (x >> j) & 1)

    def member(l, x):
        return sum((1 - own[b] if (x >> j) & 1 else own[b]) * (1 << j) for j, b in enumerate(GROUP[l]))

    here = [member(l, 0) for l in range(LAYERS)]

    every = (slice(None),) * (bits + 1)
    ups = wd.shape[2]

    def columns(i):
        return every + (pl.ds(i * width, width),)

    def weight_copies(l, b):
        pairs = [(wqkv_hbm.at[(l, b) + columns(i)], wq.at[l, b, i]) for i in range(3)]
        pairs += [(wout_hbm.at[l, b], wo.at[l, b]), (wup_hbm.at[l, b], wu.at[l, b]), (wdown_hbm.at[l, b], wd.at[l, b])]
        return [pltpu.make_async_copy(s, d, w_sem.at[l, b, i]) for i, (s, d) in enumerate(pairs)]

    def squares(l, b, to_q, to_o, to_u, to_d, l_to):
        out = [(wq.at[l, b, i], to_q.at[l_to, b, i]) for i in range(3)] + [(wo.at[l, b], to_o.at[l_to, b])]
        for i in range(ups):
            out.append((wu.at[(l, b) + columns(i)], to_d.at[l_to, b, i]))
            out.append((wd.at[l, b, i], to_u.at[(l_to, b) + columns(i)]))
        return out

    def staged(i):
        return wgrad.at[(i // 3,) + columns(i % 3)]

    def square_copies(l, b):
        pairs = squares(l, b, tq_hbm, to_hbm, tu_hbm, td_hbm, l)
        return [pltpu.make_async_copy(staged(i), d, t_sem.at[i]) for i, (_, d) in enumerate(pairs)]

    def transpose_block(lb, carry):
        l, b = lb // BLOCKS, lb % BLOCKS
        for c in weight_copies(l, b):
            c.wait()
        copies = square_copies(l, b)
        for i, (s, _) in enumerate(squares(l, b, tq_hbm, to_hbm, tu_hbm, td_hbm, l)):
            pl.when(lb > 0)(copies[i].wait)
            staged(i)[...] = s[...].reshape(width, width).T.reshape(s.shape)
            pl.when(lb < lbs - 1)(copies[i].start)
        return carry

    def transposed_copies(l):
        out = []
        for b in range(BLOCKS):
            if l * BLOCKS + b == lbs - 1:
                pairs = squares(l, b, wq, wo, wu, wd, 1 - l)
                out += [pltpu.make_async_copy(staged(i), d, t_sem.at[i]) for i, (_, d) in enumerate(pairs)]
            else:
                pairs = ((tq_hbm, wq), (to_hbm, wo), (tu_hbm, wu), (td_hbm, wd))
                out += [pltpu.make_async_copy(s.at[l, b], d.at[1 - l, b], v_sem.at[l, b, i]) for i, (s, d) in enumerate(pairs)]
        return out

    def weight(ref, *at):
        w = ref[at]
        return w.reshape(-1, w.shape[-1])

    barrier = pltpu.get_barrier_semaphore()
    partners = {(S0,), (S1,), (S0, S1)} | {(b,) for bits_of in SUM for b in bits_of}
    partners |= {tuple(sorted(flips_of(l, x))) for l in range(LAYERS) for x in range(1, members)}
    partners = sorted({tuple(sorted(p)) for p in partners})
    for p in partners:
        pl.semaphore_signal(barrier, inc=1, device_id=device(p), device_id_type=pl.DeviceIdType.MESH)

    def remote(src, dst, send, recv, to):
        return pltpu.make_async_remote_copy(
            src_ref=src, dst_ref=dst, send_sem=send, recv_sem=recv, device_id=to, device_id_type=pl.DeviceIdType.MESH
        )

    def forward_copies(l, first, count):
        at = all_f.at[l, here[l], pl.ds(first, count)]
        return [
            remote(at, at, a_send.at[l, x - 1, 0], a_recv.at[l, x - 1, 0], device(flips_of(l, x)))
            for x in range(1, members)
        ]

    def backward_copies(l, first, count):
        at = pl.ds(first, count)
        return [
            remote(
                slice_b.at[l, member(l, x), at], part_b.at[l, here[l], at],
                a_send.at[l, x - 1, 1], a_recv.at[l, x - 1, 1], device(flips_of(l, x)),
            )
            for x in range(1, members)
        ]

    def own_backward(l, first, count):
        at = pl.ds(first, count)
        return pltpu.make_async_copy(slice_b.at[l, here[l], at], part_b.at[l, here[l], at], a_own.at[l])

    def start_forward(l, f):
        for c in forward_copies(l, f, 1):
            c.start()

    def start_backward(l, f):
        for c in backward_copies(l, f, 1) + [own_backward(l, f, 1)]:
            c.start()

    def wait_factors(l):
        own_backward(l, 0, frames).wait()
        for c in forward_copies(l, 0, frames) + backward_copies(l, 0, frames):
            c.wait_recv()

    def place(l, s, h):
        value = {("section", k): (s >> k) & 1 for k in range(2)} | {("dp", k): (h >> k) & 1 for k in range(bits)}
        return tuple(value[b] for b in reversed(SUM[l])), sum(value[b] << j for j, b in enumerate(GROUP[l]))

    def start_small(l):
        rows = jnp.transpose(dsm_ref[l]).reshape(sections, hi, TILE, SMALL)
        for s in range(sections):
            for h in range(hi):
                at, g = place(l, s, h)
                small_t[(l, g) + at] = rows[s, h]
        for c in small_copies(l):
            c.start()

    def small_copies(l):
        return [
            remote(
                small_t.at[l, member(l, x)], small_in.at[l, here[l]],
                s_send.at[l, x - 1], s_recv.at[l, x - 1], device(flips_of(l, x)),
            )
            for x in range(1, members)
        ]

    def halves(l, k, other):
        b = own[SUM[l][k]]
        fixed = tuple(own[SUM[l][j]] for j in range(k - 1, -1, -1))
        return (slice(None),) * (bits - 1 - k) + ((1 - b) if other else b,) + fixed

    def own_at(l):
        return tuple(own[b] for b in reversed(SUM[l]))

    def piece(p):
        size = wgrad.shape[-1] // PIECES
        return (slice(None), pl.ds(p * size, size))

    def halving_copy(u, k, p):
        l = u // BLOCKS
        return remote(
            wgrad.at[(u,) + halves(l, k, True) + piece(p)],
            into[k].at[(u,) + (slice(None),) * (bits - 1 - k) + piece(p)],
            c_send.at[u, k, p], c_recv.at[u, k, p], device((SUM[l][k],)),
        )

    def small_halving_copy(l, k):
        return remote(
            small_sum.at[(l,) + halves(l, k, True)], small_into[k].at[l], t_send.at[l, k], t_recv.at[l, k],
            device((SUM[l][k],)),
        )

    cols = wgrad.shape[-1] - width

    def own_rows(u, g):
        return wgrad.at[(u,) + own_at(u // BLOCKS) + (pl.ds(pl.multiple_of(g * TILE, TILE), TILE), pl.ds(0, cols))]

    def row_copies(u):
        l = u // BLOCKS
        return [
            remote(
                own_rows(u, member(l, x)), rows_ref.at[u, here[l]], d_send.at[u, x - 1], d_recv.at[u, x - 1],
                device(flips_of(l, x)),
            )
            for x in range(1, members)
        ]

    def final_copies(u):
        l = u // BLOCKS
        down = wgrad.at[(u,) + own_at(l) + (slice(None), pl.ds(cols, width))]
        return [
            pltpu.make_async_copy(own_rows(u, here[l]), rows_ref.at[u, here[l]], d_own.at[u, 0]),
            pltpu.make_async_copy(down, down_ref.at[u], d_own.at[u, 1]),
        ]

    def store_rows(u, first, v):
        c = v.shape[1]
        v = v.astype(BF).reshape(sections, hi, TILE, c)
        for s in range(sections):
            for h in range(hi):
                at, g = place(u // BLOCKS, s, h)
                wgrad[(u,) + at + (slice(g * TILE, (g + 1) * TILE), slice(first, first + c))] = v[s, h]

    def store_down(u, first, v):
        l = u // BLOCKS
        c = v.shape[1]
        order = free_bits(l) + (D0,)
        v = v.astype(BF).reshape(1 << len(order), members * TILE, c)
        for j in range(1 << len(order)):
            value = {b: (j >> (len(order) - 1 - i)) & 1 for i, b in enumerate(order)}
            at = tuple(value[b] for b in reversed(SUM[l]))
            wgrad[(u,) + at + (slice(None), slice(first, first + c))] = v[j]

    def form(u):
        l, b = u // BLOCKS, u % BLOCKS
        q, o = 3 * width // members, 4 * width // members
        runs = 1 << len(free_bits(l))
        run = wu.shape[-1] // (members * runs)
        fixed = {bit: own[bit] for bit in GROUP[l]}

        def flat(ref, first, count):
            v = ref[l, :, :, b, :, first:first + count]
            return v.reshape(members * frames * READ, count)

        def up_run(j):
            at = {bit: (j >> (len(free_bits(l)) - 1 - i)) & 1 for i, bit in enumerate(free_bits(l))} | fixed
            w = wd[1 - l, b, 2 * at[S1] + at[S0], at[D2], at[D1]]
            return w.reshape(-1, w.shape[-1])

        def down_run(j):
            start = pl.multiple_of(run_start(run, l, j, fixed), run)
            return weight(wu, 1 - l, b, *every, pl.ds(start, run))

        u_all, dh_all = flat(all_f, 2 * width, width), flat(part_b, o, width)
        up_rows = jnp.concatenate([up_run(j) for j in range(runs)], axis=0)
        down_cols = jnp.concatenate([down_run(j) for j in range(runs)], axis=1)
        lift, slope = gelu_and_slope(nt(u_all, up_rows))
        dup = (nn(dh_all, down_cols) * slope).astype(BF)
        store_rows(u, 0, tn(flat(all_f, 0, width), flat(part_b, 0, q)))
        store_rows(u, q, tn(flat(all_f, width, width), flat(part_b, q, o - q)))
        store_rows(u, o, tn(u_all, dup))
        store_down(u, cols, tn(lift.astype(BF), dh_all))
        for p in range(PIECES):
            halving_copy(u, 0, p).start()
        if b == 0:
            for c in small_copies(l):
                c.wait_recv()
            total = small_t[l, here[l]]
            for x in range(1, members):
                total = total + small_in[l, member(l, x)]
            small_sum[l] = total
            small_halving_copy(l, 0).start()

    def halve(u, k, p):
        l = u // BLOCKS
        halving_copy(u, k, p).wait_recv()
        at = (u,) + halves(l, k, False) + piece(p)
        wgrad[at] = wgrad[at] + into[k][(u,) + (slice(None),) * (bits - 1 - k) + piece(p)]
        if k + 1 < bits:
            halving_copy(u, k + 1, p).start()
        elif p + 1 == PIECES:
            for c in row_copies(u) + final_copies(u):
                c.start()
        if u % BLOCKS == 0 and p == 0:
            small_halving_copy(l, k).wait_recv()
            at = (l,) + halves(l, k, False)
            small_sum[at] = small_sum[at] + small_into[k][l]
            if k + 1 < bits:
                small_halving_copy(l, k + 1).start()
            else:
                small_ref[l] = small_sum[(l,) + own_at(l)]

    def finish(u):
        for c in final_copies(u) + row_copies(u):
            c.wait()
        for k in range(bits):
            for p in range(PIECES):
                halving_copy(u, k, p).wait_send()
        if u % BLOCKS == 0:
            l = u // BLOCKS
            for c in forward_copies(l, 0, frames) + backward_copies(l, 0, frames) + small_copies(l):
                c.wait_send()
            for k in range(bits):
                small_halving_copy(l, k).wait_send()

    def frame_copies():
        return [
            remote(src.at[p, 0], dst, f_send.at[k, i], f_recv.at[k, i], {"section": p})
            for k, p in enumerate(peers)
            for i, (src, dst) in enumerate(((frames_hbm, z0.at[me, tokens0]), (cot_hbm, cot_v.at[me])))
        ]

    def own_frames():
        return [
            pltpu.make_async_copy(src.at[me, 0], dst, f_own.at[i])
            for i, (src, dst) in enumerate(((frames_hbm, z0.at[me, tokens0]), (cot_hbm, cot_v.at[me])))
        ]

    def output_copies(i, src, dst):
        copies = [
            remote(src(p), dst.at[me], o_send.at[k, i], o_recv.at[k, i], {"section": p}) for k, p in enumerate(peers)
        ]
        return copies, pltpu.make_async_copy(src(me), dst.at[me], o_own.at[i])

    results = (0, lambda f: res_v.at[f], res_out)
    frame_grads = (1, lambda f: z0.at[f, tokens0], fgrad_out)

    def start_frame_grad(f):
        _, src, dst = frame_grads
        k = (f - me + sections) % sections

        @pl.when(k == 0)
        def _():
            output_copies(*frame_grads)[1].start()

        @pl.when(k > 0)
        def _():
            at = (lax.max(k - 1, 0), 1)
            remote(src(f), dst.at[me], o_send.at[at], o_recv.at[at], {"section": f}).start()

    def start_output(i, src, dst):
        copies, own = output_copies(i, src, dst)
        for c in copies + [own]:
            c.start()

    def spread_heads(v):
        return jnp.concatenate([v] * HEADS, axis=0) * mask_ref[...]

    def gather_heads(v):
        return jnp.sum((v * mask_ref[...].astype(F32)).reshape(HEADS, READ, width), axis=0)

    def live_at(f):
        return jnp.where(f < len_ref[me], 1.0, 0.0).astype(F32)

    def keep_slices(lb, f, first, v):
        c = v.shape[1] // members
        for s in range(members):
            slice_b[lb // BLOCKS, s, f, lb % BLOCKS, :, first:first + c] = v[:, s * c:(s + 1) * c]

    def add_gain_grad(l, i, v):
        dsm_ref[l, READ + MEM + i:READ + MEM + i + 1, :] += jnp.sum(v, axis=0, keepdims=True)

    def gain(i):
        return gains[i:i + 1, :]

    def block_forward(lb, f, h):
        xh, r = normalize(h)
        xa[lb, f], ra[lb, f] = xh, r
        g = (xh * gain(2 + lb)).astype(BF)
        all_f[lb // BLOCKS, here[lb // BLOCKS], f, lb % BLOCKS, :, :width] = g
        l, b = lb // BLOCKS, lb % BLOCKS
        q, k, v = (nn(g, weight(wq, l, b, i)).astype(BF) for i in range(3))
        for i, part in enumerate((q, k, v)):
            qkv[lb, f, :, i * width:(i + 1) * width] = part
        s = nt(k, spread_heads(q)) * HEAD ** (-0.5)
        e = jnp.exp(s - jnp.max(s, axis=0, keepdims=True))
        p = e / jnp.sum(e, axis=0, keepdims=True)
        pt[lb, f] = p
        o = gather_heads(tn(p.astype(BF), v)).astype(BF)
        all_f[lb // BLOCKS, here[lb // BLOCKS], f, lb % BLOCKS, :, width:2 * width] = o
        h = h + nn(o, weight(wo, l, b))
        xh, r = normalize(h)
        xm[lb, f], rm[lb, f] = xh, r
        u = (xh * gain(6 + lb)).astype(BF)
        all_f[lb // BLOCKS, here[lb // BLOCKS], f, lb % BLOCKS, :, 2 * width:] = u
        x = nn(u, weight(wu, l, b))
        lift, slope = gelu_and_slope(x)
        lift, gp[lb, f] = lift.astype(BF), slope.astype(BF)
        return h + nn(lift, weight(wd, l, b))

    def block_backward(lb, f, dh):
        l, b = lb // BLOCKS, lb % BLOCKS
        dhb = dh.astype(BF)
        for s in range(members):
            slice_b[lb // BLOCKS, s, f, lb % BLOCKS, :, 4 * width // members:] = dhb
        dup = (nn(dhb, weight(wu, 1 - l, b)) * gp[lb, f].astype(F32)).astype(BF)
        du = nn(dup, weight(wd, 1 - l, b))
        xh = xm[lb, f]
        add_gain_grad(lb // BLOCKS, 3 + lb % BLOCKS, du * xh)
        dh = dh + normalize_back(du * gain(6 + lb), xh, rm[lb, f])
        dhb = dh.astype(BF)
        keep_slices(lb, f, 3 * width // members, dhb)
        do = spread_heads(nn(dhb, weight(wo, 1 - l, b)).astype(BF))
        joined = qkv[lb, f]
        q, k, v = joined[:, :width], joined[:, width:2 * width], joined[:, 2 * width:]
        p = pt[lb, f]
        dp = nt(v, do)
        ds = (p * (dp - jnp.sum(p * dp, axis=0, keepdims=True)) * HEAD ** (-0.5)).astype(BF)
        dv = nn(p.astype(BF), do)
        dk = nn(ds, spread_heads(q))
        dq = gather_heads(tn(ds, k))
        dj = [d.astype(BF) for d in (dq, dk, dv)]
        keep_slices(lb, f, 0, jnp.concatenate(dj, axis=1))
        dg = sum(nn(d, weight(wq, 1 - l, b, i)) for i, d in enumerate(dj))
        xh = xa[lb, f]
        add_gain_grad(lb // BLOCKS, 1 + lb % BLOCKS, dg * xh)
        return dh + normalize_back(dg * gain(2 + lb), xh, ra[lb, f])

    def layer_forward(l, f, z, xh_ref, rs_ref, at, bt, inputs):
        live = live_at(f)
        m = mem[...]
        rows = z.shape[1] - READ
        n_in = rows - MEM
        if inputs is not None:
            z[f, :n_in] = inputs
        z[f, n_in:rows] = m.astype(BF)
        zz = z[f, :rows]
        xh, r = normalize(zz.astype(F32))
        xh_ref[f, :rows], rs_ref[f, :rows] = xh, r
        n = (xh * gain(l)).astype(BF)
        a = softmax_lanes(nt(rw_ref[l], n))
        at[f] = a
        h = nn(a.astype(BF), zz)
        for b in range(BLOCKS):
            h = block_forward(l * BLOCKS + b, f, h)
        y = h.astype(BF)
        z[f, rows:] = y
        xh, r = normalize(y.astype(F32))
        xh_ref[f, rows:], rs_ref[f, rows:] = xh, r
        n = (xh_ref[f] * gain(10 + l)).astype(BF)
        b = softmax_lanes(nt(ww_ref[l], n))
        bt[f] = b
        written = nn(b.astype(BF), z[f])
        rate = dec_col[l]
        updated = rate * z[f, n_in:rows].astype(F32) + (1.0 - rate) * written
        mem[...] = live * updated + (1.0 - live) * m
        return (live * y.astype(F32)).astype(BF)

    def layer_backward(l, f, z, xh_ref, rs_ref, at, bt, dy_out, middle=None):
        live = live_at(f)
        rows = z.shape[1] - READ
        n_in = rows - MEM
        dm = dmem[...]
        rate = dec_col[l]
        dt = ((live * (1.0 - rate)) * dm).astype(BF)
        zf = z[f]
        b = bt[f]
        dl = softmax_lanes_back(b, nt(dt, zf)).astype(BF)
        dz = tn(b.astype(BF), dt)
        dn = tn(dl, ww_ref[l])
        xh = xh_ref[f]
        dsm_ref[l, READ:READ + MEM] += nn(dl, (xh * gain(10 + l)).astype(BF))
        add_gain_grad(l, 5, dn * xh)
        dx = dn * gain(10 + l)
        dy = dz[rows:] + normalize_back(dx[rows:], xh[rows:], rs_ref[f, rows:]) + live * dy_out
        dh = dy.astype(BF).astype(F32)
        for bb in range(BLOCKS - 1, -1, -1):
            dh = block_backward(l * BLOCKS + bb, f, dh)
            if bb and middle is not None:
                middle()
        ds = dh.astype(BF)
        xh = xh[:rows]
        a = at[f]
        dl = softmax_lanes_back(a, nt(ds, zf[:rows])).astype(BF)
        dz = dz[:rows] + tn(a.astype(BF), ds)
        dn = tn(dl, rw_ref[l])
        dsm_ref[l, :READ] += nn(dl, (xh * gain(l)).astype(BF))
        add_gain_grad(l, 0, dn * xh)
        dz = dz + normalize_back(dx[:rows] + dn * gain(l), xh, rs_ref[f, :rows])
        dmq = (dz[n_in:] + (live * rate) * dm).astype(BF).astype(F32)
        dmem[...] = dmq + (1.0 - live) * dm
        return dz[:n_in].astype(BF)

    for c in own_frames():
        c.start()
    for lb in range(lbs):
        for c in weight_copies(lb // BLOCKS, lb % BLOCKS):
            c.start()
    row = lax.broadcasted_iota(jnp.int32, (HEADS * READ, width), 0) // READ
    col = lax.broadcasted_iota(jnp.int32, (HEADS * READ, width), 1) // HEAD
    mask_ref[...] = jnp.where(row == col, 1.0, 0.0).astype(BF)
    dsm_ref[...] = jnp.zeros_like(dsm_ref)
    for l in range(LAYERS):
        gains[l:l + 1] = rg_ref[...].astype(F32)[l:l + 1]
        gains[10 + l:11 + l] = wg_ref[...].astype(F32)[l:l + 1]
        for b in range(BLOCKS):
            lb = l * BLOCKS + b
            gains[2 + lb:3 + lb] = na_ref[l].astype(F32)[b:b + 1]
            gains[6 + lb:7 + lb] = nm_ref[l].astype(F32)[b:b + 1]
        spread = jnp.broadcast_to(decay_ref[l:l + 1], (MEM, MEM))
        diagonal = lax.broadcasted_iota(jnp.int32, (MEM, MEM), 0) == lax.broadcasted_iota(jnp.int32, (MEM, MEM), 1)
        dec_col[l] = jnp.sum(jnp.where(diagonal, spread, 0.0), axis=1, keepdims=True)

    pl.semaphore_wait(barrier, len(partners))
    for c in frame_copies():
        c.start()

    kept0 = (z0, xh0, rs0, at0, bt0)
    kept1 = (z1, xh1, rs1, at1, bt1)

    lax.fori_loop(0, lbs, transpose_block, 0)
    for c in own_frames():
        c.wait()
    for c in frame_copies():
        c.wait_recv()
    mem[...] = jnp.zeros_like(mem)

    def forward0(f, carry):
        dout[f] = layer_forward(0, f, *kept0, None)
        start_forward(0, f)
        return carry

    lax.fori_loop(0, frames, forward0, 0)
    for c in transposed_copies(1):
        c.start()
    mem[...] = jnp.zeros_like(mem)

    def forward1(f, carry):
        res_v[f] = layer_forward(1, f, *kept1, dout[f])
        start_forward(1, f)
        return carry

    lax.fori_loop(0, frames, forward1, 0)
    for c in transposed_copies(0):
        c.start()
    for c in transposed_copies(1):
        c.wait()
    start_output(*results)
    dmem[...] = jnp.zeros_like(dmem)

    def backward1(i, carry):
        f = frames - 1 - i
        dout[f] = layer_backward(1, f, *kept1, cot_v[f].astype(F32))
        start_backward(1, f)
        return carry

    lax.fori_loop(0, frames, backward1, 0)
    for c in transposed_copies(0):
        c.wait()
    start_small(1)
    dmem[...] = jnp.zeros_like(dmem)

    def backward0(i, carry):
        f = frames - 1 - i

        def middle():
            @pl.when(i == 1)
            def _():
                halve(2, 0, 0)
                halve(2, 0, 1)

        z0[f, tokens0] = layer_backward(0, f, *kept0, dout[f].astype(F32), middle)
        start_backward(0, f)
        start_frame_grad(f)

        @pl.when(i == 0)
        def _():
            wait_factors(1)
            form(3)
            form(2)
            halve(3, 0, 0)
            halve(3, 0, 1)

        @pl.when(i == 2)
        def _():
            halve(3, 1, 0)
            halve(3, 1, 1)

        return carry

    lax.fori_loop(0, frames, backward0, 0)
    start_small(0)
    halve(2, 1, 0)
    halve(2, 1, 1)
    wait_factors(0)
    form(1)
    form(0)
    halve(1, 0, 0)
    halve(1, 0, 1)
    halve(3, 2, 0)
    halve(3, 2, 1)
    halve(1, 1, 0)
    halve(0, 0, 0)
    halve(1, 1, 1)
    halve(0, 0, 1)
    halve(2, 2, 0)
    halve(2, 2, 1)
    halve(0, 1, 0)
    halve(0, 1, 1)
    halve(1, 2, 0)
    halve(1, 2, 1)
    halve(0, 2, 0)
    halve(0, 2, 1)
    for u in range(lbs - 1, -1, -1):
        finish(u)
    for out in (results, frame_grads):
        copies, own = output_copies(*out)
        for c in copies + [own]:
            c.wait()
    for c in frame_copies():
        c.wait_send()


def run_fused(sections, hi, lo, lengths, decay, gains, small, frames, cot, weights):
    count, _, tok, width = frames.shape
    lbs = LAYERS * BLOCKS
    ff = weights[2].shape[-1]
    cols = (4 * width + ff) // sections
    all_cols = cols + width
    bits = hi.bit_length() - 1
    chunk = sections * TILE
    peers = sections - 1
    vm, anym = pl.BlockSpec(memory_space=pltpu.VMEM), pl.BlockSpec(memory_space=pl.ANY)
    v, dma = pltpu.VMEM, pltpu.SemaphoreType.DMA

    def sds(shape, dtype):
        return jax.ShapeDtypeStruct(shape, dtype)

    def per(c, dtype):
        return v((lbs, count, READ, c), dtype)

    def by_section(c):
        return v((LAYERS, sections, count, BLOCKS, READ, c), BF)

    rows0, rows1 = tok + MEM, READ + MEM
    lead, block = (LAYERS, BLOCKS), (2,) * bits + (width // hi,)
    transposed = [lead + (3,) + block + (width,), lead + block + (width,), lead + block + (ff,), lead + (ff // width,) + block + (width,)]
    weights = [weights[0].reshape(lead + block + (3 * width,))] + [w.reshape(s) for w, s in zip(weights[1:], transposed[1:])]
    scratch = [v(s, BF) for s in transposed]
    scratch += [v((count, READ, width), BF), v((count, READ, width), BF)]
    scratch += [v((count, r + READ, width), BF) for r in (rows0, rows1)]
    scratch += [v((count, r + READ, width), F32) for r in (rows0, rows1)]
    scratch += [v((count, r + READ, 1), F32) for r in (rows0, rows1)]
    scratch += [v((count, READ, r), F32) for r in (rows0, rows1)]
    scratch += [v((count, MEM, r + READ), F32) for r in (rows0, rows1)]
    scratch += [v((MEM, width), F32), v((MEM, width), F32), v((count, READ, width), BF)]
    scratch += [per(width, F32), per(1, F32), per(width, F32), per(1, F32)]
    scratch += [per(ff, BF), per(3 * width, BF), per(HEADS * READ, F32)]
    scratch += [v((HEADS * READ, width), BF), v((12, width), F32), v((LAYERS, MEM, 1), F32)]
    scratch += [v((LAYERS, SMALL, width), F32)]
    sliced = 4 * width // sections + width
    scratch += [by_section(sliced), by_section(3 * width), by_section(sliced)]
    scratch += [v((lbs,) + (2,) * bits + (chunk, all_cols), BF)]
    scratch += [[v((lbs,) + (2,) * (bits - 1 - k) + (chunk, all_cols), BF) for k in range(bits)]]
    scratch += [v((LAYERS, sections) + (2,) * bits + (TILE, SMALL), F32)] * 2
    scratch += [v((LAYERS,) + (2,) * bits + (TILE, SMALL), F32)]
    scratch += [[v((LAYERS,) + (2,) * (bits - 1 - k) + (TILE, SMALL), F32) for k in range(bits)]]
    scratch += [dma((LAYERS, BLOCKS, 6)), dma((LAYERS, BLOCKS, 4)), dma((12,))]
    scratch += [dma((peers, 2)), dma((peers, 2)), dma((2,)), dma((peers, 2)), dma((peers, 2)), dma((2,))]
    scratch += [dma((LAYERS, peers, 2)), dma((LAYERS, peers, 2)), dma((LAYERS,)), dma((lbs, bits, PIECES)), dma((lbs, bits, PIECES))]
    scratch += [dma((LAYERS, peers)), dma((LAYERS, peers)), dma((LAYERS, bits)), dma((LAYERS, bits))]
    scratch += [dma((lbs, peers)), dma((lbs, peers)), dma((lbs, 2))]
    return pl.pallas_call(
        functools.partial(fused_kernel, hi, lo),
        out_shape=[
            sds((count, READ, width), BF),
            sds((count, tok, width), BF),
            sds((lbs, sections, TILE, cols), BF),
            sds((lbs, chunk, width), BF),
            sds((LAYERS, TILE, SMALL), F32),
        ]
        + [sds(s, BF) for s in transposed],
        in_specs=[pl.BlockSpec(memory_space=pltpu.SMEM)] + [vm] * 7 + [anym] * 6,
        out_specs=[vm] * 5 + [anym] * 4,
        scratch_shapes=[scratch],
        compiler_params=pltpu.CompilerParams(
            collective_id=0, has_side_effects=True, vmem_limit_bytes=64 * 2**20 - 2**16
        ),
    )(lengths, decay, *gains, *small, frames, cot, *weights)[:5]


def widen_kernel(
    rows_ref, down_ref, small_ref, res_ref, fgrad_ref,
    res_out, fgrad_out, rg_out, rw_out, na_out, qkv_out, out_out, nm_out, up_out, down_out, wg_out, ww_out,
):
    sections, tile = rows_ref.shape[1:3]
    lbs = LAYERS * BLOCKS
    res_out[...] = res_ref[...]
    fgrad_out[...] = fgrad_ref[...]
    cols = [ref.shape[-1] // sections for ref in (qkv_out, out_out, up_out)]
    for u in range(lbs):
        l, b = u // BLOCKS, u % BLOCKS
        runs = 1 << len(free_bits(l))
        run = cols[2] // runs
        for s in range(sections):
            first = 0
            for ref, c in zip((qkv_out, out_out), cols):
                ref[l, b, :, s * c:(s + 1) * c] = rows_ref[u, s, :, first:first + c].astype(F32)
                first += c
            for j in range(runs):
                start = run_start(run, l, j, {bit: (s >> i) & 1 for i, bit in enumerate(GROUP[l])})
                up_out[l, b, :, start:start + run] = rows_ref[u, s, :, first + j * run:first + (j + 1) * run].astype(F32)
        down_out[l, b] = down_ref[u].astype(F32)
    diagonal = lax.broadcasted_iota(jnp.int32, (tile, tile), 0) == lax.broadcasted_iota(jnp.int32, (tile, tile), 1)

    def as_row(l, i):
        column = jnp.broadcast_to(small_ref[l][:, READ + MEM + i:READ + MEM + i + 1], (tile, tile))
        return jnp.sum(jnp.where(diagonal, column, 0.0), axis=0, keepdims=True)

    for l in range(LAYERS):
        rw_out[l] = small_ref[l][:, :READ]
        ww_out[l] = small_ref[l][:, READ:READ + MEM]
        rg_out[l:l + 1] = as_row(l, 0)
        wg_out[l:l + 1] = as_row(l, 1 + 2 * BLOCKS)
        for b in range(BLOCKS):
            na_out[l, b:b + 1] = as_row(l, 1 + b)
            nm_out[l, b:b + 1] = as_row(l, 1 + BLOCKS + b)


def widen(rows, down, sm, res, fgrad):
    sections, tile, cols = rows.shape[1:]
    width = down.shape[-1]
    vm = pl.BlockSpec(memory_space=pltpu.VMEM)

    def f32(*shape):
        return jax.ShapeDtypeStruct((LAYERS,) + shape, F32)

    out_shape = [jax.ShapeDtypeStruct(a.shape, a.dtype) for a in (res, fgrad)] + [
        f32(tile), f32(tile, READ), f32(BLOCKS, tile), f32(BLOCKS, tile, 3 * width), f32(BLOCKS, tile, width),
        f32(BLOCKS, tile), f32(BLOCKS, tile, sections * cols - 4 * width), f32(BLOCKS, *down.shape[1:]),
        f32(tile), f32(tile, MEM),
    ]
    return pl.pallas_call(
        widen_kernel, out_shape=out_shape, in_specs=[vm] * 5, out_specs=[vm] * len(out_shape)
    )(rows, down, sm, res, fgrad)


def local(
    frames, lengths, decay, read_gain, read_weight, norm_attn, w_qkv, w_out, norm_mlp, w_up, w_down,
    write_gain, write_weight, cotangent,
):
    sections, dp = lax.axis_size("section"), lax.axis_size("dp")
    clip_dev, span, tok, width = frames.shape
    hi = width // (sections * TILE)
    lo = dp // hi
    assert clip_dev == sections and span == 1 and hi * lo == dp
    res, fgrad, rows, down, sm = run_fused(
        sections, hi, lo, lengths, decay, (read_gain, norm_attn, norm_mlp, write_gain),
        [jnp.swapaxes(w, 1, 2) for w in (read_weight, write_weight)], frames, cotangent, (w_qkv, w_out, w_up, w_down),
    )
    if lo > 1:
        groups = [[h * lo + k for k in range(lo)] for h in range(hi)]

        def over_rest(v, axis):
            return lax.psum_scatter(
                v.astype(F32), "dp", scatter_dimension=axis, axis_index_groups=groups, tiled=True
            )

        rows, down, sm = over_rest(rows, 2), over_rest(down, 1), over_rest(sm, 1)
    res, fgrad, *grads = widen(rows, down, sm, res, fgrad)
    return (res[:, None], fgrad[:, None], *grads)


def solution(mesh):
    both = ("section", "dp")
    split = P("dp", "section", None, None)
    return jax.shard_map(
        local,
        mesh=mesh,
        in_specs=(split, P("dp")) + (P(),) * 11 + (split,),
        out_specs=(
            split, split, P(None, both), P(None, both, None), P(None, None, both), P(None, None, both, None),
            P(None, None, both, None), P(None, None, both), P(None, None, both, None),
            P(None, None, both, None), P(None, both), P(None, both, None),
        ),
        check_vma=False,
    )
```

```python
import functools

import jax
import jax.numpy as jnp
from jax import lax
from jax.experimental import pallas as pl
from jax.experimental.pallas import tpu as pltpu
from jax.sharding import PartitionSpec as P

HEADS = 8
HEAD = 64
MEM = 96
READ = 16
BLOCKS = 2
LAYERS = 2
EPS = 1e-05
SMALL = 128
TILE = 16
PIECES = 2
S0, S1, D0, D1, D2 = ("section", 0), ("section", 1), ("dp", 0), ("dp", 1), ("dp", 2)
ROW_BITS = (S1, S0, D2, D1, D0)
GROUP = ((S0, D1), (S1, D2)) * LAYERS
SUM = ((D0, S1, D2), (D0, S0, D1)) * LAYERS


def free_bits(u):
    return tuple(b for b in ROW_BITS if b not in GROUP[u] and b != D0)


def run_start(bit, u, j, fixed):
    free = free_bits(u)
    value = {b: (j >> (len(free) - 1 - i)) & 1 for i, b in enumerate(free)} | fixed
    return sum(value[b] * (bit << (len(ROW_BITS) - 2 - i)) for i, b in enumerate(ROW_BITS[:-1]))
BF = jnp.bfloat16
F32 = jnp.float32


def nn(a, b):
    return lax.dot_general(a, b, (((1,), (0,)), ((), ())), preferred_element_type=F32)


def nt(a, b):
    return lax.dot_general(a, b, (((1,), (1,)), ((), ())), preferred_element_type=F32)


def tn(a, b):
    return lax.dot_general(a, b, (((0,), (0,)), ((), ())), preferred_element_type=F32)


def normalize(v):
    centred = v - jnp.mean(v, axis=-1, keepdims=True)
    spread = jnp.mean(centred * centred, axis=-1, keepdims=True)
    r = lax.rsqrt(spread + EPS)
    return centred * r, r


def centre(v):
    centred = v - jnp.mean(v, axis=-1, keepdims=True)
    return centred, lax.rsqrt(jnp.mean(centred * centred, axis=-1, keepdims=True) + EPS)


def normalize_back(dx, xh, r):
    return r * (dx - jnp.mean(dx, axis=-1, keepdims=True) - xh * jnp.mean(dx * xh, axis=-1, keepdims=True))


def gelu_and_slope(x):
    c0, c1 = 0.7978845608028654, 0.044715
    x2 = x * x
    t = jnp.tanh(c0 * x * (1.0 + c1 * x2))
    return 0.5 * x * (1.0 + t), 0.5 * (1.0 + t) + 0.5 * x * (1.0 - t * t) * c0 * (1.0 + 3.0 * c1 * x2)


def softmax_lanes(v):
    e = jnp.exp(v - jnp.max(v, axis=1, keepdims=True))
    return e / jnp.sum(e, axis=1, keepdims=True)


def softmax_lanes_back(p, dp):
    return p * (dp - jnp.sum(p * dp, axis=1, keepdims=True))


def fused_kernel(
    hi, lo, len_ref, decay_ref, rg_ref, na_ref, nm_ref, wg_ref, rw_ref, ww_ref, frames_hbm, cot_hbm,
    wqkv_hbm, wout_hbm, wup_hbm, wdown_hbm, res_out, fgrad_out, rows_ref, down_ref, small_ref,
    turn_hbm, scratch,
):
    (
        wq, wo, wu, wd, cot_v, res_v, z0, z1, xh0, xh1, rs0, rs1, at0, at1, bt0, bt1,
        mem0, mem1, dmem, dt_kept, ds_kept, dlw_kept, dlr_kept, dout, xa, ra, xm, rm, gp, qkv, pt, mask_ref, gains, dec_col, dsm_ref,
        slice_b, all_f, part_b, wgrad, into, small_t, small_in, small_sum, small_into,
        w_sem, x_sem, v_sem, t_sem, f_send, f_recv, f_own, o_send, o_recv, o_own,
        a_send, a_recv, a_own, c_send, c_recv, s_send, s_recv, t_send, t_recv, d_send, d_recv, d_own,
    ) = scratch
    sections, frames = all_f.shape[1:3]
    tokens0 = pl.ds(0, frames_hbm.shape[2])
    width = dsm_ref.shape[-1]
    lbs = LAYERS * BLOCKS
    me, dp_at = lax.axis_index("section"), lax.axis_index("dp")
    bits = hi.bit_length() - 1
    peers = [(me + k) % sections for k in range(1, sections)]
    members = 1 << len(GROUP[0])
    own = {S0: me % 2, S1: (me // 2) % 2} | {("dp", k): (dp_at // (lo << k)) % 2 for k in range(bits)}
    assert sections == 4 and bits == 3

    def device(flips):
        s, d = me, dp_at
        for axis, k in flips:
            step = 1 - 2 * own[axis, k]
            s, d = (s + step * (1 << k), d) if axis == "section" else (s, d + step * (lo << k))
        return {"section": s, "dp": d}

    def flips_of(u, x):
        return tuple(b for j, b in enumerate(GROUP[u]) if (x >> j) & 1)

    def member(u, x):
        return sum((1 - own[b] if (x >> j) & 1 else own[b]) * (1 << j) for j, b in enumerate(GROUP[u]))

    here = [member(u, 0) for u in range(lbs)]

    every = (slice(None),) * (bits + 1)
    ups = wd.shape[2]

    def columns(i):
        return every + (pl.ds(i * width, width),)

    def weight_copies(l, b, to, sem):
        pairs = [(wqkv_hbm.at[(l, b) + columns(i)], wq.at[to, b, i]) for i in range(3)]
        pairs += [(wout_hbm.at[l, b], wo.at[to, b]), (wup_hbm.at[l, b], wu.at[to, b]), (wdown_hbm.at[l, b], wd.at[to, b])]
        return [pltpu.make_async_copy(s, d, sem.at[l, b, i]) for i, (s, d) in enumerate(pairs)]

    def squares(l, b):
        out = [(wq.at[l, b, i],) * 2 for i in range(3)] + [(wo.at[l, b],) * 2]
        for i in range(ups):
            pair = (wu.at[(l, b) + columns(i)], wd.at[l, b, i])
            out += [pair, pair[::-1]]
        return out

    def staged(i):
        return wgrad.at[(i // 3,) + columns(i % 3)]

    def turned(ref):
        return ref[...].reshape(width, width).T.reshape(ref.shape)

    def kept_copies():
        return [pltpu.make_async_copy(staged(i), turn_hbm.at[i], t_sem.at[i]) for i in range(4 + 2 * ups)]

    def transpose_block(b, carry):
        copies = kept_copies()
        for i, (s, _) in enumerate(squares(1, b)):
            pl.when(b > 0)(copies[i].wait)
            staged(i)[...] = turned(s)
            pl.when(b == 0)(copies[i].start)
        return carry

    def transposed_copies():
        out = []
        for b in range(BLOCKS):
            for i, (_, d) in enumerate(squares(0, b)):
                out.append(pltpu.make_async_copy(turn_hbm.at[i] if b == 0 else staged(i), d, v_sem.at[b, i]))
        return out

    def transpose_here(b, carry):
        for i, (s, d) in enumerate(squares(1, b)):
            if i < 4:
                d[...] = turned(s)
            elif i % 2 == 0:
                first, second = turned(s), turned(d)
                d[...], s[...] = first, second
        return carry

    def weight(ref, *at):
        w = ref[at]
        return w.reshape(-1, w.shape[-1])

    barrier = pltpu.get_barrier_semaphore()
    partners = {(S0,), (S1,), (S0, S1)} | {(b,) for bits_of in SUM for b in bits_of}
    partners |= {tuple(sorted(flips_of(u, x))) for u in range(lbs) for x in range(1, members)}
    partners = sorted({tuple(sorted(p)) for p in partners})
    for p in partners:
        pl.semaphore_signal(barrier, inc=1, device_id=device(p), device_id_type=pl.DeviceIdType.MESH)

    def remote(src, dst, send, recv, to):
        return pltpu.make_async_remote_copy(
            src_ref=src, dst_ref=dst, send_sem=send, recv_sem=recv, device_id=to, device_id_type=pl.DeviceIdType.MESH
        )

    def forward_copies(u, first, count):
        at = all_f.at[u, here[u], pl.ds(first, count)]
        return [
            remote(at, at, a_send.at[u, x - 1, 0], a_recv.at[u, x - 1, 0], device(flips_of(u, x)))
            for x in range(1, members)
        ]

    def backward_copies(u, first, count):
        at = pl.ds(first, count)
        return [
            remote(
                slice_b.at[u, member(u, x), at], part_b.at[u, here[u], at],
                a_send.at[u, x - 1, 1], a_recv.at[u, x - 1, 1], device(flips_of(u, x)),
            )
            for x in range(1, members)
        ]

    def own_backward(u, first, count):
        at = pl.ds(first, count)
        return pltpu.make_async_copy(slice_b.at[u, here[u], at], part_b.at[u, here[u], at], a_own.at[u])

    def start_forward(u, f):
        for c in forward_copies(u, f, 1):
            c.start()

    def start_backward(u, f):
        for c in backward_copies(u, f, 1) + [own_backward(u, f, 1)]:
            c.start()

    def wait_factors(u):
        own_backward(u, 0, frames).wait()
        for c in forward_copies(u, 0, frames) + backward_copies(u, 0, frames):
            c.wait_recv()

    def place(u, s, h):
        value = {("section", k): (s >> k) & 1 for k in range(2)} | {("dp", k): (h >> k) & 1 for k in range(bits)}
        return tuple(value[b] for b in reversed(SUM[u])), sum(value[b] << j for j, b in enumerate(GROUP[u]))

    def start_small(l):
        rows = jnp.transpose(dsm_ref[l]).reshape(sections, hi, TILE, SMALL)
        for s in range(sections):
            for h in range(hi):
                at, g = place(l * BLOCKS, s, h)
                small_t[(l, g) + at] = rows[s, h]
        for c in small_copies(l):
            c.start()

    def small_copies(l):
        u = l * BLOCKS
        return [
            remote(
                small_t.at[l, member(u, x)], small_in.at[l, here[u]],
                s_send.at[l, x - 1], s_recv.at[l, x - 1], device(flips_of(u, x)),
            )
            for x in range(1, members)
        ]

    def halves(u, k, other):
        b = own[SUM[u][k]]
        fixed = tuple(own[SUM[u][j]] for j in range(k - 1, -1, -1))
        return (slice(None),) * (bits - 1 - k) + ((1 - b) if other else b,) + fixed

    def own_at(u):
        return tuple(own[b] for b in reversed(SUM[u]))

    def piece(p):
        size = wgrad.shape[-1] // PIECES
        return (slice(None), pl.ds(p * size, size))

    def halving_copy(u, k, p):
        return remote(
            wgrad.at[(u,) + halves(u, k, True) + piece(p)],
            into[k].at[(u,) + (slice(None),) * (bits - 1 - k) + piece(p)],
            c_send.at[u, k, p], c_recv.at[u, k, p], device((SUM[u][k],)),
        )

    def small_halving_copy(l, k):
        u = l * BLOCKS
        return remote(
            small_sum.at[(l,) + halves(u, k, True)], small_into[k].at[l], t_send.at[l, k], t_recv.at[l, k],
            device((SUM[u][k],)),
        )

    cols = wgrad.shape[-1] - width

    def final_columns(p):
        size = wgrad.shape[-1] // PIECES
        return pl.ds(p * size, min(size, cols - p * size))

    def own_rows(u, g, p):
        return wgrad.at[(u,) + own_at(u) + (pl.ds(pl.multiple_of(g * TILE, TILE), TILE), final_columns(p))]

    def row_copies(u, p):
        dst = rows_ref.at[u, here[u], :, final_columns(p)]
        return [
            remote(
                own_rows(u, member(u, x), p), dst, d_send.at[u, p, x - 1], d_recv.at[u, p, x - 1], device(flips_of(u, x))
            )
            for x in range(1, members)
        ] + [pltpu.make_async_copy(own_rows(u, here[u], p), dst, d_own.at[u, p])]

    def down_copy(u):
        down = wgrad.at[(u,) + own_at(u) + (slice(None), pl.ds(cols, width))]
        return pltpu.make_async_copy(down, down_ref.at[u], d_own.at[u, PIECES])

    def store_rows(u, first, v):
        c = v.shape[1]
        v = v.astype(BF).reshape(sections, hi, TILE, c)
        for s in range(sections):
            for h in range(hi):
                at, g = place(u, s, h)
                wgrad[(u,) + at + (slice(g * TILE, (g + 1) * TILE), slice(first, first + c))] = v[s, h]

    def store_down(u, first, v):
        c = v.shape[1]
        order = free_bits(u) + (D0,)
        v = v.astype(BF).reshape(1 << len(order), members * TILE, c)
        for j in range(1 << len(order)):
            value = {b: (j >> (len(order) - 1 - i)) & 1 for i, b in enumerate(order)}
            at = tuple(value[b] for b in reversed(SUM[u]))
            wgrad[(u,) + at + (slice(None), slice(first, first + c))] = v[j]

    def form(u):
        l, b = u // BLOCKS, u % BLOCKS
        q, o = 3 * width // members, 4 * width // members
        runs = 1 << len(free_bits(u))
        run = wu.shape[-1] // (members * runs)
        fixed = {bit: own[bit] for bit in GROUP[u]}

        def flat(ref, first, count):
            v = ref[u, :, :, :, first:first + count]
            return v.reshape(members * frames * READ, count)

        def up_run(j):
            at = {bit: (j >> (len(free_bits(u)) - 1 - i)) & 1 for i, bit in enumerate(free_bits(u))} | fixed
            w = wd[1 - l, b, 2 * at[S1] + at[S0], at[D2], at[D1]]
            return w.reshape(-1, w.shape[-1])

        def down_run(j):
            start = pl.multiple_of(run_start(run, u, j, fixed), run)
            return weight(wu, 1 - l, b, *every, pl.ds(start, run))

        u_all, dh_all = flat(all_f, 2 * width, width), flat(part_b, o, width)
        up_rows = jnp.concatenate([up_run(j) for j in range(runs)], axis=0)
        down_cols = jnp.concatenate([down_run(j) for j in range(runs)], axis=1)
        lift, slope = gelu_and_slope(nt(u_all, up_rows))
        dup = (nn(dh_all, down_cols) * slope).astype(BF)
        store_rows(u, 0, tn(flat(all_f, 0, width), flat(part_b, 0, q)))
        store_rows(u, q, tn(flat(all_f, width, width), flat(part_b, q, o - q)))
        store_rows(u, o, tn(u_all, dup))
        store_down(u, cols, tn(lift.astype(BF), dh_all))
        for p in range(PIECES):
            halving_copy(u, 0, p).start()

    def halve_small(l, k):
        if k < 0:
            for c in small_copies(l):
                c.wait_recv()
            total = small_t[l, here[l * BLOCKS]]
            for x in range(1, members):
                total = total + small_in[l, member(l * BLOCKS, x)]
            small_sum[l] = total
        else:
            small_halving_copy(l, k).wait_recv()
            at = (l,) + halves(l * BLOCKS, k, False)
            small_sum[at] = small_sum[at] + small_into[k][l]
        if k + 1 < bits:
            small_halving_copy(l, k + 1).start()
        else:
            small_ref[l] = small_sum[(l,) + own_at(l * BLOCKS)]

    def halve(u, k, p):
        halving_copy(u, k, p).wait_recv()
        at = (u,) + halves(u, k, False) + piece(p)
        wgrad[at] = wgrad[at] + into[k][(u,) + (slice(None),) * (bits - 1 - k) + piece(p)]
        if k + 1 < bits:
            halving_copy(u, k + 1, p).start()
        else:
            for c in row_copies(u, p):
                c.start()
            if p + 1 == PIECES:
                down_copy(u).start()
        if u == BLOCKS and p == 0:
            halve_small(1, k)

    def finish(u):
        for p in range(PIECES):
            for c in row_copies(u, p):
                c.wait()
        down_copy(u).wait()
        for k in range(bits):
            for p in range(PIECES):
                halving_copy(u, k, p).wait_send()
        for c in forward_copies(u, 0, frames) + backward_copies(u, 0, frames):
            c.wait_send()
        if u % BLOCKS == 0:
            l = u // BLOCKS
            for c in small_copies(l):
                c.wait_send()
            for k in range(bits):
                small_halving_copy(l, k).wait_send()

    def frame_copies():
        return [
            remote(src.at[p, 0], dst, f_send.at[k, i], f_recv.at[k, i], {"section": p})
            for k, p in enumerate(peers)
            for i, (src, dst) in enumerate(((frames_hbm, z0.at[me, tokens0]), (cot_hbm, cot_v.at[me])))
        ]

    def own_frames():
        return [
            pltpu.make_async_copy(src.at[me, 0], dst, f_own.at[i])
            for i, (src, dst) in enumerate(((frames_hbm, z0.at[me, tokens0]), (cot_hbm, cot_v.at[me])))
        ]

    def output_copies(i, src, dst):
        copies = [
            remote(src(p), dst.at[me], o_send.at[k, i], o_recv.at[k, i], {"section": p}) for k, p in enumerate(peers)
        ]
        return copies, pltpu.make_async_copy(src(me), dst.at[me], o_own.at[i])

    results = (0, lambda f: res_v.at[f], res_out)
    frame_grads = (1, lambda f: z0.at[f, tokens0], fgrad_out)

    def start_output(i, src, dst):
        copies, own = output_copies(i, src, dst)
        for c in copies + [own]:
            c.start()

    def spread_heads(v):
        return jnp.concatenate([v] * HEADS, axis=0) * mask_ref[...]

    def gather_heads(v):
        return jnp.sum((v * mask_ref[...].astype(F32)).reshape(HEADS, READ, width), axis=0)

    def live_at(f):
        return jnp.where(f < len_ref[me], 1.0, 0.0).astype(F32)

    def keep_slices(lb, f, first, v):
        c = v.shape[1] // members
        for s in range(members):
            slice_b[lb, s, f, :, first:first + c] = v[:, s * c:(s + 1) * c]

    def add_gain_grad(l, i, v):
        dsm_ref[l, READ + MEM + i:READ + MEM + i + 1, :] += jnp.sum(v, axis=0, keepdims=True)

    def gain(i):
        return gains[i:i + 1, :]

    def block_forward(lb, f, h):
        centred, r = centre(h)
        xh = centred * r
        xa[lb, f], ra[lb, f] = xh, r
        g = (xh * gain(2 + lb)).astype(BF)
        wide = (centred * gain(2 + lb)).astype(BF)
        all_f[lb, here[lb], f, :, :width] = g
        l, b = lb // BLOCKS, lb % BLOCKS
        q, k, v = ((nn(wide, weight(wq, l, b, i)) * r).astype(BF) for i in range(3))
        yield
        for i, part in enumerate((q, k, v)):
            qkv[lb, f, :, i * width:(i + 1) * width] = part
        s = nt(k, spread_heads(q)) * HEAD ** (-0.5)
        yield
        e = jnp.exp(s - jnp.max(s, axis=0, keepdims=True))
        p = e / jnp.sum(e, axis=0, keepdims=True)
        pt[lb, f] = p
        o = tn(p.astype(BF), v)
        yield
        o = gather_heads(o).astype(BF)
        all_f[lb, here[lb], f, :, width:2 * width] = o
        h = h + nn(o, weight(wo, l, b))
        yield
        centred, r = centre(h)
        xh = centred * r
        xm[lb, f], rm[lb, f] = xh, r
        u = (xh * gain(6 + lb)).astype(BF)
        wide = (centred * gain(6 + lb)).astype(BF)
        all_f[lb, here[lb], f, :, 2 * width:] = u
        x = nn(wide, weight(wu, l, b)) * r
        yield
        lift, slope = gelu_and_slope(x)
        lift, gp[lb, f] = lift.astype(BF), slope.astype(BF)
        h = h + nn(lift, weight(wd, l, b))
        yield
        return h

    def block_backward(lb, f, dh):
        l, b = lb // BLOCKS, lb % BLOCKS
        dhb = dh.astype(BF)
        for s in range(members):
            slice_b[lb, s, f, :, 4 * width // members:] = dhb
        dup = (nn(dhb, weight(wu, 1 - l, b)) * gp[lb, f].astype(F32)).astype(BF)
        du = nn(dup, weight(wd, 1 - l, b))
        xh = xm[lb, f]
        add_gain_grad(lb // BLOCKS, 3 + lb % BLOCKS, du * xh)
        dh = dh + normalize_back(du * gain(6 + lb), xh, rm[lb, f])
        dhb = dh.astype(BF)
        keep_slices(lb, f, 3 * width // members, dhb)
        do = spread_heads(nn(dhb, weight(wo, 1 - l, b)).astype(BF))
        joined = qkv[lb, f]
        q, k, v = joined[:, :width], joined[:, width:2 * width], joined[:, 2 * width:]
        p = pt[lb, f]
        dp = nt(v, do)
        ds = (p * (dp - jnp.sum(p * dp, axis=0, keepdims=True)) * HEAD ** (-0.5)).astype(BF)
        dv = nn(p.astype(BF), do)
        dk = nn(ds, spread_heads(q))
        dq = gather_heads(tn(ds, k))
        dj = [d.astype(BF) for d in (dq, dk, dv)]
        keep_slices(lb, f, 0, jnp.concatenate(dj, axis=1))
        dg = sum(nn(d, weight(wq, 1 - l, b, i)) for i, d in enumerate(dj))
        xh = xa[lb, f]
        add_gain_grad(lb // BLOCKS, 1 + lb % BLOCKS, dg * xh)
        return dh + normalize_back(dg * gain(2 + lb), xh, ra[lb, f])

    def layer_forward(l, f, z, xh_ref, rs_ref, at, bt, mem, read_inputs, store):
        live = live_at(f)
        inputs = read_inputs(f)
        m = mem[...]
        rows = z.shape[1] - READ
        n_in = rows - MEM
        if inputs is not None:
            z[f, :n_in] = inputs
        z[f, n_in:rows] = m.astype(BF)
        zz = z[f, :rows]
        xh, r = normalize(zz.astype(F32))
        xh_ref[f, :rows], rs_ref[f, :rows] = xh, r
        n = (xh * gain(l)).astype(BF)
        logits = nt(rw_ref[l], n)
        yield
        a = softmax_lanes(logits)
        at[f] = a
        h = nn(a.astype(BF), zz)
        yield
        for b in range(BLOCKS):
            h = yield from block_forward(l * BLOCKS + b, f, h)
        y = h.astype(BF)
        z[f, rows:] = y
        xh, r = normalize(y.astype(F32))
        xh_ref[f, rows:], rs_ref[f, rows:] = xh, r
        n = (xh_ref[f] * gain(10 + l)).astype(BF)
        logits = nt(ww_ref[l], n)
        yield
        b = softmax_lanes(logits)
        bt[f] = b
        written = nn(b.astype(BF), z[f])
        yield
        rate = dec_col[l]
        updated = rate * z[f, n_in:rows].astype(F32) + (1.0 - rate) * written
        mem[...] = live * updated + (1.0 - live) * m
        store(f, (live * y.astype(F32)).astype(BF))

    def layer_backward(l, f, z, xh_ref, rs_ref, at, bt, dy_out, middle=None):
        live = live_at(f)
        rows = z.shape[1] - READ
        n_in = rows - MEM
        later = n_in if l == 0 else 0
        dm = dmem[...]
        rate = dec_col[l]
        dt = ((live * (1.0 - rate)) * dm).astype(BF)
        zf = z[f]
        b = bt[f]
        dl = softmax_lanes_back(b, nt(dt, zf)).astype(BF)
        dz = tn(b[:, later:].astype(BF), dt)
        dn = tn(dl[:, later:], ww_ref[l])
        xh = xh_ref[f, later:]
        if l == 0:
            dt_kept[f], dlw_kept[f] = dt, dl
        else:
            dsm_ref[l, READ:READ + MEM] += nn(dl, (xh * gain(10 + l)).astype(BF))
        add_gain_grad(l, 5, dn * xh)
        dx = dn * gain(10 + l)
        tail = rows - later
        dy = dz[tail:] + normalize_back(dx[tail:], xh[tail:], rs_ref[f, rows:]) + live * dy_out
        dh = dy.astype(BF).astype(F32)
        for bb in range(BLOCKS - 1, -1, -1):
            dh = block_backward(l * BLOCKS + bb, f, dh)
            start_backward(l * BLOCKS + bb, f)
            if bb and middle is not None:
                middle()
        ds = dh.astype(BF)
        xh = xh[:tail]
        a = at[f]
        dl = softmax_lanes_back(a, nt(ds, zf[:rows])).astype(BF)
        dz = dz[:tail] + tn(a[:, later:].astype(BF), ds)
        dn = tn(dl[:, later:], rw_ref[l])
        if l == 0:
            ds_kept[f], dlr_kept[f] = ds, dl
        else:
            dsm_ref[l, :READ] += nn(dl, (xh * gain(l)).astype(BF))
        add_gain_grad(l, 0, dn * xh)
        dz = dz + normalize_back(dx[:tail] + dn * gain(l), xh, rs_ref[f, later:rows])
        dmq = (dz[n_in - later:] + (live * rate) * dm).astype(BF).astype(F32)
        dmem[...] = dmq + (1.0 - live) * dm
        return dz[:n_in].astype(BF)

    def frame_backward(f):
        rows = z0.shape[1] - READ
        n_in = rows - MEM
        dlw, dlr = dlw_kept[f], dlr_kept[f]
        xh = xh0[f]
        dsm_ref[0, READ:READ + MEM] += nn(dlw, (xh * gain(10)).astype(BF))
        dsm_ref[0, :READ] += nn(dlr, (xh[:rows] * gain(0)).astype(BF))
        xh = xh[:n_in]
        dz = tn(bt0[f][:, :n_in].astype(BF), dt_kept[f]) + tn(at0[f][:, :n_in].astype(BF), ds_kept[f])
        dnw, dnr = tn(dlw[:, :n_in], ww_ref[0]), tn(dlr[:, :n_in], rw_ref[0])
        add_gain_grad(0, 5, dnw * xh)
        add_gain_grad(0, 0, dnr * xh)
        z0[f, tokens0] = (dz + normalize_back(dnw * gain(10) + dnr * gain(0), xh, rs0[f, :n_in])).astype(BF)

    for c in own_frames():
        c.start()
    for lb in range(lbs):
        for c in weight_copies(lb // BLOCKS, lb % BLOCKS, lb // BLOCKS, w_sem):
            c.start()
    row = lax.broadcasted_iota(jnp.int32, (HEADS * READ, width), 0) // READ
    col = lax.broadcasted_iota(jnp.int32, (HEADS * READ, width), 1) // HEAD
    mask_ref[...] = jnp.where(row == col, 1.0, 0.0).astype(BF)
    dsm_ref[...] = jnp.zeros_like(dsm_ref)
    for l in range(LAYERS):
        gains[l:l + 1] = rg_ref[...].astype(F32)[l:l + 1]
        gains[10 + l:11 + l] = wg_ref[...].astype(F32)[l:l + 1]
        for b in range(BLOCKS):
            lb = l * BLOCKS + b
            gains[2 + lb:3 + lb] = na_ref[l].astype(F32)[b:b + 1]
            gains[6 + lb:7 + lb] = nm_ref[l].astype(F32)[b:b + 1]
        spread = jnp.broadcast_to(decay_ref[l:l + 1], (MEM, MEM))
        diagonal = lax.broadcasted_iota(jnp.int32, (MEM, MEM), 0) == lax.broadcasted_iota(jnp.int32, (MEM, MEM), 1)
        dec_col[l] = jnp.sum(jnp.where(diagonal, spread, 0.0), axis=1, keepdims=True)

    pl.semaphore_wait(barrier, len(partners))
    for c in frame_copies():
        c.start()

    def together(*chains):
        chains = list(chains)
        while chains:
            for c in list(chains):
                try:
                    next(c)
                except StopIteration:
                    chains.remove(c)

    def keep(ref):
        def store(f, v):
            ref[f] = v

        return store

    kept0 = (z0, xh0, rs0, at0, bt0)
    kept1 = (z1, xh1, rs1, at1, bt1)

    for lb in range(lbs):
        for c in weight_copies(lb // BLOCKS, lb % BLOCKS, lb // BLOCKS, w_sem):
            c.wait()
    lax.fori_loop(0, BLOCKS, transpose_block, 0)
    for c in own_frames():
        c.wait()
    for c in frame_copies():
        c.wait_recv()
    mem0[...] = jnp.zeros_like(mem0)
    mem1[...] = jnp.zeros_like(mem1)

    def chain0(f):
        return layer_forward(0, f, *kept0, mem0, lambda f: None, keep(dout))

    def chain1(f):
        return layer_forward(1, f, *kept1, mem1, lambda f: dout[f], keep(res_v))

    def send_forward(l, f):
        for b in range(BLOCKS):
            start_forward(l * BLOCKS + b, f)

    def forward(f, carry):
        together(chain0(f), chain1(f - 1))
        send_forward(0, f)
        send_forward(1, f - 1)
        return carry

    together(chain0(0))
    send_forward(0, 0)
    lax.fori_loop(1, frames, forward, 0)
    for c in transposed_copies():
        c.start()
    together(chain1(frames - 1))
    send_forward(1, frames - 1)
    again = [c for b in range(BLOCKS) for c in weight_copies(0, b, 1, x_sem)]
    for c in again:
        c.start()
    for c in transposed_copies():
        c.wait()
    start_output(*results)
    dmem[...] = jnp.zeros_like(dmem)

    def backward1(i, carry):
        f = frames - 1 - i
        dout[f] = layer_backward(1, f, *kept1, cot_v[f].astype(F32))
        return carry

    lax.fori_loop(0, frames, backward1, 0)
    for c in again:
        c.wait()
    lax.fori_loop(0, BLOCKS, transpose_here, 0)
    start_small(1)
    dmem[...] = jnp.zeros_like(dmem)

    def backward0(i, carry):
        f = frames - 1 - i

        def middle():
            @pl.when(i == 0)
            def _():
                halve(3, 0, 0)
                halve(3, 0, 1)
                halve(2, 0, 0)
                halve(2, 0, 1)

        layer_backward(0, f, *kept0, dout[f].astype(F32), middle)

        @pl.when(i == 2)
        def _():
            halve(3, 1, 0)
            halve(3, 1, 1)

        return carry

    for u in (3, 2):
        wait_factors(u)
        form(u)
    halve_small(1, -1)
    lax.fori_loop(0, frames, backward0, 0)
    for f in range(frames):
        frame_backward(f)
    start_small(0)
    halve(2, 1, 0)
    halve(2, 1, 1)
    for u in (1, 0):
        wait_factors(u)
        form(u)
    for u in (1, 0):
        for p in range(PIECES):
            halve(u, 0, p)
    halve_small(0, -1)
    halve(3, 2, 0)
    halve(3, 2, 1)
    halve(1, 1, 0)
    halve(0, 1, 0)
    halve_small(0, 0)
    halve(2, 2, 0)
    halve(2, 2, 1)
    halve(1, 1, 1)
    halve(0, 1, 1)
    start_output(*frame_grads)
    halve_small(0, 1)
    halve(1, 2, 0)
    halve(0, 2, 0)
    halve_small(0, 2)
    halve(1, 2, 1)
    halve(0, 2, 1)
    for u in range(lbs - 1, -1, -1):
        finish(u)
    for out in (results, frame_grads):
        copies, own = output_copies(*out)
        for c in copies + [own]:
            c.wait()
    for c in frame_copies():
        c.wait_send()


def run_fused(sections, hi, lo, lengths, decay, gains, small, frames, cot, weights):
    count, _, tok, width = frames.shape
    lbs = LAYERS * BLOCKS
    ff = weights[2].shape[-1]
    cols = (4 * width + ff) // sections
    all_cols = cols + width
    bits = hi.bit_length() - 1
    chunk = sections * TILE
    peers = sections - 1
    vm, anym = pl.BlockSpec(memory_space=pltpu.VMEM), pl.BlockSpec(memory_space=pl.ANY)
    v, dma = pltpu.VMEM, pltpu.SemaphoreType.DMA

    def sds(shape, dtype):
        return jax.ShapeDtypeStruct(shape, dtype)

    def per(c, dtype):
        return v((lbs, count, READ, c), dtype)

    def by_section(c):
        return v((lbs, sections, count, READ, c), BF)

    rows0, rows1 = tok + MEM, READ + MEM
    lead, block = (LAYERS, BLOCKS), (2,) * bits + (width // hi,)
    transposed = [lead + (3,) + block + (width,), lead + block + (width,), lead + block + (ff,), lead + (ff // width,) + block + (width,)]
    weights = [weights[0].reshape(lead + block + (3 * width,))] + [w.reshape(s) for w, s in zip(weights[1:], transposed[1:])]
    scratch = [v(s, BF) for s in transposed]
    scratch += [v((count, READ, width), BF), v((count, READ, width), BF)]
    scratch += [v((count, r + READ, width), BF) for r in (rows0, rows1)]
    scratch += [v((count, r + READ, width), F32) for r in (rows0, rows1)]
    scratch += [v((count, r + READ, 1), F32) for r in (rows0, rows1)]
    scratch += [v((count, READ, r), F32) for r in (rows0, rows1)]
    scratch += [v((count, MEM, r + READ), F32) for r in (rows0, rows1)]
    scratch += [v((MEM, width), F32)] * 3
    scratch += [v((count, MEM, width), BF), v((count, READ, width), BF)]
    scratch += [v((count, MEM, rows0 + READ), BF), v((count, READ, rows0), BF), v((count, READ, width), BF)]
    scratch += [per(width, F32), per(1, F32), per(width, F32), per(1, F32)]
    scratch += [per(ff, BF), per(3 * width, BF), per(HEADS * READ, F32)]
    scratch += [v((HEADS * READ, width), BF), v((12, width), F32), v((LAYERS, MEM, 1), F32)]
    scratch += [v((LAYERS, SMALL, width), F32)]
    sliced = 4 * width // sections + width
    scratch += [by_section(sliced), by_section(3 * width), by_section(sliced)]
    scratch += [v((lbs,) + (2,) * bits + (chunk, all_cols), BF)]
    scratch += [[v((lbs,) + (2,) * (bits - 1 - k) + (chunk, all_cols), BF) for k in range(bits)]]
    scratch += [v((LAYERS, sections) + (2,) * bits + (TILE, SMALL), F32)] * 2
    scratch += [v((LAYERS,) + (2,) * bits + (TILE, SMALL), F32)]
    scratch += [[v((LAYERS,) + (2,) * (bits - 1 - k) + (TILE, SMALL), F32) for k in range(bits)]]
    scratch += [dma((LAYERS, BLOCKS, 6)), dma((LAYERS, BLOCKS, 6)), dma((BLOCKS, 12)), dma((12,))]
    scratch += [dma((peers, 2)), dma((peers, 2)), dma((2,)), dma((peers, 2)), dma((peers, 2)), dma((2,))]
    scratch += [dma((lbs, peers, 2)), dma((lbs, peers, 2)), dma((lbs,)), dma((lbs, bits, PIECES)), dma((lbs, bits, PIECES))]
    scratch += [dma((LAYERS, peers)), dma((LAYERS, peers)), dma((LAYERS, bits)), dma((LAYERS, bits))]
    scratch += [dma((lbs, PIECES, peers)), dma((lbs, PIECES, peers)), dma((lbs, PIECES + 1))]
    return pl.pallas_call(
        functools.partial(fused_kernel, hi, lo),
        out_shape=[
            sds((count, READ, width), BF),
            sds((count, tok, width), BF),
            sds((lbs, sections, TILE, cols), BF),
            sds((lbs, chunk, width), BF),
            sds((LAYERS, TILE, SMALL), F32),
        ]
        + [sds((4 + 2 * (ff // width),) + block + (width,), BF)],
        in_specs=[pl.BlockSpec(memory_space=pltpu.SMEM)] + [vm] * 7 + [anym] * 6,
        out_specs=[vm] * 5 + [anym],
        scratch_shapes=[scratch],
        compiler_params=pltpu.CompilerParams(
            collective_id=0, has_side_effects=True, vmem_limit_bytes=64 * 2**20 - 2**16
        ),
    )(lengths, decay, *gains, *small, frames, cot, *weights)[:5]


def widen_kernel(
    rows_ref, down_ref, small_ref, res_ref, fgrad_ref,
    res_out, fgrad_out, rg_out, rw_out, na_out, qkv_out, out_out, nm_out, up_out, down_out, wg_out, ww_out,
):
    sections, tile = rows_ref.shape[1:3]
    lbs = LAYERS * BLOCKS
    res_out[...] = res_ref[...]
    fgrad_out[...] = fgrad_ref[...]
    cols = [ref.shape[-1] // sections for ref in (qkv_out, out_out, up_out)]
    for u in range(lbs):
        l, b = u // BLOCKS, u % BLOCKS
        runs = 1 << len(free_bits(u))
        run = cols[2] // runs
        for s in range(sections):
            first = 0
            for ref, c in zip((qkv_out, out_out), cols):
                ref[l, b, :, s * c:(s + 1) * c] = rows_ref[u, s, :, first:first + c].astype(F32)
                first += c
            for j in range(runs):
                start = run_start(run, u, j, {bit: (s >> i) & 1 for i, bit in enumerate(GROUP[u])})
                up_out[l, b, :, start:start + run] = rows_ref[u, s, :, first + j * run:first + (j + 1) * run].astype(F32)
        down_out[l, b] = down_ref[u].astype(F32)
    diagonal = lax.broadcasted_iota(jnp.int32, (tile, tile), 0) == lax.broadcasted_iota(jnp.int32, (tile, tile), 1)

    def as_row(l, i):
        column = jnp.broadcast_to(small_ref[l][:, READ + MEM + i:READ + MEM + i + 1], (tile, tile))
        return jnp.sum(jnp.where(diagonal, column, 0.0), axis=0, keepdims=True)

    for l in range(LAYERS):
        rw_out[l] = small_ref[l][:, :READ]
        ww_out[l] = small_ref[l][:, READ:READ + MEM]
        rg_out[l:l + 1] = as_row(l, 0)
        wg_out[l:l + 1] = as_row(l, 1 + 2 * BLOCKS)
        for b in range(BLOCKS):
            na_out[l, b:b + 1] = as_row(l, 1 + b)
            nm_out[l, b:b + 1] = as_row(l, 1 + BLOCKS + b)


def widen(rows, down, sm, res, fgrad):
    sections, tile, cols = rows.shape[1:]
    width = down.shape[-1]
    vm = pl.BlockSpec(memory_space=pltpu.VMEM)

    def f32(*shape):
        return jax.ShapeDtypeStruct((LAYERS,) + shape, F32)

    out_shape = [jax.ShapeDtypeStruct(a.shape, a.dtype) for a in (res, fgrad)] + [
        f32(tile), f32(tile, READ), f32(BLOCKS, tile), f32(BLOCKS, tile, 3 * width), f32(BLOCKS, tile, width),
        f32(BLOCKS, tile), f32(BLOCKS, tile, sections * cols - 4 * width), f32(BLOCKS, *down.shape[1:]),
        f32(tile), f32(tile, MEM),
    ]
    return pl.pallas_call(
        widen_kernel, out_shape=out_shape, in_specs=[vm] * 5, out_specs=[vm] * len(out_shape)
    )(rows, down, sm, res, fgrad)


def local(
    frames, lengths, decay, read_gain, read_weight, norm_attn, w_qkv, w_out, norm_mlp, w_up, w_down,
    write_gain, write_weight, cotangent,
):
    sections, dp = lax.axis_size("section"), lax.axis_size("dp")
    clip_dev, span, tok, width = frames.shape
    hi = width // (sections * TILE)
    lo = dp // hi
    assert clip_dev == sections and span == 1 and hi * lo == dp
    res, fgrad, rows, down, sm = run_fused(
        sections, hi, lo, lengths, decay, (read_gain, norm_attn, norm_mlp, write_gain),
        [jnp.swapaxes(w, 1, 2) for w in (read_weight, write_weight)], frames, cotangent, (w_qkv, w_out, w_up, w_down),
    )
    if lo > 1:
        groups = [[h * lo + k for k in range(lo)] for h in range(hi)]

        def over_rest(v, axis):
            return lax.psum_scatter(
                v.astype(F32), "dp", scatter_dimension=axis, axis_index_groups=groups, tiled=True
            )

        rows, down, sm = over_rest(rows, 2), over_rest(down, 1), over_rest(sm, 1)
    res, fgrad, *grads = widen(rows, down, sm, res, fgrad)
    return (res[:, None], fgrad[:, None], *grads)


def solution(mesh):
    both = ("section", "dp")
    split = P("dp", "section", None, None)
    return jax.shard_map(
        local,
        mesh=mesh,
        in_specs=(split, P("dp")) + (P(),) * 11 + (split,),
        out_specs=(
            split, split, P(None, both), P(None, both, None), P(None, None, both), P(None, None, both, None),
            P(None, None, both, None), P(None, None, both), P(None, None, both, None),
            P(None, None, both, None), P(None, both), P(None, both, None),
        ),
        check_vma=False,
    )
```

```python
import functools

import jax
import jax.numpy as jnp
from jax import lax
from jax.experimental import pallas as pl
from jax.experimental.pallas import tpu as pltpu
from jax.sharding import PartitionSpec as P

HEADS = 8
HEAD = 64
MEM = 96
READ = 16
BLOCKS = 2
LAYERS = 2
EPS = 1e-05
SMALL = 128
TILE = 16
PIECES = 2
S0, S1, D0, D1, D2 = ("section", 0), ("section", 1), ("dp", 0), ("dp", 1), ("dp", 2)
ROW_BITS = (S1, S0, D2, D1, D0)
GROUP = ((S0, D1), (S1, D2)) * LAYERS
SUM = ((D0, S1, D2), (D0, S0, D1)) * LAYERS


def free_bits(u):
    return tuple(b for b in ROW_BITS if b not in GROUP[u] and b != D0)


def run_start(bit, u, j, fixed):
    free = free_bits(u)
    value = {b: (j >> (len(free) - 1 - i)) & 1 for i, b in enumerate(free)} | fixed
    return sum(value[b] * (bit << (len(ROW_BITS) - 2 - i)) for i, b in enumerate(ROW_BITS[:-1]))
BF = jnp.bfloat16
F32 = jnp.float32


def nn(a, b):
    return lax.dot_general(a, b, (((1,), (0,)), ((), ())), preferred_element_type=F32)


def nt(a, b):
    return lax.dot_general(a, b, (((1,), (1,)), ((), ())), preferred_element_type=F32)


def tn(a, b):
    return lax.dot_general(a, b, (((0,), (0,)), ((), ())), preferred_element_type=F32)


def normalize(v):
    centred = v - jnp.mean(v, axis=-1, keepdims=True)
    spread = jnp.mean(centred * centred, axis=-1, keepdims=True)
    r = lax.rsqrt(spread + EPS)
    return centred * r, r


def centre(v):
    centred = v - jnp.mean(v, axis=-1, keepdims=True)
    return centred, lax.rsqrt(jnp.mean(centred * centred, axis=-1, keepdims=True) + EPS)


def normalize_back(dx, xh, r):
    return r * (dx - jnp.mean(dx, axis=-1, keepdims=True) - xh * jnp.mean(dx * xh, axis=-1, keepdims=True))


def gelu_and_slope(x):
    c0, c1 = 0.7978845608028654, 0.044715
    x2 = x * x
    t = jnp.tanh(c0 * x * (1.0 + c1 * x2))
    return 0.5 * x * (1.0 + t), 0.5 * (1.0 + t) + 0.5 * x * (1.0 - t * t) * c0 * (1.0 + 3.0 * c1 * x2)


def softmax_lanes(v):
    e = jnp.exp(v - jnp.max(v, axis=1, keepdims=True))
    return e / jnp.sum(e, axis=1, keepdims=True)


def softmax_lanes_back(p, dp):
    return p * (dp - jnp.sum(p * dp, axis=1, keepdims=True))


def fused_kernel(
    hi, lo, len_ref, decay_ref, rg_ref, na_ref, nm_ref, wg_ref, rw_ref, ww_ref, frames_hbm, cot_hbm,
    wqkv_hbm, wout_hbm, wup_hbm, wdown_hbm, res_out, fgrad_out, rows_ref, down_ref, small_ref,
    turn_hbm, scratch,
):
    (
        wq, wo, wu, wd, cot_v, res_v, z0, z1, xh0, xh1, rs0, rs1, at0, at1, bt0, bt1,
        mem0, mem1, dmem0, dmem1, dt_kept, ds_kept, dlw_kept, dlr_kept, dout, xa, ra, xm, rm, gp, qkv, pt, mask_ref, gains, dec_col, dsm_ref,
        slice_b, all_f, part_b, wgrad, into, small_t, small_in, small_sum, small_into,
        w_sem, x_sem, v_sem, t_sem, f_send, f_recv, f_own, o_send, o_recv, o_own,
        a_send, a_recv, a_own, c_send, c_recv, s_send, s_recv, t_send, t_recv, d_send, d_recv, d_own,
    ) = scratch
    sections, frames = all_f.shape[1:3]
    tokens0 = pl.ds(0, frames_hbm.shape[2])
    width = dsm_ref.shape[-1]
    lbs = LAYERS * BLOCKS
    me, dp_at = lax.axis_index("section"), lax.axis_index("dp")
    bits = hi.bit_length() - 1
    peers = [(me + k) % sections for k in range(1, sections)]
    members = 1 << len(GROUP[0])
    own = {S0: me % 2, S1: (me // 2) % 2} | {("dp", k): (dp_at // (lo << k)) % 2 for k in range(bits)}
    assert sections == 4 and bits == 3

    def device(flips):
        s, d = me, dp_at
        for axis, k in flips:
            step = 1 - 2 * own[axis, k]
            s, d = (s + step * (1 << k), d) if axis == "section" else (s, d + step * (lo << k))
        return {"section": s, "dp": d}

    def flips_of(u, x):
        return tuple(b for j, b in enumerate(GROUP[u]) if (x >> j) & 1)

    def member(u, x):
        return sum((1 - own[b] if (x >> j) & 1 else own[b]) * (1 << j) for j, b in enumerate(GROUP[u]))

    here = [member(u, 0) for u in range(lbs)]

    every = (slice(None),) * (bits + 1)
    ups = wd.shape[2]

    def columns(i):
        return every + (pl.ds(i * width, width),)

    def weight_copies(l, b, to, sem):
        pairs = [(wqkv_hbm.at[(l, b) + columns(i)], wq.at[to, b, i]) for i in range(3)]
        pairs += [(wout_hbm.at[l, b], wo.at[to, b]), (wup_hbm.at[l, b], wu.at[to, b]), (wdown_hbm.at[l, b], wd.at[to, b])]
        return [pltpu.make_async_copy(s, d, sem.at[l, b, i]) for i, (s, d) in enumerate(pairs)]

    def squares(l, b):
        out = [(wq.at[l, b, i],) * 2 for i in range(3)] + [(wo.at[l, b],) * 2]
        for i in range(ups):
            pair = (wu.at[(l, b) + columns(i)], wd.at[l, b, i])
            out += [pair, pair[::-1]]
        return out

    def staged(i):
        return wgrad.at[(i // 3,) + columns(i % 3)]

    def turned(ref):
        return ref[...].reshape(width, width).T.reshape(ref.shape)

    def kept_copies():
        return [pltpu.make_async_copy(staged(i), turn_hbm.at[i], t_sem.at[i]) for i in range(4 + 2 * ups)]

    def transpose_block(b, carry):
        copies = kept_copies()
        for i, (s, _) in enumerate(squares(1, b)):
            pl.when(b > 0)(copies[i].wait)
            staged(i)[...] = turned(s)
            pl.when(b == 0)(copies[i].start)
        return carry

    def transposed_copies():
        out = []
        for b in range(BLOCKS):
            for i, (_, d) in enumerate(squares(0, b)):
                out.append(pltpu.make_async_copy(turn_hbm.at[i] if b == 0 else staged(i), d, v_sem.at[b, i]))
        return out

    def transpose_here(b, carry):
        for i, (s, d) in enumerate(squares(1, b)):
            if i < 4:
                d[...] = turned(s)
            elif i % 2 == 0:
                first, second = turned(s), turned(d)
                d[...], s[...] = first, second
        return carry

    def weight(ref, *at):
        w = ref[at]
        return w.reshape(-1, w.shape[-1])

    barrier = pltpu.get_barrier_semaphore()
    partners = {(S0,), (S1,), (S0, S1)} | {(b,) for bits_of in SUM for b in bits_of}
    partners |= {tuple(sorted(flips_of(u, x))) for u in range(lbs) for x in range(1, members)}
    partners = sorted({tuple(sorted(p)) for p in partners})
    for p in partners:
        pl.semaphore_signal(barrier, inc=1, device_id=device(p), device_id_type=pl.DeviceIdType.MESH)

    def remote(src, dst, send, recv, to):
        return pltpu.make_async_remote_copy(
            src_ref=src, dst_ref=dst, send_sem=send, recv_sem=recv, device_id=to, device_id_type=pl.DeviceIdType.MESH
        )

    def forward_copies(u, first, count):
        at = all_f.at[u, here[u], pl.ds(first, count)]
        return [
            remote(at, at, a_send.at[u, x - 1, 0], a_recv.at[u, x - 1, 0], device(flips_of(u, x)))
            for x in range(1, members)
        ]

    def backward_copies(u, first, count):
        at = pl.ds(first, count)
        return [
            remote(
                slice_b.at[u, member(u, x), at], part_b.at[u, here[u], at],
                a_send.at[u, x - 1, 1], a_recv.at[u, x - 1, 1], device(flips_of(u, x)),
            )
            for x in range(1, members)
        ]

    def own_backward(u, first, count):
        at = pl.ds(first, count)
        return pltpu.make_async_copy(slice_b.at[u, here[u], at], part_b.at[u, here[u], at], a_own.at[u])

    def start_forward(u, f):
        for c in forward_copies(u, f, 1):
            c.start()

    def start_backward(u, f):
        for c in backward_copies(u, f, 1) + [own_backward(u, f, 1)]:
            c.start()

    def wait_factors(u):
        own_backward(u, 0, frames).wait()
        for c in forward_copies(u, 0, frames) + backward_copies(u, 0, frames):
            c.wait_recv()

    def place(u, s, h):
        value = {("section", k): (s >> k) & 1 for k in range(2)} | {("dp", k): (h >> k) & 1 for k in range(bits)}
        return tuple(value[b] for b in reversed(SUM[u])), sum(value[b] << j for j, b in enumerate(GROUP[u]))

    def start_small(l):
        rows = jnp.transpose(dsm_ref[l]).reshape(sections, hi, TILE, SMALL)
        for s in range(sections):
            for h in range(hi):
                at, g = place(l * BLOCKS, s, h)
                small_t[(l, g) + at] = rows[s, h]
        for c in small_copies(l):
            c.start()

    def small_copies(l):
        u = l * BLOCKS
        return [
            remote(
                small_t.at[l, member(u, x)], small_in.at[l, here[u]],
                s_send.at[l, x - 1], s_recv.at[l, x - 1], device(flips_of(u, x)),
            )
            for x in range(1, members)
        ]

    def halves(u, k, other):
        b = own[SUM[u][k]]
        fixed = tuple(own[SUM[u][j]] for j in range(k - 1, -1, -1))
        return (slice(None),) * (bits - 1 - k) + ((1 - b) if other else b,) + fixed

    def own_at(u):
        return tuple(own[b] for b in reversed(SUM[u]))

    def piece(p):
        size = wgrad.shape[-1] // PIECES
        return (slice(None), pl.ds(p * size, size))

    def halving_copy(u, k, p):
        return remote(
            wgrad.at[(u,) + halves(u, k, True) + piece(p)],
            into[k].at[(u,) + (slice(None),) * (bits - 1 - k) + piece(p)],
            c_send.at[u, k, p], c_recv.at[u, k, p], device((SUM[u][k],)),
        )

    def small_halving_copy(l, k):
        u = l * BLOCKS
        return remote(
            small_sum.at[(l,) + halves(u, k, True)], small_into[k].at[l], t_send.at[l, k], t_recv.at[l, k],
            device((SUM[u][k],)),
        )

    cols = wgrad.shape[-1] - width

    def final_columns(p):
        size = wgrad.shape[-1] // PIECES
        return pl.ds(p * size, min(size, cols - p * size))

    def own_rows(u, g, p):
        return wgrad.at[(u,) + own_at(u) + (pl.ds(pl.multiple_of(g * TILE, TILE), TILE), final_columns(p))]

    def row_copies(u, p):
        dst = rows_ref.at[u, here[u], :, final_columns(p)]
        return [
            remote(
                own_rows(u, member(u, x), p), dst, d_send.at[u, p, x - 1], d_recv.at[u, p, x - 1], device(flips_of(u, x))
            )
            for x in range(1, members)
        ] + [pltpu.make_async_copy(own_rows(u, here[u], p), dst, d_own.at[u, p])]

    def down_copy(u):
        down = wgrad.at[(u,) + own_at(u) + (slice(None), pl.ds(cols, width))]
        return pltpu.make_async_copy(down, down_ref.at[u], d_own.at[u, PIECES])

    def store_rows(u, first, v):
        c = v.shape[1]
        v = v.astype(BF).reshape(sections, hi, TILE, c)
        for s in range(sections):
            for h in range(hi):
                at, g = place(u, s, h)
                wgrad[(u,) + at + (slice(g * TILE, (g + 1) * TILE), slice(first, first + c))] = v[s, h]

    def store_down(u, first, v):
        c = v.shape[1]
        order = free_bits(u) + (D0,)
        v = v.astype(BF).reshape(1 << len(order), members * TILE, c)
        for j in range(1 << len(order)):
            value = {b: (j >> (len(order) - 1 - i)) & 1 for i, b in enumerate(order)}
            at = tuple(value[b] for b in reversed(SUM[u]))
            wgrad[(u,) + at + (slice(None), slice(first, first + c))] = v[j]

    def form(u):
        l, b = u // BLOCKS, u % BLOCKS
        q, o = 3 * width // members, 4 * width // members
        runs = 1 << len(free_bits(u))
        run = wu.shape[-1] // (members * runs)
        fixed = {bit: own[bit] for bit in GROUP[u]}

        def flat(ref, first, count):
            v = ref[u, :, :, :, first:first + count]
            return v.reshape(members * frames * READ, count)

        def up_run(j):
            at = {bit: (j >> (len(free_bits(u)) - 1 - i)) & 1 for i, bit in enumerate(free_bits(u))} | fixed
            w = wd[1 - l, b, 2 * at[S1] + at[S0], at[D2], at[D1]]
            return w.reshape(-1, w.shape[-1])

        def down_run(j):
            start = pl.multiple_of(run_start(run, u, j, fixed), run)
            return weight(wu, 1 - l, b, *every, pl.ds(start, run))

        u_all, dh_all = flat(all_f, 2 * width, width), flat(part_b, o, width)
        up_rows = jnp.concatenate([up_run(j) for j in range(runs)], axis=0)
        down_cols = jnp.concatenate([down_run(j) for j in range(runs)], axis=1)
        lift, slope = gelu_and_slope(nt(u_all, up_rows))
        dup = (nn(dh_all, down_cols) * slope).astype(BF)
        store_rows(u, 0, tn(flat(all_f, 0, width), flat(part_b, 0, q)))
        store_rows(u, q, tn(flat(all_f, width, width), flat(part_b, q, o - q)))
        store_rows(u, o, tn(u_all, dup))
        store_down(u, cols, tn(lift.astype(BF), dh_all))
        for p in range(PIECES):
            halving_copy(u, 0, p).start()

    def halve_small(l, k):
        if k < 0:
            for c in small_copies(l):
                c.wait_recv()
            total = small_t[l, here[l * BLOCKS]]
            for x in range(1, members):
                total = total + small_in[l, member(l * BLOCKS, x)]
            small_sum[l] = total
        else:
            small_halving_copy(l, k).wait_recv()
            at = (l,) + halves(l * BLOCKS, k, False)
            small_sum[at] = small_sum[at] + small_into[k][l]
        if k + 1 < bits:
            small_halving_copy(l, k + 1).start()
        else:
            small_ref[l] = small_sum[(l,) + own_at(l * BLOCKS)]

    def halve(u, k, p):
        halving_copy(u, k, p).wait_recv()
        at = (u,) + halves(u, k, False) + piece(p)
        wgrad[at] = wgrad[at] + into[k][(u,) + (slice(None),) * (bits - 1 - k) + piece(p)]
        if k + 1 < bits:
            halving_copy(u, k + 1, p).start()
        elif u != lbs - 1:
            send_rows(u, p)

    def send_rows(u, p):
        for c in row_copies(u, p):
            c.start()
        if p + 1 == PIECES:
            down_copy(u).start()

    def finish(u):
        for p in range(PIECES):
            for c in row_copies(u, p):
                c.wait()
        down_copy(u).wait()
        for k in range(bits):
            for p in range(PIECES):
                halving_copy(u, k, p).wait_send()
        for c in forward_copies(u, 0, frames) + backward_copies(u, 0, frames):
            c.wait_send()
        if u % BLOCKS == 0:
            l = u // BLOCKS
            for c in small_copies(l):
                c.wait_send()
            for k in range(bits):
                small_halving_copy(l, k).wait_send()

    def frame_copies():
        return [
            remote(src.at[p, 0], dst, f_send.at[k, i], f_recv.at[k, i], {"section": p})
            for k, p in enumerate(peers)
            for i, (src, dst) in enumerate(((frames_hbm, z0.at[me, tokens0]), (cot_hbm, cot_v.at[me])))
        ]

    def own_frames():
        return [
            pltpu.make_async_copy(src.at[me, 0], dst, f_own.at[i])
            for i, (src, dst) in enumerate(((frames_hbm, z0.at[me, tokens0]), (cot_hbm, cot_v.at[me])))
        ]

    def output_copies(i, src, dst):
        copies = [
            remote(src(p), dst.at[me], o_send.at[k, i], o_recv.at[k, i], {"section": p}) for k, p in enumerate(peers)
        ]
        return copies, pltpu.make_async_copy(src(me), dst.at[me], o_own.at[i])

    results = (0, lambda f: res_v.at[f], res_out)
    frame_grads = (1, lambda f: z0.at[f, tokens0], fgrad_out)

    def start_output(i, src, dst):
        copies, own = output_copies(i, src, dst)
        for c in copies + [own]:
            c.start()

    def spread_heads(v):
        return jnp.concatenate([v] * HEADS, axis=0) * mask_ref[...]

    def gather_heads(v):
        return jnp.sum((v * mask_ref[...].astype(F32)).reshape(HEADS, READ, width), axis=0)

    def live_at(f):
        return jnp.where(f < len_ref[me], 1.0, 0.0).astype(F32)

    def keep_slices(lb, f, first, v):
        c = v.shape[1] // members
        for s in range(members):
            slice_b[lb, s, f, :, first:first + c] = v[:, s * c:(s + 1) * c]

    def add_gain_grad(l, i, v):
        dsm_ref[l, READ + MEM + i:READ + MEM + i + 1, :] += jnp.sum(v, axis=0, keepdims=True)

    def gain(i):
        return gains[i:i + 1, :]

    def block_forward(lb, f, h):
        centred, r = centre(h)
        xh = centred * r
        xa[lb, f], ra[lb, f] = xh, r
        g = (xh * gain(2 + lb)).astype(BF)
        wide = (centred * gain(2 + lb)).astype(BF)
        all_f[lb, here[lb], f, :, :width] = g
        l, b = lb // BLOCKS, lb % BLOCKS
        q, k, v = ((nn(wide, weight(wq, l, b, i)) * r).astype(BF) for i in range(3))
        yield
        for i, part in enumerate((q, k, v)):
            qkv[lb, f, :, i * width:(i + 1) * width] = part
        s = nt(k, spread_heads(q)) * HEAD ** (-0.5)
        yield
        e = jnp.exp(s - jnp.max(s, axis=0, keepdims=True))
        p = e / jnp.sum(e, axis=0, keepdims=True)
        pt[lb, f] = p
        o = tn(p.astype(BF), v)
        yield
        o = gather_heads(o).astype(BF)
        all_f[lb, here[lb], f, :, width:2 * width] = o
        h = h + nn(o, weight(wo, l, b))
        yield
        centred, r = centre(h)
        xh = centred * r
        xm[lb, f], rm[lb, f] = xh, r
        u = (xh * gain(6 + lb)).astype(BF)
        wide = (centred * gain(6 + lb)).astype(BF)
        all_f[lb, here[lb], f, :, 2 * width:] = u
        x = nn(wide, weight(wu, l, b)) * r
        yield
        lift, slope = gelu_and_slope(x)
        lift, gp[lb, f] = lift.astype(BF), slope.astype(BF)
        h = h + nn(lift, weight(wd, l, b))
        yield
        return h

    def block_backward(lb, f, dh):
        l, b = lb // BLOCKS, lb % BLOCKS
        dhb = dh.astype(BF)
        for s in range(members):
            slice_b[lb, s, f, :, 4 * width // members:] = dhb
        dup = nn(dhb, weight(wu, 1 - l, b))
        yield
        dup = (dup * gp[lb, f].astype(F32)).astype(BF)
        du = nn(dup, weight(wd, 1 - l, b))
        yield
        xh = xm[lb, f]
        add_gain_grad(lb // BLOCKS, 3 + lb % BLOCKS, du * xh)
        dh = dh + normalize_back(du * gain(6 + lb), xh, rm[lb, f])
        dhb = dh.astype(BF)
        keep_slices(lb, f, 3 * width // members, dhb)
        do = nn(dhb, weight(wo, 1 - l, b))
        yield
        do = spread_heads(do.astype(BF))
        joined = qkv[lb, f]
        q, k, v = joined[:, :width], joined[:, width:2 * width], joined[:, 2 * width:]
        p = pt[lb, f]
        dp = nt(v, do)
        yield
        ds = (p * (dp - jnp.sum(p * dp, axis=0, keepdims=True)) * HEAD ** (-0.5)).astype(BF)
        dv = nn(p.astype(BF), do)
        dk = nn(ds, spread_heads(q))
        dq = tn(ds, k)
        yield
        dq = gather_heads(dq)
        dj = [d.astype(BF) for d in (dq, dk, dv)]
        keep_slices(lb, f, 0, jnp.concatenate(dj, axis=1))
        dg = sum(nn(d, weight(wq, 1 - l, b, i)) for i, d in enumerate(dj))
        yield
        xh = xa[lb, f]
        add_gain_grad(lb // BLOCKS, 1 + lb % BLOCKS, dg * xh)
        return dh + normalize_back(dg * gain(2 + lb), xh, ra[lb, f])

    def layer_forward(l, f, z, xh_ref, rs_ref, at, bt, mem, read_inputs, store):
        live = live_at(f)
        inputs = read_inputs(f)
        m = mem[...]
        rows = z.shape[1] - READ
        n_in = rows - MEM
        if inputs is not None:
            z[f, :n_in] = inputs
        z[f, n_in:rows] = m.astype(BF)
        zz = z[f, :rows]
        xh, r = normalize(zz.astype(F32))
        xh_ref[f, :rows], rs_ref[f, :rows] = xh, r
        n = (xh * gain(l)).astype(BF)
        logits = nt(rw_ref[l], n)
        yield
        a = softmax_lanes(logits)
        at[f] = a
        h = nn(a.astype(BF), zz)
        yield
        for b in range(BLOCKS):
            h = yield from block_forward(l * BLOCKS + b, f, h)
        y = h.astype(BF)
        z[f, rows:] = y
        xh, r = normalize(y.astype(F32))
        xh_ref[f, rows:], rs_ref[f, rows:] = xh, r
        n = (xh_ref[f] * gain(10 + l)).astype(BF)
        logits = nt(ww_ref[l], n)
        yield
        b = softmax_lanes(logits)
        bt[f] = b
        written = nn(b.astype(BF), z[f])
        yield
        rate = dec_col[l]
        updated = rate * z[f, n_in:rows].astype(F32) + (1.0 - rate) * written
        mem[...] = live * updated + (1.0 - live) * m
        store(f, (live * y.astype(F32)).astype(BF))

    def layer_backward(l, f, z, xh_ref, rs_ref, at, bt, dmem, read_grad, store, middle=None):
        live = live_at(f)
        rows = z.shape[1] - READ
        n_in = rows - MEM
        later = n_in if l == 0 else 0
        dm = dmem[...]
        rate = dec_col[l]
        dt = ((live * (1.0 - rate)) * dm).astype(BF)
        zf = z[f]
        b = bt[f]
        dl = nt(dt, zf)
        yield
        dl = softmax_lanes_back(b, dl).astype(BF)
        dz = tn(b[:, later:].astype(BF), dt)
        dn = tn(dl[:, later:], ww_ref[l])
        yield
        xh = xh_ref[f, later:]
        if l == 0:
            dt_kept[f], dlw_kept[f] = dt, dl
        else:
            dsm_ref[l, READ:READ + MEM] += nn(dl, (xh * gain(10 + l)).astype(BF))
        add_gain_grad(l, 5, dn * xh)
        dx = dn * gain(10 + l)
        tail = rows - later
        dy = dz[tail:] + normalize_back(dx[tail:], xh[tail:], rs_ref[f, rows:]) + live * read_grad(f)
        dh = dy.astype(BF).astype(F32)
        for bb in range(BLOCKS - 1, -1, -1):
            dh = yield from block_backward(l * BLOCKS + bb, f, dh)
            if bb and middle is not None:
                middle()
        ds = dh.astype(BF)
        xh = xh[:tail]
        a = at[f]
        dl = nt(ds, zf[:rows])
        yield
        dl = softmax_lanes_back(a, dl).astype(BF)
        dz = dz[:tail] + tn(a[:, later:].astype(BF), ds)
        dn = tn(dl[:, later:], rw_ref[l])
        yield
        if l == 0:
            ds_kept[f], dlr_kept[f] = ds, dl
        else:
            dsm_ref[l, :READ] += nn(dl, (xh * gain(l)).astype(BF))
        add_gain_grad(l, 0, dn * xh)
        dz = dz + normalize_back(dx[:tail] + dn * gain(l), xh, rs_ref[f, later:rows])
        dmq = (dz[n_in - later:] + (live * rate) * dm).astype(BF).astype(F32)
        dmem[...] = dmq + (1.0 - live) * dm
        store(f, dz[:n_in].astype(BF))

    def frame_backward(f):
        rows = z0.shape[1] - READ
        n_in = rows - MEM
        dlw, dlr = dlw_kept[f], dlr_kept[f]
        xh = xh0[f]
        dsm_ref[0, READ:READ + MEM] += nn(dlw, (xh * gain(10)).astype(BF))
        dsm_ref[0, :READ] += nn(dlr, (xh[:rows] * gain(0)).astype(BF))
        xh = xh[:n_in]
        dz = tn(bt0[f][:, :n_in].astype(BF), dt_kept[f]) + tn(at0[f][:, :n_in].astype(BF), ds_kept[f])
        dnw, dnr = tn(dlw[:, :n_in], ww_ref[0]), tn(dlr[:, :n_in], rw_ref[0])
        add_gain_grad(0, 5, dnw * xh)
        add_gain_grad(0, 0, dnr * xh)
        z0[f, tokens0] = (dz + normalize_back(dnw * gain(10) + dnr * gain(0), xh, rs0[f, :n_in])).astype(BF)

    for c in own_frames():
        c.start()
    for lb in range(lbs):
        for c in weight_copies(lb // BLOCKS, lb % BLOCKS, lb // BLOCKS, w_sem):
            c.start()
    row = lax.broadcasted_iota(jnp.int32, (HEADS * READ, width), 0) // READ
    col = lax.broadcasted_iota(jnp.int32, (HEADS * READ, width), 1) // HEAD
    mask_ref[...] = jnp.where(row == col, 1.0, 0.0).astype(BF)
    dsm_ref[...] = jnp.zeros_like(dsm_ref)
    for l in range(LAYERS):
        gains[l:l + 1] = rg_ref[...].astype(F32)[l:l + 1]
        gains[10 + l:11 + l] = wg_ref[...].astype(F32)[l:l + 1]
        for b in range(BLOCKS):
            lb = l * BLOCKS + b
            gains[2 + lb:3 + lb] = na_ref[l].astype(F32)[b:b + 1]
            gains[6 + lb:7 + lb] = nm_ref[l].astype(F32)[b:b + 1]
        spread = jnp.broadcast_to(decay_ref[l:l + 1], (MEM, MEM))
        diagonal = lax.broadcasted_iota(jnp.int32, (MEM, MEM), 0) == lax.broadcasted_iota(jnp.int32, (MEM, MEM), 1)
        dec_col[l] = jnp.sum(jnp.where(diagonal, spread, 0.0), axis=1, keepdims=True)

    pl.semaphore_wait(barrier, len(partners))
    for c in frame_copies():
        c.start()

    def together(*chains):
        chains = list(chains)
        while chains:
            for c in list(chains):
                try:
                    next(c)
                except StopIteration:
                    chains.remove(c)

    def keep(ref):
        def store(f, v):
            ref[f] = v

        return store

    kept0 = (z0, xh0, rs0, at0, bt0)
    kept1 = (z1, xh1, rs1, at1, bt1)

    for lb in range(lbs):
        for c in weight_copies(lb // BLOCKS, lb % BLOCKS, lb // BLOCKS, w_sem):
            c.wait()
    lax.fori_loop(0, BLOCKS, transpose_block, 0)
    for c in own_frames():
        c.wait()
    for c in frame_copies():
        c.wait_recv()
    mem0[...] = jnp.zeros_like(mem0)
    mem1[...] = jnp.zeros_like(mem1)

    def chain0(f):
        return layer_forward(0, f, *kept0, mem0, lambda f: None, keep(dout))

    def chain1(f):
        return layer_forward(1, f, *kept1, mem1, lambda f: dout[f], keep(res_v))

    def send_forward(l, f):
        for b in range(BLOCKS):
            start_forward(l * BLOCKS + b, f)

    def forward(f, carry):
        together(chain0(f), chain1(f - 1))
        send_forward(0, f)
        send_forward(1, f - 1)
        return carry

    together(chain0(0))
    send_forward(0, 0)
    lax.fori_loop(1, frames, forward, 0)
    for c in transposed_copies():
        c.start()
    together(chain1(frames - 1))
    send_forward(1, frames - 1)
    again = [c for b in range(BLOCKS) for c in weight_copies(0, b, 1, x_sem)]
    for c in again:
        c.start()
    for c in transposed_copies():
        c.wait()
    start_output(*results)
    dmem0[...] = jnp.zeros_like(dmem0)
    dmem1[...] = jnp.zeros_like(dmem1)

    def back0(f, middle=None):
        return layer_backward(0, f, *kept0, dmem0, lambda f: dout[f].astype(F32), lambda f, v: None, middle)

    def back1(f):
        return layer_backward(1, f, *kept1, dmem1, lambda f: cot_v[f].astype(F32), keep(dout))

    def send_backward(l, f):
        for b in range(BLOCKS - 1, -1, -1):
            start_backward(l * BLOCKS + b, f)

    def backward(i, carry):
        f = frames - 1 - i
        together(back1(f), back0(f + 1))
        send_backward(1, f)
        send_backward(0, f + 1)
        return carry

    together(back1(frames - 1))
    send_backward(1, frames - 1)
    for c in again:
        c.wait()
    lax.fori_loop(0, BLOCKS, transpose_here, 0)
    lax.fori_loop(1, frames, backward, 0)
    start_small(1)
    together(back0(0, lambda: start_backward(1, 0)))
    start_backward(0, 0)
    for u in (3, 2):
        wait_factors(u)
        form(u)
    halve_small(1, -1)
    for f in range(frames):
        frame_backward(f)
    start_small(0)
    halve_small(1, 0)
    for u in (3, 2):
        for p in range(PIECES):
            halve(u, 0, p)
    for u in (1, 0):
        wait_factors(u)
        form(u)
    halve_small(0, -1)
    halve(1, 0, 0)
    halve(1, 0, 1)
    halve_small(0, 0)
    halve(0, 0, 0)
    halve(0, 0, 1)
    start_output(*frame_grads)
    halve_small(1, 1)
    halve(3, 1, 0)
    halve(2, 1, 0)
    halve(3, 1, 1)
    halve(2, 1, 1)
    halve_small(0, 1)
    halve_small(1, 2)
    halve(3, 2, 0)
    halve(2, 2, 0)
    halve(1, 1, 0)
    halve(0, 1, 0)
    halve(3, 2, 1)
    halve(2, 2, 1)
    halve(1, 1, 1)
    halve(0, 1, 1)
    for p in range(PIECES):
        send_rows(lbs - 1, p)
    halve(1, 2, 0)
    halve(0, 2, 0)
    halve(1, 2, 1)
    halve(0, 2, 1)
    halve_small(0, 2)
    for u in range(lbs - 1, -1, -1):
        finish(u)
    for out in (results, frame_grads):
        copies, own = output_copies(*out)
        for c in copies + [own]:
            c.wait()
    for c in frame_copies():
        c.wait_send()


def run_fused(sections, hi, lo, lengths, decay, gains, small, frames, cot, weights):
    count, _, tok, width = frames.shape
    lbs = LAYERS * BLOCKS
    ff = weights[2].shape[-1]
    cols = (4 * width + ff) // sections
    all_cols = cols + width
    bits = hi.bit_length() - 1
    chunk = sections * TILE
    peers = sections - 1
    vm, anym = pl.BlockSpec(memory_space=pltpu.VMEM), pl.BlockSpec(memory_space=pl.ANY)
    v, dma = pltpu.VMEM, pltpu.SemaphoreType.DMA

    def sds(shape, dtype):
        return jax.ShapeDtypeStruct(shape, dtype)

    def per(c, dtype):
        return v((lbs, count, READ, c), dtype)

    def by_section(c):
        return v((lbs, sections, count, READ, c), BF)

    rows0, rows1 = tok + MEM, READ + MEM
    lead, block = (LAYERS, BLOCKS), (2,) * bits + (width // hi,)
    transposed = [lead + (3,) + block + (width,), lead + block + (width,), lead + block + (ff,), lead + (ff // width,) + block + (width,)]
    weights = [weights[0].reshape(lead + block + (3 * width,))] + [w.reshape(s) for w, s in zip(weights[1:], transposed[1:])]
    scratch = [v(s, BF) for s in transposed]
    scratch += [v((count, READ, width), BF), v((count, READ, width), BF)]
    scratch += [v((count, r + READ, width), BF) for r in (rows0, rows1)]
    scratch += [v((count, r + READ, width), F32) for r in (rows0, rows1)]
    scratch += [v((count, r + READ, 1), F32) for r in (rows0, rows1)]
    scratch += [v((count, READ, r), F32) for r in (rows0, rows1)]
    scratch += [v((count, MEM, r + READ), F32) for r in (rows0, rows1)]
    scratch += [v((MEM, width), F32)] * 4
    scratch += [v((count, MEM, width), BF), v((count, READ, width), BF)]
    scratch += [v((count, MEM, rows0 + READ), BF), v((count, READ, rows0), BF), v((count, READ, width), BF)]
    scratch += [per(width, F32), per(1, F32), per(width, F32), per(1, F32)]
    scratch += [per(ff, BF), per(3 * width, BF), per(HEADS * READ, F32)]
    scratch += [v((HEADS * READ, width), BF), v((12, width), F32), v((LAYERS, MEM, 1), F32)]
    scratch += [v((LAYERS, SMALL, width), F32)]
    sliced = 4 * width // sections + width
    scratch += [by_section(sliced), by_section(3 * width), by_section(sliced)]
    scratch += [v((lbs,) + (2,) * bits + (chunk, all_cols), BF)]
    scratch += [[v((lbs,) + (2,) * (bits - 1 - k) + (chunk, all_cols), BF) for k in range(bits)]]
    scratch += [v((LAYERS, sections) + (2,) * bits + (TILE, SMALL), F32)] * 2
    scratch += [v((LAYERS,) + (2,) * bits + (TILE, SMALL), F32)]
    scratch += [[v((LAYERS,) + (2,) * (bits - 1 - k) + (TILE, SMALL), F32) for k in range(bits)]]
    scratch += [dma((LAYERS, BLOCKS, 6)), dma((LAYERS, BLOCKS, 6)), dma((BLOCKS, 12)), dma((12,))]
    scratch += [dma((peers, 2)), dma((peers, 2)), dma((2,)), dma((peers, 2)), dma((peers, 2)), dma((2,))]
    scratch += [dma((lbs, peers, 2)), dma((lbs, peers, 2)), dma((lbs,)), dma((lbs, bits, PIECES)), dma((lbs, bits, PIECES))]
    scratch += [dma((LAYERS, peers)), dma((LAYERS, peers)), dma((LAYERS, bits)), dma((LAYERS, bits))]
    scratch += [dma((lbs, PIECES, peers)), dma((lbs, PIECES, peers)), dma((lbs, PIECES + 1))]
    return pl.pallas_call(
        functools.partial(fused_kernel, hi, lo),
        out_shape=[
            sds((count, READ, width), BF),
            sds((count, tok, width), BF),
            sds((lbs, sections, TILE, cols), BF),
            sds((lbs, chunk, width), BF),
            sds((LAYERS, TILE, SMALL), F32),
        ]
        + [sds((4 + 2 * (ff // width),) + block + (width,), BF)],
        in_specs=[pl.BlockSpec(memory_space=pltpu.SMEM)] + [vm] * 7 + [anym] * 6,
        out_specs=[vm] * 5 + [anym],
        scratch_shapes=[scratch],
        compiler_params=pltpu.CompilerParams(
            collective_id=0, has_side_effects=True, vmem_limit_bytes=64 * 2**20 - 2**16
        ),
    )(lengths, decay, *gains, *small, frames, cot, *weights)[:5]


def widen_kernel(
    rows_ref, down_ref, small_ref, res_ref, fgrad_ref,
    res_out, fgrad_out, rg_out, rw_out, na_out, qkv_out, out_out, nm_out, up_out, down_out, wg_out, ww_out,
):
    sections, tile = rows_ref.shape[1:3]
    lbs = LAYERS * BLOCKS
    res_out[...] = res_ref[...]
    fgrad_out[...] = fgrad_ref[...]
    cols = [ref.shape[-1] // sections for ref in (qkv_out, out_out, up_out)]
    for u in range(lbs):
        l, b = u // BLOCKS, u % BLOCKS
        runs = 1 << len(free_bits(u))
        run = cols[2] // runs
        for s in range(sections):
            first = 0
            for ref, c in zip((qkv_out, out_out), cols):
                ref[l, b, :, s * c:(s + 1) * c] = rows_ref[u, s, :, first:first + c].astype(F32)
                first += c
            for j in range(runs):
                start = run_start(run, u, j, {bit: (s >> i) & 1 for i, bit in enumerate(GROUP[u])})
                up_out[l, b, :, start:start + run] = rows_ref[u, s, :, first + j * run:first + (j + 1) * run].astype(F32)
        down_out[l, b] = down_ref[u].astype(F32)
    diagonal = lax.broadcasted_iota(jnp.int32, (tile, tile), 0) == lax.broadcasted_iota(jnp.int32, (tile, tile), 1)

    def as_row(l, i):
        column = jnp.broadcast_to(small_ref[l][:, READ + MEM + i:READ + MEM + i + 1], (tile, tile))
        return jnp.sum(jnp.where(diagonal, column, 0.0), axis=0, keepdims=True)

    for l in range(LAYERS):
        rw_out[l] = small_ref[l][:, :READ]
        ww_out[l] = small_ref[l][:, READ:READ + MEM]
        rg_out[l:l + 1] = as_row(l, 0)
        wg_out[l:l + 1] = as_row(l, 1 + 2 * BLOCKS)
        for b in range(BLOCKS):
            na_out[l, b:b + 1] = as_row(l, 1 + b)
            nm_out[l, b:b + 1] = as_row(l, 1 + BLOCKS + b)


def widen(rows, down, sm, res, fgrad):
    sections, tile, cols = rows.shape[1:]
    width = down.shape[-1]
    vm = pl.BlockSpec(memory_space=pltpu.VMEM)

    def f32(*shape):
        return jax.ShapeDtypeStruct((LAYERS,) + shape, F32)

    out_shape = [jax.ShapeDtypeStruct(a.shape, a.dtype) for a in (res, fgrad)] + [
        f32(tile), f32(tile, READ), f32(BLOCKS, tile), f32(BLOCKS, tile, 3 * width), f32(BLOCKS, tile, width),
        f32(BLOCKS, tile), f32(BLOCKS, tile, sections * cols - 4 * width), f32(BLOCKS, *down.shape[1:]),
        f32(tile), f32(tile, MEM),
    ]
    return pl.pallas_call(
        widen_kernel, out_shape=out_shape, in_specs=[vm] * 5, out_specs=[vm] * len(out_shape)
    )(rows, down, sm, res, fgrad)


def local(
    frames, lengths, decay, read_gain, read_weight, norm_attn, w_qkv, w_out, norm_mlp, w_up, w_down,
    write_gain, write_weight, cotangent,
):
    sections, dp = lax.axis_size("section"), lax.axis_size("dp")
    clip_dev, span, tok, width = frames.shape
    hi = width // (sections * TILE)
    lo = dp // hi
    assert clip_dev == sections and span == 1 and hi * lo == dp
    res, fgrad, rows, down, sm = run_fused(
        sections, hi, lo, lengths, decay, (read_gain, norm_attn, norm_mlp, write_gain),
        [jnp.swapaxes(w, 1, 2) for w in (read_weight, write_weight)], frames, cotangent, (w_qkv, w_out, w_up, w_down),
    )
    if lo > 1:
        groups = [[h * lo + k for k in range(lo)] for h in range(hi)]

        def over_rest(v, axis):
            return lax.psum_scatter(
                v.astype(F32), "dp", scatter_dimension=axis, axis_index_groups=groups, tiled=True
            )

        rows, down, sm = over_rest(rows, 2), over_rest(down, 1), over_rest(sm, 1)
    res, fgrad, *grads = widen(rows, down, sm, res, fgrad)
    return (res[:, None], fgrad[:, None], *grads)


def solution(mesh):
    both = ("section", "dp")
    split = P("dp", "section", None, None)
    return jax.shard_map(
        local,
        mesh=mesh,
        in_specs=(split, P("dp")) + (P(),) * 11 + (split,),
        out_specs=(
            split, split, P(None, both), P(None, both, None), P(None, None, both), P(None, None, both, None),
            P(None, None, both, None), P(None, None, both), P(None, None, both, None),
            P(None, None, both, None), P(None, both), P(None, both, None),
        ),
        check_vma=False,
    )
```

```python
import functools

import jax
import jax.numpy as jnp
from jax import lax
from jax.experimental import pallas as pl
from jax.experimental.pallas import tpu as pltpu
from jax.sharding import PartitionSpec as P

HEADS = 8
HEAD = 64
MEM = 96
READ = 16
BLOCKS = 2
LAYERS = 2
EPS = 1e-05
SMALL = 128
TILE = 16
PIECES = 3
S0, S1, D0, D1, D2 = ("section", 0), ("section", 1), ("dp", 0), ("dp", 1), ("dp", 2)
ROW_BITS = (S1, S0, D2, D1, D0)
GROUP = ((S0, D1), (S1, D2)) * LAYERS
SUM = ((D0, S1, D2), (D0, S0, D1)) * LAYERS


def free_bits(u):
    return tuple(b for b in ROW_BITS if b not in GROUP[u] and b != D0)


def run_start(bit, u, j, fixed):
    free = free_bits(u)
    value = {b: (j >> (len(free) - 1 - i)) & 1 for i, b in enumerate(free)} | fixed
    return sum(value[b] * (bit << (len(ROW_BITS) - 2 - i)) for i, b in enumerate(ROW_BITS[:-1]))
BF = jnp.bfloat16
F32 = jnp.float32


def nn(a, b):
    return lax.dot_general(a, b, (((1,), (0,)), ((), ())), preferred_element_type=F32)


def nt(a, b):
    return lax.dot_general(a, b, (((1,), (1,)), ((), ())), preferred_element_type=F32)


def tn(a, b):
    return lax.dot_general(a, b, (((0,), (0,)), ((), ())), preferred_element_type=F32)


def normalize(v):
    centred = v - jnp.mean(v, axis=-1, keepdims=True)
    spread = jnp.mean(centred * centred, axis=-1, keepdims=True)
    r = lax.rsqrt(spread + EPS)
    return centred * r, r


def centre(v):
    centred = v - jnp.mean(v, axis=-1, keepdims=True)
    return centred, lax.rsqrt(jnp.mean(centred * centred, axis=-1, keepdims=True) + EPS)


def normalize_back(dx, xh, r):
    return r * (dx - jnp.mean(dx, axis=-1, keepdims=True) - xh * jnp.mean(dx * xh, axis=-1, keepdims=True))


def gelu_and_slope(x):
    c0, c1 = 0.7978845608028654, 0.044715
    x2 = x * x
    t = jnp.tanh(c0 * x * (1.0 + c1 * x2))
    return 0.5 * x * (1.0 + t), 0.5 * (1.0 + t) + 0.5 * x * (1.0 - t * t) * c0 * (1.0 + 3.0 * c1 * x2)


def softmax_lanes(v):
    e = jnp.exp(v - jnp.max(v, axis=1, keepdims=True))
    return e / jnp.sum(e, axis=1, keepdims=True)


def softmax_lanes_back(p, dp):
    return p * (dp - jnp.sum(p * dp, axis=1, keepdims=True))


def fused_kernel(
    hi, lo, len_ref, decay_ref, rg_ref, na_ref, nm_ref, wg_ref, rw_ref, ww_ref, frames_hbm, cot_hbm,
    wqkv_hbm, wout_hbm, wup_hbm, wdown_hbm, res_out, fgrad_out, rows_ref, down_ref, small_ref,
    turn_hbm, scratch,
):
    (
        wq, wo, wu, wd, cot_v, res_v, z0, z1, xh0, xh1, rs0, rs1, at0, at1, bt0, bt1,
        mem0, mem1, dmem0, dmem1, dt_kept, ds_kept, dlw_kept, dlr_kept, dout, xa, ra, xm, rm, gp, qkv, pt, mask_ref, gains, dec_col, dsm_ref,
        slice_b, all_f, part_b, wgrad, into, small_t, small_in, small_sum, small_into,
        w_sem, x_sem, v_sem, t_sem, f_send, f_recv, f_own, o_send, o_recv, o_own,
        a_send, a_recv, a_own, c_send, c_recv, s_send, s_recv, t_send, t_recv, d_send, d_recv, d_own,
    ) = scratch
    sections, frames = all_f.shape[1:3]
    tokens0 = pl.ds(0, frames_hbm.shape[2])
    width = dsm_ref.shape[-1]
    lbs = LAYERS * BLOCKS
    me, dp_at = lax.axis_index("section"), lax.axis_index("dp")
    bits = hi.bit_length() - 1
    peers = [(me + k) % sections for k in range(1, sections)]
    members = 1 << len(GROUP[0])
    own = {S0: me % 2, S1: (me // 2) % 2} | {("dp", k): (dp_at // (lo << k)) % 2 for k in range(bits)}
    assert sections == 4 and bits == 3

    def device(flips):
        s, d = me, dp_at
        for axis, k in flips:
            step = 1 - 2 * own[axis, k]
            s, d = (s + step * (1 << k), d) if axis == "section" else (s, d + step * (lo << k))
        return {"section": s, "dp": d}

    def flips_of(u, x):
        return tuple(b for j, b in enumerate(GROUP[u]) if (x >> j) & 1)

    def member(u, x):
        return sum((1 - own[b] if (x >> j) & 1 else own[b]) * (1 << j) for j, b in enumerate(GROUP[u]))

    here = [member(u, 0) for u in range(lbs)]

    every = (slice(None),) * (bits + 1)
    ups = wd.shape[2]

    def columns(i):
        return every + (pl.ds(i * width, width),)

    def weight_copies(l, b, to, sem):
        pairs = [(wqkv_hbm.at[(l, b) + columns(i)], wq.at[to, b, i]) for i in range(3)]
        pairs += [(wout_hbm.at[l, b], wo.at[to, b]), (wup_hbm.at[l, b], wu.at[to, b]), (wdown_hbm.at[l, b], wd.at[to, b])]
        return [pltpu.make_async_copy(s, d, sem.at[l, b, i]) for i, (s, d) in enumerate(pairs)]

    def squares(l, b):
        out = [(wq.at[l, b, i],) * 2 for i in range(3)] + [(wo.at[l, b],) * 2]
        for i in range(ups):
            pair = (wu.at[(l, b) + columns(i)], wd.at[l, b, i])
            out += [pair, pair[::-1]]
        return out

    def staged(i):
        return wgrad.at[(i // 3,) + columns(i % 3)]

    def turned(ref):
        return ref[...].reshape(width, width).T.reshape(ref.shape)

    def kept_copies():
        return [pltpu.make_async_copy(staged(i), turn_hbm.at[i], t_sem.at[i]) for i in range(4 + 2 * ups)]

    def transpose_block(b, carry):
        copies = kept_copies()
        for i, (s, _) in enumerate(squares(1, b)):
            pl.when(b > 0)(copies[i].wait)
            staged(i)[...] = turned(s)
            pl.when(b == 0)(copies[i].start)
        return carry

    def transposed_copies():
        out = []
        for b in range(BLOCKS):
            for i, (_, d) in enumerate(squares(0, b)):
                out.append(pltpu.make_async_copy(turn_hbm.at[i] if b == 0 else staged(i), d, v_sem.at[b, i]))
        return out

    def transpose_here(b, carry):
        for i, (s, d) in enumerate(squares(1, b)):
            if i < 4:
                d[...] = turned(s)
            elif i % 2 == 0:
                first, second = turned(s), turned(d)
                d[...], s[...] = first, second
        return carry

    def weight(ref, *at):
        w = ref[at]
        return w.reshape(-1, w.shape[-1])

    barrier = pltpu.get_barrier_semaphore()
    partners = {(S0,), (S1,), (S0, S1)} | {(b,) for bits_of in SUM for b in bits_of}
    partners |= {tuple(sorted(flips_of(u, x))) for u in range(lbs) for x in range(1, members)}
    partners = sorted({tuple(sorted(p)) for p in partners})
    for p in partners:
        pl.semaphore_signal(barrier, inc=1, device_id=device(p), device_id_type=pl.DeviceIdType.MESH)

    def remote(src, dst, send, recv, to):
        return pltpu.make_async_remote_copy(
            src_ref=src, dst_ref=dst, send_sem=send, recv_sem=recv, device_id=to, device_id_type=pl.DeviceIdType.MESH
        )

    def forward_copies(u, first, count):
        at = all_f.at[u, here[u], pl.ds(first, count)]
        return [
            remote(at, at, a_send.at[u, x - 1, 0], a_recv.at[u, x - 1, 0], device(flips_of(u, x)))
            for x in range(1, members)
        ]

    def backward_copies(u, first, count):
        at = pl.ds(first, count)
        return [
            remote(
                slice_b.at[u, member(u, x), at], part_b.at[u, here[u], at],
                a_send.at[u, x - 1, 1], a_recv.at[u, x - 1, 1], device(flips_of(u, x)),
            )
            for x in range(1, members)
        ]

    def own_backward(u, first, count):
        at = pl.ds(first, count)
        return pltpu.make_async_copy(slice_b.at[u, here[u], at], part_b.at[u, here[u], at], a_own.at[u])

    def start_forward(u, f):
        for c in forward_copies(u, f, 1):
            c.start()

    def start_backward(u, f):
        for c in backward_copies(u, f, 1) + [own_backward(u, f, 1)]:
            c.start()

    def wait_factors(u):
        own_backward(u, 0, frames).wait()
        for c in forward_copies(u, 0, frames) + backward_copies(u, 0, frames):
            c.wait_recv()

    def place(u, s, h):
        value = {("section", k): (s >> k) & 1 for k in range(2)} | {("dp", k): (h >> k) & 1 for k in range(bits)}
        return tuple(value[b] for b in reversed(SUM[u])), sum(value[b] << j for j, b in enumerate(GROUP[u]))

    def start_small(l):
        rows = jnp.transpose(dsm_ref[l]).reshape(sections, hi, TILE, SMALL)
        for s in range(sections):
            for h in range(hi):
                at, g = place(l * BLOCKS, s, h)
                small_t[(l, g) + at] = rows[s, h]
        for c in small_copies(l):
            c.start()

    def small_copies(l):
        u = l * BLOCKS
        return [
            remote(
                small_t.at[l, member(u, x)], small_in.at[l, here[u]],
                s_send.at[l, x - 1], s_recv.at[l, x - 1], device(flips_of(u, x)),
            )
            for x in range(1, members)
        ]

    def halves(u, k, other):
        b = own[SUM[u][k]]
        fixed = tuple(own[SUM[u][j]] for j in range(k - 1, -1, -1))
        return (slice(None),) * (bits - 1 - k) + ((1 - b) if other else b,) + fixed

    def own_at(u):
        return tuple(own[b] for b in reversed(SUM[u]))

    def piece(p):
        size = wgrad.shape[-1] // PIECES
        return (slice(None), pl.ds(p * size, size))

    def halving_copy(u, k, p):
        return remote(
            wgrad.at[(u,) + halves(u, k, True) + piece(p)],
            into[k].at[(u,) + (slice(None),) * (bits - 1 - k) + piece(p)],
            c_send.at[u, k, p], c_recv.at[u, k, p], device((SUM[u][k],)),
        )

    def small_halving_copy(l, k):
        u = l * BLOCKS
        return remote(
            small_sum.at[(l,) + halves(u, k, True)], small_into[k].at[l], t_send.at[l, k], t_recv.at[l, k],
            device((SUM[u][k],)),
        )

    cols = wgrad.shape[-1] - width

    def final_columns(p):
        size = wgrad.shape[-1] // PIECES
        return pl.ds(p * size, min(size, cols - p * size))

    def own_rows(u, g, p):
        return wgrad.at[(u,) + own_at(u) + (pl.ds(pl.multiple_of(g * TILE, TILE), TILE), final_columns(p))]

    def row_copies(u, p):
        if p * (wgrad.shape[-1] // PIECES) >= cols:
            return []
        dst = rows_ref.at[u, here[u], :, final_columns(p)]
        return [
            remote(
                own_rows(u, member(u, x), p), dst, d_send.at[u, p, x - 1], d_recv.at[u, p, x - 1], device(flips_of(u, x))
            )
            for x in range(1, members)
        ] + [pltpu.make_async_copy(own_rows(u, here[u], p), dst, d_own.at[u, p])]

    def down_copy(u):
        down = wgrad.at[(u,) + own_at(u) + (slice(None), pl.ds(cols, width))]
        return pltpu.make_async_copy(down, down_ref.at[u], d_own.at[u, PIECES])

    def store_rows(u, first, v):
        c = v.shape[1]
        v = v.astype(BF).reshape(sections, hi, TILE, c)
        for s in range(sections):
            for h in range(hi):
                at, g = place(u, s, h)
                wgrad[(u,) + at + (slice(g * TILE, (g + 1) * TILE), slice(first, first + c))] = v[s, h]

    def store_down(u, first, v):
        c = v.shape[1]
        order = free_bits(u) + (D0,)
        v = v.astype(BF).reshape(1 << len(order), members * TILE, c)
        for j in range(1 << len(order)):
            value = {b: (j >> (len(order) - 1 - i)) & 1 for i, b in enumerate(order)}
            at = tuple(value[b] for b in reversed(SUM[u]))
            wgrad[(u,) + at + (slice(None), slice(first, first + c))] = v[j]

    def form(u):
        l, b = u // BLOCKS, u % BLOCKS
        q, o = 3 * width // members, 4 * width // members
        runs = 1 << len(free_bits(u))
        run = wu.shape[-1] // (members * runs)
        fixed = {bit: own[bit] for bit in GROUP[u]}

        def flat(ref, first, count):
            v = ref[u, :, :, :, first:first + count]
            return v.reshape(members * frames * READ, count)

        def up_run(j):
            at = {bit: (j >> (len(free_bits(u)) - 1 - i)) & 1 for i, bit in enumerate(free_bits(u))} | fixed
            w = wd[1 - l, b, 2 * at[S1] + at[S0], at[D2], at[D1]]
            return w.reshape(-1, w.shape[-1])

        def down_run(j):
            start = pl.multiple_of(run_start(run, u, j, fixed), run)
            return weight(wu, 1 - l, b, *every, pl.ds(start, run))

        u_all, dh_all = flat(all_f, 2 * width, width), flat(part_b, o, width)
        up_rows = jnp.concatenate([up_run(j) for j in range(runs)], axis=0)
        down_cols = jnp.concatenate([down_run(j) for j in range(runs)], axis=1)
        lift, slope = gelu_and_slope(nt(u_all, up_rows))
        dup = (nn(dh_all, down_cols) * slope).astype(BF)
        store_rows(u, 0, tn(flat(all_f, 0, width), flat(part_b, 0, q)))
        store_rows(u, q, tn(flat(all_f, width, width), flat(part_b, q, o - q)))
        store_rows(u, o, tn(u_all, dup))
        store_down(u, cols, tn(lift.astype(BF), dh_all))
        for p in range(PIECES):
            halving_copy(u, 0, p).start()

    def halve_small(l, k):
        if k < 0:
            for c in small_copies(l):
                c.wait_recv()
            total = small_t[l, here[l * BLOCKS]]
            for x in range(1, members):
                total = total + small_in[l, member(l * BLOCKS, x)]
            small_sum[l] = total
        else:
            small_halving_copy(l, k).wait_recv()
            at = (l,) + halves(l * BLOCKS, k, False)
            small_sum[at] = small_sum[at] + small_into[k][l]
        if k + 1 < bits:
            small_halving_copy(l, k + 1).start()
        else:
            small_ref[l] = small_sum[(l,) + own_at(l * BLOCKS)]

    def halve(u, k, p):
        halving_copy(u, k, p).wait_recv()
        at = (u,) + halves(u, k, False) + piece(p)
        wgrad[at] = wgrad[at] + into[k][(u,) + (slice(None),) * (bits - 1 - k) + piece(p)]
        if k + 1 < bits:
            halving_copy(u, k + 1, p).start()
        elif u != lbs - 1:
            send_rows(u, p)

    def send_rows(u, p):
        for c in row_copies(u, p):
            c.start()
        if p + 1 == PIECES:
            down_copy(u).start()

    def finish(u):
        for p in range(PIECES):
            for c in row_copies(u, p):
                c.wait()
        down_copy(u).wait()
        for k in range(bits):
            for p in range(PIECES):
                halving_copy(u, k, p).wait_send()
        for c in forward_copies(u, 0, frames) + backward_copies(u, 0, frames):
            c.wait_send()
        if u % BLOCKS == 0:
            l = u // BLOCKS
            for c in small_copies(l):
                c.wait_send()
            for k in range(bits):
                small_halving_copy(l, k).wait_send()

    def frame_copies():
        return [
            remote(src.at[p, 0], dst, f_send.at[k, i], f_recv.at[k, i], {"section": p})
            for k, p in enumerate(peers)
            for i, (src, dst) in enumerate(((frames_hbm, z0.at[me, tokens0]), (cot_hbm, cot_v.at[me])))
        ]

    def own_frames():
        return [
            pltpu.make_async_copy(src.at[me, 0], dst, f_own.at[i])
            for i, (src, dst) in enumerate(((frames_hbm, z0.at[me, tokens0]), (cot_hbm, cot_v.at[me])))
        ]

    def output_copies(i, src, dst):
        copies = [
            remote(src(p), dst.at[me], o_send.at[k, i], o_recv.at[k, i], {"section": p}) for k, p in enumerate(peers)
        ]
        return copies, pltpu.make_async_copy(src(me), dst.at[me], o_own.at[i])

    results = (0, lambda f: res_v.at[f], res_out)
    frame_grads = (1, lambda f: z0.at[f, tokens0], fgrad_out)

    def start_output(i, src, dst):
        copies, own = output_copies(i, src, dst)
        for c in copies + [own]:
            c.start()

    def spread_heads(v):
        return jnp.concatenate([v] * HEADS, axis=0) * mask_ref[...]

    def gather_heads(v):
        return jnp.sum((v * mask_ref[...].astype(F32)).reshape(HEADS, READ, width), axis=0)

    def live_at(f):
        return jnp.where(f < len_ref[me], 1.0, 0.0).astype(F32)

    def keep_slices(lb, f, first, v):
        c = v.shape[1] // members
        for s in range(members):
            slice_b[lb, s, f, :, first:first + c] = v[:, s * c:(s + 1) * c]

    def add_gain_grad(l, i, v):
        dsm_ref[l, READ + MEM + i:READ + MEM + i + 1, :] += jnp.sum(v, axis=0, keepdims=True)

    def gain(i):
        return gains[i:i + 1, :]

    def block_forward(lb, f, h):
        centred, r = centre(h)
        xh = centred * r
        xa[lb, f], ra[lb, f] = xh, r
        g = (xh * gain(2 + lb)).astype(BF)
        wide = (centred * gain(2 + lb)).astype(BF)
        all_f[lb, here[lb], f, :, :width] = g
        l, b = lb // BLOCKS, lb % BLOCKS
        q, k, v = ((nn(wide, weight(wq, l, b, i)) * r).astype(BF) for i in range(3))
        yield
        for i, part in enumerate((q, k, v)):
            qkv[lb, f, :, i * width:(i + 1) * width] = part
        s = nt(k, spread_heads(q)) * HEAD ** (-0.5)
        yield
        e = jnp.exp(s - jnp.max(s, axis=0, keepdims=True))
        p = e / jnp.sum(e, axis=0, keepdims=True)
        pt[lb, f] = p
        o = tn(p.astype(BF), v)
        yield
        o = gather_heads(o).astype(BF)
        all_f[lb, here[lb], f, :, width:2 * width] = o
        h = h + nn(o, weight(wo, l, b))
        yield
        centred, r = centre(h)
        xh = centred * r
        xm[lb, f], rm[lb, f] = xh, r
        u = (xh * gain(6 + lb)).astype(BF)
        wide = (centred * gain(6 + lb)).astype(BF)
        all_f[lb, here[lb], f, :, 2 * width:] = u
        x = nn(wide, weight(wu, l, b)) * r
        yield
        lift, slope = gelu_and_slope(x)
        lift, gp[lb, f] = lift.astype(BF), slope.astype(BF)
        h = h + nn(lift, weight(wd, l, b))
        yield
        return h

    def block_backward(lb, f, dh):
        l, b = lb // BLOCKS, lb % BLOCKS
        dhb = dh.astype(BF)
        for s in range(members):
            slice_b[lb, s, f, :, 4 * width // members:] = dhb
        dup = nn(dhb, weight(wu, 1 - l, b))
        yield
        dup = (dup * gp[lb, f].astype(F32)).astype(BF)
        du = nn(dup, weight(wd, 1 - l, b))
        yield
        xh = xm[lb, f]
        add_gain_grad(lb // BLOCKS, 3 + lb % BLOCKS, du * xh)
        dh = dh + normalize_back(du * gain(6 + lb), xh, rm[lb, f])
        dhb = dh.astype(BF)
        keep_slices(lb, f, 3 * width // members, dhb)
        do = nn(dhb, weight(wo, 1 - l, b))
        yield
        do = spread_heads(do.astype(BF))
        joined = qkv[lb, f]
        q, k, v = joined[:, :width], joined[:, width:2 * width], joined[:, 2 * width:]
        p = pt[lb, f]
        dp = nt(v, do)
        yield
        ds = (p * (dp - jnp.sum(p * dp, axis=0, keepdims=True)) * HEAD ** (-0.5)).astype(BF)
        dv = nn(p.astype(BF), do)
        dk = nn(ds, spread_heads(q))
        dq = tn(ds, k)
        yield
        dq = gather_heads(dq)
        dj = [d.astype(BF) for d in (dq, dk, dv)]
        keep_slices(lb, f, 0, jnp.concatenate(dj, axis=1))
        dg = sum(nn(d, weight(wq, 1 - l, b, i)) for i, d in enumerate(dj))
        yield
        xh = xa[lb, f]
        add_gain_grad(lb // BLOCKS, 1 + lb % BLOCKS, dg * xh)
        return dh + normalize_back(dg * gain(2 + lb), xh, ra[lb, f])

    def layer_forward(l, f, z, xh_ref, rs_ref, at, bt, mem, read_inputs, store):
        live = live_at(f)
        inputs = read_inputs(f)
        m = mem[...]
        rows = z.shape[1] - READ
        n_in = rows - MEM
        if inputs is not None:
            z[f, :n_in] = inputs
        z[f, n_in:rows] = m.astype(BF)
        zz = z[f, :rows]
        xh, r = normalize(zz.astype(F32))
        xh_ref[f, :rows], rs_ref[f, :rows] = xh, r
        n = (xh * gain(l)).astype(BF)
        logits = nt(rw_ref[l], n)
        yield
        a = softmax_lanes(logits)
        at[f] = a
        h = nn(a.astype(BF), zz)
        yield
        for b in range(BLOCKS):
            h = yield from block_forward(l * BLOCKS + b, f, h)
        y = h.astype(BF)
        z[f, rows:] = y
        xh, r = normalize(y.astype(F32))
        xh_ref[f, rows:], rs_ref[f, rows:] = xh, r
        n = (xh_ref[f] * gain(10 + l)).astype(BF)
        logits = nt(ww_ref[l], n)
        yield
        b = softmax_lanes(logits)
        bt[f] = b
        written = nn(b.astype(BF), z[f])
        yield
        rate = dec_col[l]
        updated = rate * z[f, n_in:rows].astype(F32) + (1.0 - rate) * written
        mem[...] = live * updated + (1.0 - live) * m
        store(f, (live * y.astype(F32)).astype(BF))

    def layer_backward(l, f, z, xh_ref, rs_ref, at, bt, dmem, read_grad, store, middle=None):
        live = live_at(f)
        rows = z.shape[1] - READ
        n_in = rows - MEM
        later = n_in if l == 0 else 0
        dm = dmem[...]
        rate = dec_col[l]
        dt = ((live * (1.0 - rate)) * dm).astype(BF)
        zf = z[f]
        b = bt[f]
        dl = nt(dt, zf)
        yield
        dl = softmax_lanes_back(b, dl).astype(BF)
        dz = tn(b[:, later:].astype(BF), dt)
        dn = tn(dl[:, later:], ww_ref[l])
        yield
        xh = xh_ref[f, later:]
        if l == 0:
            dt_kept[f], dlw_kept[f] = dt, dl
        else:
            dsm_ref[l, READ:READ + MEM] += nn(dl, (xh * gain(10 + l)).astype(BF))
        add_gain_grad(l, 5, dn * xh)
        dx = dn * gain(10 + l)
        tail = rows - later
        dy = dz[tail:] + normalize_back(dx[tail:], xh[tail:], rs_ref[f, rows:]) + live * read_grad(f)
        dh = dy.astype(BF).astype(F32)
        for bb in range(BLOCKS - 1, -1, -1):
            dh = yield from block_backward(l * BLOCKS + bb, f, dh)
            if bb and middle is not None:
                middle()
        ds = dh.astype(BF)
        xh = xh[:tail]
        a = at[f]
        dl = nt(ds, zf[:rows])
        yield
        dl = softmax_lanes_back(a, dl).astype(BF)
        dz = dz[:tail] + tn(a[:, later:].astype(BF), ds)
        dn = tn(dl[:, later:], rw_ref[l])
        yield
        if l == 0:
            ds_kept[f], dlr_kept[f] = ds, dl
        else:
            dsm_ref[l, :READ] += nn(dl, (xh * gain(l)).astype(BF))
        add_gain_grad(l, 0, dn * xh)
        dz = dz + normalize_back(dx[:tail] + dn * gain(l), xh, rs_ref[f, later:rows])
        dmq = (dz[n_in - later:] + (live * rate) * dm).astype(BF).astype(F32)
        dmem[...] = dmq + (1.0 - live) * dm
        store(f, dz[:n_in].astype(BF))

    def frame_backward(f):
        rows = z0.shape[1] - READ
        n_in = rows - MEM
        dlw, dlr = dlw_kept[f], dlr_kept[f]
        xh = xh0[f]
        dsm_ref[0, READ:READ + MEM] += nn(dlw, (xh * gain(10)).astype(BF))
        dsm_ref[0, :READ] += nn(dlr, (xh[:rows] * gain(0)).astype(BF))
        xh = xh[:n_in]
        dz = tn(bt0[f][:, :n_in].astype(BF), dt_kept[f]) + tn(at0[f][:, :n_in].astype(BF), ds_kept[f])
        dnw, dnr = tn(dlw[:, :n_in], ww_ref[0]), tn(dlr[:, :n_in], rw_ref[0])
        add_gain_grad(0, 5, dnw * xh)
        add_gain_grad(0, 0, dnr * xh)
        z0[f, tokens0] = (dz + normalize_back(dnw * gain(10) + dnr * gain(0), xh, rs0[f, :n_in])).astype(BF)

    for c in own_frames():
        c.start()
    loads = [[c for b in range(BLOCKS) for c in weight_copies(l, b, l, w_sem)] for l in range(LAYERS)]
    for c in loads[1] + loads[0]:
        c.start()
    row = lax.broadcasted_iota(jnp.int32, (HEADS * READ, width), 0) // READ
    col = lax.broadcasted_iota(jnp.int32, (HEADS * READ, width), 1) // HEAD
    mask_ref[...] = jnp.where(row == col, 1.0, 0.0).astype(BF)
    dsm_ref[...] = jnp.zeros_like(dsm_ref)
    for l in range(LAYERS):
        gains[l:l + 1] = rg_ref[...].astype(F32)[l:l + 1]
        gains[10 + l:11 + l] = wg_ref[...].astype(F32)[l:l + 1]
        for b in range(BLOCKS):
            lb = l * BLOCKS + b
            gains[2 + lb:3 + lb] = na_ref[l].astype(F32)[b:b + 1]
            gains[6 + lb:7 + lb] = nm_ref[l].astype(F32)[b:b + 1]
        spread = jnp.broadcast_to(decay_ref[l:l + 1], (MEM, MEM))
        diagonal = lax.broadcasted_iota(jnp.int32, (MEM, MEM), 0) == lax.broadcasted_iota(jnp.int32, (MEM, MEM), 1)
        dec_col[l] = jnp.sum(jnp.where(diagonal, spread, 0.0), axis=1, keepdims=True)

    pl.semaphore_wait(barrier, len(partners))
    for c in frame_copies():
        c.start()

    def together(*chains):
        chains = list(chains)
        while chains:
            for c in list(chains):
                try:
                    next(c)
                except StopIteration:
                    chains.remove(c)

    def keep(ref):
        def store(f, v):
            ref[f] = v

        return store

    kept0 = (z0, xh0, rs0, at0, bt0)
    kept1 = (z1, xh1, rs1, at1, bt1)

    for c in loads[1]:
        c.wait()
    lax.fori_loop(0, BLOCKS, transpose_block, 0)
    for c in loads[0]:
        c.wait()
    for c in own_frames():
        c.wait()
    for c in frame_copies():
        c.wait_recv()
    mem0[...] = jnp.zeros_like(mem0)
    mem1[...] = jnp.zeros_like(mem1)

    def chain0(f):
        return layer_forward(0, f, *kept0, mem0, lambda f: None, keep(dout))

    def chain1(f):
        return layer_forward(1, f, *kept1, mem1, lambda f: dout[f], keep(res_v))

    def send_forward(l, f):
        for b in range(BLOCKS):
            start_forward(l * BLOCKS + b, f)

    def forward(f, carry):
        together(chain0(f), chain1(f - 1))
        send_forward(0, f)
        send_forward(1, f - 1)
        return carry

    together(chain0(0))
    send_forward(0, 0)
    lax.fori_loop(1, frames, forward, 0)
    for c in transposed_copies():
        c.start()
    together(chain1(frames - 1))
    send_forward(1, frames - 1)
    again = [c for b in range(BLOCKS) for c in weight_copies(0, b, 1, x_sem)]
    for c in again:
        c.start()
    for c in transposed_copies():
        c.wait()
    start_output(*results)
    dmem0[...] = jnp.zeros_like(dmem0)
    dmem1[...] = jnp.zeros_like(dmem1)

    def back0(f, middle=None):
        return layer_backward(0, f, *kept0, dmem0, lambda f: dout[f].astype(F32), lambda f, v: None, middle)

    def back1(f):
        return layer_backward(1, f, *kept1, dmem1, lambda f: cot_v[f].astype(F32), keep(dout))

    def send_backward(l, f):
        for b in range(BLOCKS - 1, -1, -1):
            start_backward(l * BLOCKS + b, f)

    def backward(i, carry):
        f = frames - 1 - i
        together(back1(f), back0(f + 1))
        send_backward(1, f)
        send_backward(0, f + 1)
        return carry

    together(back1(frames - 1))
    send_backward(1, frames - 1)
    for c in again:
        c.wait()
    lax.fori_loop(0, BLOCKS, transpose_here, 0)
    lax.fori_loop(1, frames, backward, 0)
    start_small(1)
    together(back0(0, lambda: start_backward(1, 0)))
    start_backward(0, 0)
    for u in (3, 2):
        wait_factors(u)
        form(u)
    halve_small(1, -1)
    for f in range(frames):
        frame_backward(f)
    start_small(0)
    halve_small(1, 0)
    for u in (3, 2):
        for p in range(PIECES):
            halve(u, 0, p)
    for u in (1, 0):
        wait_factors(u)
        form(u)
    halve_small(0, -1)
    for p in range(PIECES):
        halve(1, 0, p)
    halve_small(0, 0)
    for p in range(PIECES):
        halve(0, 0, p)
    start_output(*frame_grads)
    halve_small(1, 1)
    halve(3, 1, 0)
    halve(2, 1, 0)
    halve(3, 1, 1)
    halve(2, 1, 1)
    halve(3, 2, 0)
    halve(2, 2, 0)
    halve(3, 1, 2)
    halve(2, 1, 2)
    halve_small(0, 1)
    halve(3, 2, 1)
    halve(2, 2, 1)
    halve_small(1, 2)
    halve(1, 1, 0)
    halve(0, 1, 0)
    halve(3, 2, 2)
    halve(2, 2, 2)
    halve(1, 1, 1)
    halve(0, 1, 1)
    halve(1, 2, 0)
    halve(0, 2, 0)
    halve(1, 1, 2)
    halve(0, 1, 2)
    for p in range(PIECES):
        send_rows(lbs - 1, p)
    halve(1, 2, 1)
    halve(0, 2, 1)
    halve_small(0, 2)
    halve(1, 2, 2)
    halve(0, 2, 2)
    for u in range(lbs - 1, -1, -1):
        finish(u)
    for out in (results, frame_grads):
        copies, own = output_copies(*out)
        for c in copies + [own]:
            c.wait()
    for c in frame_copies():
        c.wait_send()


def run_fused(sections, hi, lo, lengths, decay, gains, small, frames, cot, weights):
    count, _, tok, width = frames.shape
    lbs = LAYERS * BLOCKS
    ff = weights[2].shape[-1]
    cols = (4 * width + ff) // sections
    all_cols = cols + width
    bits = hi.bit_length() - 1
    chunk = sections * TILE
    peers = sections - 1
    vm, anym = pl.BlockSpec(memory_space=pltpu.VMEM), pl.BlockSpec(memory_space=pl.ANY)
    v, dma = pltpu.VMEM, pltpu.SemaphoreType.DMA

    def sds(shape, dtype):
        return jax.ShapeDtypeStruct(shape, dtype)

    def per(c, dtype):
        return v((lbs, count, READ, c), dtype)

    def by_section(c):
        return v((lbs, sections, count, READ, c), BF)

    rows0, rows1 = tok + MEM, READ + MEM
    lead, block = (LAYERS, BLOCKS), (2,) * bits + (width // hi,)
    transposed = [lead + (3,) + block + (width,), lead + block + (width,), lead + block + (ff,), lead + (ff // width,) + block + (width,)]
    weights = [weights[0].reshape(lead + block + (3 * width,))] + [w.reshape(s) for w, s in zip(weights[1:], transposed[1:])]
    scratch = [v(s, BF) for s in transposed]
    scratch += [v((count, READ, width), BF), v((count, READ, width), BF)]
    scratch += [v((count, r + READ, width), BF) for r in (rows0, rows1)]
    scratch += [v((count, r + READ, width), F32) for r in (rows0, rows1)]
    scratch += [v((count, r + READ, 1), F32) for r in (rows0, rows1)]
    scratch += [v((count, READ, r), F32) for r in (rows0, rows1)]
    scratch += [v((count, MEM, r + READ), F32) for r in (rows0, rows1)]
    scratch += [v((MEM, width), F32)] * 4
    scratch += [v((count, MEM, width), BF), v((count, READ, width), BF)]
    scratch += [v((count, MEM, rows0 + READ), BF), v((count, READ, rows0), BF), v((count, READ, width), BF)]
    scratch += [per(width, F32), per(1, F32), per(width, F32), per(1, F32)]
    scratch += [per(ff, BF), per(3 * width, BF), per(HEADS * READ, F32)]
    scratch += [v((HEADS * READ, width), BF), v((12, width), F32), v((LAYERS, MEM, 1), F32)]
    scratch += [v((LAYERS, SMALL, width), F32)]
    sliced = 4 * width // sections + width
    scratch += [by_section(sliced), by_section(3 * width), by_section(sliced)]
    scratch += [v((lbs,) + (2,) * bits + (chunk, all_cols), BF)]
    scratch += [[v((lbs,) + (2,) * (bits - 1 - k) + (chunk, all_cols), BF) for k in range(bits)]]
    scratch += [v((LAYERS, sections) + (2,) * bits + (TILE, SMALL), F32)] * 2
    scratch += [v((LAYERS,) + (2,) * bits + (TILE, SMALL), F32)]
    scratch += [[v((LAYERS,) + (2,) * (bits - 1 - k) + (TILE, SMALL), F32) for k in range(bits)]]
    scratch += [dma((LAYERS, BLOCKS, 6)), dma((LAYERS, BLOCKS, 6)), dma((BLOCKS, 12)), dma((12,))]
    scratch += [dma((peers, 2)), dma((peers, 2)), dma((2,)), dma((peers, 2)), dma((peers, 2)), dma((2,))]
    scratch += [dma((lbs, peers, 2)), dma((lbs, peers, 2)), dma((lbs,)), dma((lbs, bits, PIECES)), dma((lbs, bits, PIECES))]
    scratch += [dma((LAYERS, peers)), dma((LAYERS, peers)), dma((LAYERS, bits)), dma((LAYERS, bits))]
    scratch += [dma((lbs, PIECES, peers)), dma((lbs, PIECES, peers)), dma((lbs, PIECES + 1))]
    return pl.pallas_call(
        functools.partial(fused_kernel, hi, lo),
        out_shape=[
            sds((count, READ, width), BF),
            sds((count, tok, width), BF),
            sds((lbs, sections, TILE, cols), BF),
            sds((lbs, chunk, width), BF),
            sds((LAYERS, TILE, SMALL), F32),
        ]
        + [sds((4 + 2 * (ff // width),) + block + (width,), BF)],
        in_specs=[pl.BlockSpec(memory_space=pltpu.SMEM)] + [vm] * 7 + [anym] * 6,
        out_specs=[vm] * 5 + [anym],
        scratch_shapes=[scratch],
        compiler_params=pltpu.CompilerParams(
            collective_id=0, has_side_effects=True, vmem_limit_bytes=64 * 2**20 - 2**16
        ),
    )(lengths, decay, *gains, *small, frames, cot, *weights)[:5]


def widen_kernel(
    rows_ref, down_ref, small_ref, res_ref, fgrad_ref,
    res_out, fgrad_out, rg_out, rw_out, na_out, qkv_out, out_out, nm_out, up_out, down_out, wg_out, ww_out,
):
    sections, tile = rows_ref.shape[1:3]
    lbs = LAYERS * BLOCKS
    res_out[...] = res_ref[...]
    fgrad_out[...] = fgrad_ref[...]
    cols = [ref.shape[-1] // sections for ref in (qkv_out, out_out, up_out)]
    for u in range(lbs):
        l, b = u // BLOCKS, u % BLOCKS
        runs = 1 << len(free_bits(u))
        run = cols[2] // runs
        for s in range(sections):
            first = 0
            for ref, c in zip((qkv_out, out_out), cols):
                ref[l, b, :, s * c:(s + 1) * c] = rows_ref[u, s, :, first:first + c].astype(F32)
                first += c
            for j in range(runs):
                start = run_start(run, u, j, {bit: (s >> i) & 1 for i, bit in enumerate(GROUP[u])})
                up_out[l, b, :, start:start + run] = rows_ref[u, s, :, first + j * run:first + (j + 1) * run].astype(F32)
        down_out[l, b] = down_ref[u].astype(F32)
    diagonal = lax.broadcasted_iota(jnp.int32, (tile, tile), 0) == lax.broadcasted_iota(jnp.int32, (tile, tile), 1)

    def as_row(l, i):
        column = jnp.broadcast_to(small_ref[l][:, READ + MEM + i:READ + MEM + i + 1], (tile, tile))
        return jnp.sum(jnp.where(diagonal, column, 0.0), axis=0, keepdims=True)

    for l in range(LAYERS):
        rw_out[l] = small_ref[l][:, :READ]
        ww_out[l] = small_ref[l][:, READ:READ + MEM]
        rg_out[l:l + 1] = as_row(l, 0)
        wg_out[l:l + 1] = as_row(l, 1 + 2 * BLOCKS)
        for b in range(BLOCKS):
            na_out[l, b:b + 1] = as_row(l, 1 + b)
            nm_out[l, b:b + 1] = as_row(l, 1 + BLOCKS + b)


def widen(rows, down, sm, res, fgrad):
    sections, tile, cols = rows.shape[1:]
    width = down.shape[-1]
    vm = pl.BlockSpec(memory_space=pltpu.VMEM)

    def f32(*shape):
        return jax.ShapeDtypeStruct((LAYERS,) + shape, F32)

    out_shape = [jax.ShapeDtypeStruct(a.shape, a.dtype) for a in (res, fgrad)] + [
        f32(tile), f32(tile, READ), f32(BLOCKS, tile), f32(BLOCKS, tile, 3 * width), f32(BLOCKS, tile, width),
        f32(BLOCKS, tile), f32(BLOCKS, tile, sections * cols - 4 * width), f32(BLOCKS, *down.shape[1:]),
        f32(tile), f32(tile, MEM),
    ]
    return pl.pallas_call(
        widen_kernel, out_shape=out_shape, in_specs=[vm] * 5, out_specs=[vm] * len(out_shape)
    )(rows, down, sm, res, fgrad)


def local(
    frames, lengths, decay, read_gain, read_weight, norm_attn, w_qkv, w_out, norm_mlp, w_up, w_down,
    write_gain, write_weight, cotangent,
):
    sections, dp = lax.axis_size("section"), lax.axis_size("dp")
    clip_dev, span, tok, width = frames.shape
    hi = width // (sections * TILE)
    lo = dp // hi
    assert clip_dev == sections and span == 1 and hi * lo == dp
    res, fgrad, rows, down, sm = run_fused(
        sections, hi, lo, lengths, decay, (read_gain, norm_attn, norm_mlp, write_gain),
        [jnp.swapaxes(w, 1, 2) for w in (read_weight, write_weight)], frames, cotangent, (w_qkv, w_out, w_up, w_down),
    )
    if lo > 1:
        groups = [[h * lo + k for k in range(lo)] for h in range(hi)]

        def over_rest(v, axis):
            return lax.psum_scatter(
                v.astype(F32), "dp", scatter_dimension=axis, axis_index_groups=groups, tiled=True
            )

        rows, down, sm = over_rest(rows, 2), over_rest(down, 1), over_rest(sm, 1)
    res, fgrad, *grads = widen(rows, down, sm, res, fgrad)
    return (res[:, None], fgrad[:, None], *grads)


def solution(mesh):
    both = ("section", "dp")
    split = P("dp", "section", None, None)
    return jax.shard_map(
        local,
        mesh=mesh,
        in_specs=(split, P("dp")) + (P(),) * 11 + (split,),
        out_specs=(
            split, split, P(None, both), P(None, both, None), P(None, None, both), P(None, None, both, None),
            P(None, None, both, None), P(None, None, both), P(None, None, both, None),
            P(None, None, both, None), P(None, both), P(None, both, None),
        ),
        check_vma=False,
    )
```

```python
import functools

import jax
import jax.numpy as jnp
from jax import lax
from jax.experimental import pallas as pl
from jax.experimental.pallas import tpu as pltpu
from jax.sharding import PartitionSpec as P

HEADS = 8
HEAD = 64
MEM = 96
READ = 16
BLOCKS = 2
LAYERS = 2
EPS = 1e-05
SMALL = 128
TILE = 16
PIECES = 3
S0, S1, D0, D1, D2 = ("section", 0), ("section", 1), ("dp", 0), ("dp", 1), ("dp", 2)
ROW_BITS = (S1, S0, D2, D1, D0)
GROUP = ((S0, D1), (S1, D2)) * LAYERS
SUM = ((D0, S1, D2), (D0, S0, D1)) * LAYERS


def free_bits(u):
    return tuple(b for b in ROW_BITS if b not in GROUP[u] and b != D0)


def run_start(bit, u, j, fixed):
    free = free_bits(u)
    value = {b: (j >> (len(free) - 1 - i)) & 1 for i, b in enumerate(free)} | fixed
    return sum(value[b] * (bit << (len(ROW_BITS) - 2 - i)) for i, b in enumerate(ROW_BITS[:-1]))
BF = jnp.bfloat16
F32 = jnp.float32


def nn(a, b):
    return lax.dot_general(a, b, (((1,), (0,)), ((), ())), preferred_element_type=F32)


def nt(a, b):
    return lax.dot_general(a, b, (((1,), (1,)), ((), ())), preferred_element_type=F32)


def tn(a, b):
    return lax.dot_general(a, b, (((0,), (0,)), ((), ())), preferred_element_type=F32)


def normalize(v):
    centred = v - jnp.mean(v, axis=-1, keepdims=True)
    spread = jnp.mean(centred * centred, axis=-1, keepdims=True)
    r = lax.rsqrt(spread + EPS)
    return centred * r, r


def centre(v):
    centred = v - jnp.mean(v, axis=-1, keepdims=True)
    return centred, lax.rsqrt(jnp.mean(centred * centred, axis=-1, keepdims=True) + EPS)


def normalize_back(dx, xh, r):
    return r * (dx - jnp.mean(dx, axis=-1, keepdims=True) - xh * jnp.mean(dx * xh, axis=-1, keepdims=True))


def gelu_and_slope(x):
    c0, c1 = 0.7978845608028654, 0.044715
    x2 = x * x
    t = jnp.tanh(c0 * x * (1.0 + c1 * x2))
    return 0.5 * x * (1.0 + t), 0.5 * (1.0 + t) + 0.5 * x * (1.0 - t * t) * c0 * (1.0 + 3.0 * c1 * x2)


def softmax_lanes(v):
    e = jnp.exp(v - jnp.max(v, axis=1, keepdims=True))
    return e / jnp.sum(e, axis=1, keepdims=True)


def softmax_lanes_back(p, dp):
    return p * (dp - jnp.sum(p * dp, axis=1, keepdims=True))


def fused_kernel(
    hi, lo, len_ref, decay_ref, rg_ref, na_ref, nm_ref, wg_ref, rw_ref, ww_ref, frames_hbm, cot_hbm,
    wqkv_hbm, wout_hbm, wup_hbm, wdown_hbm, res_out, fgrad_out, rows_ref, down_ref, small_ref,
    turn_hbm, scratch,
):
    (
        wq, wo, wu, wd, cot_v, res_v, z0, z1, xh0, xh1, rs0, rs1, at0, at1, bt0, bt1,
        mem0, mem1, dmem0, dmem1, dt_kept, ds_kept, dlw_kept, dlr_kept, dout, xa, ra, xm, rm, gp, qkv, pt, mask_ref, gains, dec_col, dsm_ref,
        slice_b, all_f, part_b, wgrad, into, small_t, small_in, small_sum, small_into,
        w_sem, x_sem, v_sem, t_sem, f_send, f_recv, f_own, o_send, o_recv, o_own,
        a_send, a_recv, a_own, c_send, c_recv, s_send, s_recv, t_send, t_recv, d_send, d_recv, d_own,
    ) = scratch
    sections, frames = all_f.shape[1:3]
    tokens0 = pl.ds(0, frames_hbm.shape[2])
    width = dsm_ref.shape[-1]
    lbs = LAYERS * BLOCKS
    me, dp_at = lax.axis_index("section"), lax.axis_index("dp")
    bits = hi.bit_length() - 1
    peers = [(me + k) % sections for k in range(1, sections)]
    members = 1 << len(GROUP[0])
    own = {S0: me % 2, S1: (me // 2) % 2} | {("dp", k): (dp_at // (lo << k)) % 2 for k in range(bits)}
    assert sections == 4 and bits == 3

    def device(flips):
        s, d = me, dp_at
        for axis, k in flips:
            step = 1 - 2 * own[axis, k]
            s, d = (s + step * (1 << k), d) if axis == "section" else (s, d + step * (lo << k))
        return {"section": s, "dp": d}

    def flips_of(u, x):
        return tuple(b for j, b in enumerate(GROUP[u]) if (x >> j) & 1)

    def member(u, x):
        return sum((1 - own[b] if (x >> j) & 1 else own[b]) * (1 << j) for j, b in enumerate(GROUP[u]))

    here = [member(u, 0) for u in range(lbs)]

    every = (slice(None),) * (bits + 1)
    ups = wd.shape[2]

    def columns(i):
        return every + (pl.ds(i * width, width),)

    def weight_copies(l, b, to, sem):
        pairs = [(wqkv_hbm.at[(l, b) + columns(i)], wq.at[to, b, i]) for i in range(3)]
        pairs += [(wout_hbm.at[l, b], wo.at[to, b]), (wup_hbm.at[l, b], wu.at[to, b]), (wdown_hbm.at[l, b], wd.at[to, b])]
        return [pltpu.make_async_copy(s, d, sem.at[l, b, i]) for i, (s, d) in enumerate(pairs)]

    def squares(l, b):
        out = [(wq.at[l, b, i],) * 2 for i in range(3)] + [(wo.at[l, b],) * 2]
        for i in range(ups):
            pair = (wu.at[(l, b) + columns(i)], wd.at[l, b, i])
            out += [pair, pair[::-1]]
        return out

    def staged(i):
        return wgrad.at[(i // 3,) + columns(i % 3)]

    def turned(ref):
        return ref[...].reshape(width, width).T.reshape(ref.shape)

    def kept_copies():
        return [pltpu.make_async_copy(staged(i), turn_hbm.at[i], t_sem.at[i]) for i in range(4 + 2 * ups)]

    def transpose_block(b, carry):
        copies = kept_copies()
        for i, (s, _) in enumerate(squares(1, b)):
            pl.when(b > 0)(copies[i].wait)
            staged(i)[...] = turned(s)
            pl.when(b == 0)(copies[i].start)
        return carry

    def transposed_copies():
        out = []
        for b in range(BLOCKS):
            for i, (_, d) in enumerate(squares(0, b)):
                out.append(pltpu.make_async_copy(turn_hbm.at[i] if b == 0 else staged(i), d, v_sem.at[b, i]))
        return out

    def transpose_here(b, carry):
        for i, (s, d) in enumerate(squares(1, b)):
            if i < 4:
                d[...] = turned(s)
            elif i % 2 == 0:
                first, second = turned(s), turned(d)
                d[...], s[...] = first, second
        return carry

    def weight(ref, *at):
        w = ref[at]
        return w.reshape(-1, w.shape[-1])

    barrier = pltpu.get_barrier_semaphore()
    partners = {(S0,), (S1,), (S0, S1)} | {(b,) for bits_of in SUM for b in bits_of}
    partners |= {tuple(sorted(flips_of(u, x))) for u in range(lbs) for x in range(1, members)}
    partners = sorted({tuple(sorted(p)) for p in partners})
    for p in partners:
        pl.semaphore_signal(barrier, inc=1, device_id=device(p), device_id_type=pl.DeviceIdType.MESH)

    def remote(src, dst, send, recv, to):
        return pltpu.make_async_remote_copy(
            src_ref=src, dst_ref=dst, send_sem=send, recv_sem=recv, device_id=to, device_id_type=pl.DeviceIdType.MESH
        )

    def forward_copies(u, first, count):
        at = all_f.at[u, here[u], pl.ds(first, count)]
        return [
            remote(at, at, a_send.at[u, x - 1, 0], a_recv.at[u, x - 1, 0], device(flips_of(u, x)))
            for x in range(1, members)
        ]

    def backward_copies(u, first, count):
        at = pl.ds(first, count)
        return [
            remote(
                slice_b.at[u, member(u, x), at], part_b.at[u, here[u], at],
                a_send.at[u, x - 1, 1], a_recv.at[u, x - 1, 1], device(flips_of(u, x)),
            )
            for x in range(1, members)
        ]

    def own_backward(u, first, count):
        at = pl.ds(first, count)
        return pltpu.make_async_copy(slice_b.at[u, here[u], at], part_b.at[u, here[u], at], a_own.at[u])

    def start_forward(u, f):
        for c in forward_copies(u, f, 1):
            c.start()

    def start_backward(u, f):
        for c in backward_copies(u, f, 1) + [own_backward(u, f, 1)]:
            c.start()

    def wait_factors(u):
        own_backward(u, 0, frames).wait()
        for c in forward_copies(u, 0, frames) + backward_copies(u, 0, frames):
            c.wait_recv()

    def place(u, s, h):
        value = {("section", k): (s >> k) & 1 for k in range(2)} | {("dp", k): (h >> k) & 1 for k in range(bits)}
        return tuple(value[b] for b in reversed(SUM[u])), sum(value[b] << j for j, b in enumerate(GROUP[u]))

    def start_small(l):
        rows = jnp.transpose(dsm_ref[l]).reshape(sections, hi, TILE, SMALL)
        for s in range(sections):
            for h in range(hi):
                at, g = place(l * BLOCKS, s, h)
                small_t[(l, g) + at] = rows[s, h]
        for c in small_copies(l):
            c.start()

    def small_copies(l):
        u = l * BLOCKS
        return [
            remote(
                small_t.at[l, member(u, x)], small_in.at[l, here[u]],
                s_send.at[l, x - 1], s_recv.at[l, x - 1], device(flips_of(u, x)),
            )
            for x in range(1, members)
        ]

    def halves(u, k, other):
        b = own[SUM[u][k]]
        fixed = tuple(own[SUM[u][j]] for j in range(k - 1, -1, -1))
        return (slice(None),) * (bits - 1 - k) + ((1 - b) if other else b,) + fixed

    def own_at(u):
        return tuple(own[b] for b in reversed(SUM[u]))

    def piece(p):
        size = wgrad.shape[-1] // PIECES
        return (slice(None), pl.ds(p * size, size))

    def halving_copy(u, k, p):
        return remote(
            wgrad.at[(u,) + halves(u, k, True) + piece(p)],
            into[k].at[(u,) + (slice(None),) * (bits - 1 - k) + piece(p)],
            c_send.at[u, k, p], c_recv.at[u, k, p], device((SUM[u][k],)),
        )

    def small_halving_copy(l, k):
        u = l * BLOCKS
        return remote(
            small_sum.at[(l,) + halves(u, k, True)], small_into[k].at[l], t_send.at[l, k], t_recv.at[l, k],
            device((SUM[u][k],)),
        )

    cols = wgrad.shape[-1] - width

    def final_columns(p):
        size = wgrad.shape[-1] // PIECES
        return pl.ds(p * size, min(size, cols - p * size))

    def own_rows(u, g, p):
        return wgrad.at[(u,) + own_at(u) + (pl.ds(pl.multiple_of(g * TILE, TILE), TILE), final_columns(p))]

    def row_copies(u, p):
        if p * (wgrad.shape[-1] // PIECES) >= cols:
            return []
        dst = rows_ref.at[u, here[u], :, final_columns(p)]
        return [
            remote(
                own_rows(u, member(u, x), p), dst, d_send.at[u, p, x - 1], d_recv.at[u, p, x - 1], device(flips_of(u, x))
            )
            for x in range(1, members)
        ] + [pltpu.make_async_copy(own_rows(u, here[u], p), dst, d_own.at[u, p])]

    def down_copy(u):
        down = wgrad.at[(u,) + own_at(u) + (slice(None), pl.ds(cols, width))]
        return pltpu.make_async_copy(down, down_ref.at[u], d_own.at[u, PIECES])

    def store_rows(u, first, v):
        c = v.shape[1]
        v = v.astype(BF).reshape(sections, hi, TILE, c)
        for s in range(sections):
            for h in range(hi):
                at, g = place(u, s, h)
                wgrad[(u,) + at + (slice(g * TILE, (g + 1) * TILE), slice(first, first + c))] = v[s, h]

    def store_down(u, first, v):
        c = v.shape[1]
        order = free_bits(u) + (D0,)
        v = v.astype(BF).reshape(1 << len(order), members * TILE, c)
        for j in range(1 << len(order)):
            value = {b: (j >> (len(order) - 1 - i)) & 1 for i, b in enumerate(order)}
            at = tuple(value[b] for b in reversed(SUM[u]))
            wgrad[(u,) + at + (slice(None), slice(first, first + c))] = v[j]

    def form(u):
        l, b = u // BLOCKS, u % BLOCKS
        q, o = 3 * width // members, 4 * width // members
        runs = 1 << len(free_bits(u))
        run = wu.shape[-1] // (members * runs)
        fixed = {bit: own[bit] for bit in GROUP[u]}

        def flat(ref, first, count):
            v = ref[u, :, :, :, first:first + count]
            return v.reshape(members * frames * READ, count)

        def up_run(j):
            at = {bit: (j >> (len(free_bits(u)) - 1 - i)) & 1 for i, bit in enumerate(free_bits(u))} | fixed
            w = wd[1 - l, b, 2 * at[S1] + at[S0], at[D2], at[D1]]
            return w.reshape(-1, w.shape[-1])

        def down_run(j):
            start = pl.multiple_of(run_start(run, u, j, fixed), run)
            return weight(wu, 1 - l, b, *every, pl.ds(start, run))

        u_all, dh_all = flat(all_f, 2 * width, width), flat(part_b, o, width)
        up_rows = jnp.concatenate([up_run(j) for j in range(runs)], axis=0)
        down_cols = jnp.concatenate([down_run(j) for j in range(runs)], axis=1)
        lift, slope = gelu_and_slope(nt(u_all, up_rows))
        dup = (nn(dh_all, down_cols) * slope).astype(BF)
        store_rows(u, 0, tn(flat(all_f, 0, width), flat(part_b, 0, q)))
        store_rows(u, q, tn(flat(all_f, width, width), flat(part_b, q, o - q)))
        store_rows(u, o, tn(u_all, dup))
        store_down(u, cols, tn(lift.astype(BF), dh_all))
        for p in range(PIECES):
            halving_copy(u, 0, p).start()

    def halve_small(l, k):
        if k < 0:
            for c in small_copies(l):
                c.wait_recv()
            total = small_t[l, here[l * BLOCKS]]
            for x in range(1, members):
                total = total + small_in[l, member(l * BLOCKS, x)]
            small_sum[l] = total
        else:
            small_halving_copy(l, k).wait_recv()
            at = (l,) + halves(l * BLOCKS, k, False)
            small_sum[at] = small_sum[at] + small_into[k][l]
        if k + 1 < bits:
            small_halving_copy(l, k + 1).start()
        else:
            small_ref[l] = small_sum[(l,) + own_at(l * BLOCKS)]

    def halve(u, k, p):
        halving_copy(u, k, p).wait_recv()
        at = (u,) + halves(u, k, False) + piece(p)
        wgrad[at] = wgrad[at] + into[k][(u,) + (slice(None),) * (bits - 1 - k) + piece(p)]
        if k + 1 < bits:
            halving_copy(u, k + 1, p).start()
        elif u != lbs - 1:
            send_rows(u, p)

    def send_rows(u, p):
        for c in row_copies(u, p):
            c.start()
        if p + 1 == PIECES:
            down_copy(u).start()

    def finish(u):
        for p in range(PIECES):
            for c in row_copies(u, p):
                c.wait()
        down_copy(u).wait()
        for k in range(bits):
            for p in range(PIECES):
                halving_copy(u, k, p).wait_send()
        for c in forward_copies(u, 0, frames) + backward_copies(u, 0, frames):
            c.wait_send()
        if u % BLOCKS == 0:
            l = u // BLOCKS
            for c in small_copies(l):
                c.wait_send()
            for k in range(bits):
                small_halving_copy(l, k).wait_send()

    def frame_copies():
        return [
            remote(src.at[p, 0], dst, f_send.at[k, i], f_recv.at[k, i], {"section": p})
            for k, p in enumerate(peers)
            for i, (src, dst) in enumerate(((frames_hbm, z0.at[me, tokens0]), (cot_hbm, cot_v.at[me])))
        ]

    def own_frames():
        return [
            pltpu.make_async_copy(src.at[me, 0], dst, f_own.at[i])
            for i, (src, dst) in enumerate(((frames_hbm, z0.at[me, tokens0]), (cot_hbm, cot_v.at[me])))
        ]

    def output_copies(i, src, dst):
        copies = [
            remote(src(p), dst.at[me], o_send.at[k, i], o_recv.at[k, i], {"section": p}) for k, p in enumerate(peers)
        ]
        return copies, pltpu.make_async_copy(src(me), dst.at[me], o_own.at[i])

    results = (0, lambda f: res_v.at[f], res_out)
    frame_grads = (1, lambda f: z0.at[f, tokens0], fgrad_out)

    def start_output(i, src, dst):
        copies, own = output_copies(i, src, dst)
        for c in copies + [own]:
            c.start()

    def spread_heads(v):
        return jnp.concatenate([v] * HEADS, axis=0) * mask_ref[...]

    def gather_heads(v):
        return jnp.sum((v * mask_ref[...].astype(F32)).reshape(HEADS, READ, width), axis=0)

    def live_at(f):
        return jnp.where(f < len_ref[me], 1.0, 0.0).astype(F32)

    def keep_slices(lb, f, first, v):
        c = v.shape[1] // members
        for s in range(members):
            slice_b[lb, s, f, :, first:first + c] = v[:, s * c:(s + 1) * c]

    def add_gain_grad(l, i, v):
        dsm_ref[l, READ + MEM + i:READ + MEM + i + 1, :] += jnp.sum(v, axis=0, keepdims=True)

    def gain(i):
        return gains[i:i + 1, :]

    def block_forward(lb, f, h):
        centred, r = centre(h)
        xh = centred * r
        xa[lb, f], ra[lb, f] = xh, r
        g = (xh * gain(2 + lb)).astype(BF)
        wide = (centred * gain(2 + lb)).astype(BF)
        all_f[lb, here[lb], f, :, :width] = g
        l, b = lb // BLOCKS, lb % BLOCKS
        q, k, v = ((nn(wide, weight(wq, l, b, i)) * r).astype(BF) for i in range(3))
        yield
        for i, part in enumerate((q, k, v)):
            qkv[lb, f, :, i * width:(i + 1) * width] = part
        s = nt(k, spread_heads(q)) * HEAD ** (-0.5)
        yield
        e = jnp.exp(s - jnp.max(s, axis=0, keepdims=True))
        p = e / jnp.sum(e, axis=0, keepdims=True)
        pt[lb, f] = p
        o = tn(p.astype(BF), v)
        yield
        o = gather_heads(o).astype(BF)
        all_f[lb, here[lb], f, :, width:2 * width] = o
        h = h + nn(o, weight(wo, l, b))
        yield
        centred, r = centre(h)
        xh = centred * r
        xm[lb, f], rm[lb, f] = xh, r
        u = (xh * gain(6 + lb)).astype(BF)
        wide = (centred * gain(6 + lb)).astype(BF)
        all_f[lb, here[lb], f, :, 2 * width:] = u
        x = nn(wide, weight(wu, l, b)) * r
        yield
        lift, slope = gelu_and_slope(x)
        lift, gp[lb, f] = lift.astype(BF), slope.astype(BF)
        h = h + nn(lift, weight(wd, l, b))
        yield
        return h

    def block_backward(lb, f, dh):
        l, b = lb // BLOCKS, lb % BLOCKS
        dhb = dh.astype(BF)
        for s in range(members):
            slice_b[lb, s, f, :, 4 * width // members:] = dhb
        dup = nn(dhb, weight(wu, 1 - l, b))
        yield
        dup = (dup * gp[lb, f].astype(F32)).astype(BF)
        du = nn(dup, weight(wd, 1 - l, b))
        yield
        xh = xm[lb, f]
        add_gain_grad(lb // BLOCKS, 3 + lb % BLOCKS, du * xh)
        dh = dh + normalize_back(du * gain(6 + lb), xh, rm[lb, f])
        dhb = dh.astype(BF)
        keep_slices(lb, f, 3 * width // members, dhb)
        do = nn(dhb, weight(wo, 1 - l, b))
        yield
        do = spread_heads(do.astype(BF))
        joined = qkv[lb, f]
        q, k, v = joined[:, :width], joined[:, width:2 * width], joined[:, 2 * width:]
        p = pt[lb, f]
        dp = nt(v, do)
        yield
        ds = (p * (dp - jnp.sum(p * dp, axis=0, keepdims=True)) * HEAD ** (-0.5)).astype(BF)
        dv = nn(p.astype(BF), do)
        dk = nn(ds, spread_heads(q))
        dq = tn(ds, k)
        yield
        dq = gather_heads(dq)
        dj = [d.astype(BF) for d in (dq, dk, dv)]
        keep_slices(lb, f, 0, jnp.concatenate(dj, axis=1))
        dg = sum(nn(d, weight(wq, 1 - l, b, i)) for i, d in enumerate(dj))
        yield
        xh = xa[lb, f]
        add_gain_grad(lb // BLOCKS, 1 + lb % BLOCKS, dg * xh)
        return dh + normalize_back(dg * gain(2 + lb), xh, ra[lb, f])

    def layer_forward(l, f, z, xh_ref, rs_ref, at, bt, mem, read_inputs, store):
        live = live_at(f)
        inputs = read_inputs(f)
        m = mem[...]
        rows = z.shape[1] - READ
        n_in = rows - MEM
        if inputs is not None:
            z[f, :n_in] = inputs
        z[f, n_in:rows] = m.astype(BF)
        zz = z[f, :rows]
        xh, r = normalize(zz.astype(F32))
        xh_ref[f, :rows], rs_ref[f, :rows] = xh, r
        n = (xh * gain(l)).astype(BF)
        logits = nt(rw_ref[l], n)
        yield
        a = softmax_lanes(logits)
        at[f] = a
        h = nn(a.astype(BF), zz)
        yield
        for b in range(BLOCKS):
            h = yield from block_forward(l * BLOCKS + b, f, h)
        y = h.astype(BF)
        z[f, rows:] = y
        xh, r = normalize(y.astype(F32))
        xh_ref[f, rows:], rs_ref[f, rows:] = xh, r
        n = (xh_ref[f] * gain(10 + l)).astype(BF)
        logits = nt(ww_ref[l], n)
        yield
        b = softmax_lanes(logits)
        bt[f] = b
        written = nn(b.astype(BF), z[f])
        yield
        rate = dec_col[l]
        updated = rate * z[f, n_in:rows].astype(F32) + (1.0 - rate) * written
        mem[...] = live * updated + (1.0 - live) * m
        store(f, (live * y.astype(F32)).astype(BF))

    def layer_backward(l, f, z, xh_ref, rs_ref, at, bt, dmem, read_grad, store, middle=None):
        live = live_at(f)
        rows = z.shape[1] - READ
        n_in = rows - MEM
        later = n_in if l == 0 else 0
        dm = dmem[...]
        rate = dec_col[l]
        dt = ((live * (1.0 - rate)) * dm).astype(BF)
        zf = z[f]
        b = bt[f]
        dl = nt(dt, zf)
        yield
        dl = softmax_lanes_back(b, dl).astype(BF)
        dz = tn(b[:, later:].astype(BF), dt)
        dn = tn(dl[:, later:], ww_ref[l])
        yield
        xh = xh_ref[f, later:]
        if l == 0:
            dt_kept[f], dlw_kept[f] = dt, dl
        else:
            dsm_ref[l, READ:READ + MEM] += nn(dl, (xh * gain(10 + l)).astype(BF))
        add_gain_grad(l, 5, dn * xh)
        dx = dn * gain(10 + l)
        tail = rows - later
        dy = dz[tail:] + normalize_back(dx[tail:], xh[tail:], rs_ref[f, rows:]) + live * read_grad(f)
        dh = dy.astype(BF).astype(F32)
        for bb in range(BLOCKS - 1, -1, -1):
            dh = yield from block_backward(l * BLOCKS + bb, f, dh)
            if bb and middle is not None:
                middle()
        ds = dh.astype(BF)
        xh = xh[:tail]
        a = at[f]
        dl = nt(ds, zf[:rows])
        yield
        dl = softmax_lanes_back(a, dl).astype(BF)
        dz = dz[:tail] + tn(a[:, later:].astype(BF), ds)
        dn = tn(dl[:, later:], rw_ref[l])
        yield
        if l == 0:
            ds_kept[f], dlr_kept[f] = ds, dl
        else:
            dsm_ref[l, :READ] += nn(dl, (xh * gain(l)).astype(BF))
        add_gain_grad(l, 0, dn * xh)
        dz = dz + normalize_back(dx[:tail] + dn * gain(l), xh, rs_ref[f, later:rows])
        dmq = (dz[n_in - later:] + (live * rate) * dm).astype(BF).astype(F32)
        dmem[...] = dmq + (1.0 - live) * dm
        store(f, dz[:n_in].astype(BF))

    def frame_backward(f):
        rows = z0.shape[1] - READ
        n_in = rows - MEM
        dlw, dlr = dlw_kept[f], dlr_kept[f]
        xh = xh0[f]
        dsm_ref[0, READ:READ + MEM] += nn(dlw, (xh * gain(10)).astype(BF))
        dsm_ref[0, :READ] += nn(dlr, (xh[:rows] * gain(0)).astype(BF))
        xh = xh[:n_in]
        dz = tn(bt0[f][:, :n_in].astype(BF), dt_kept[f]) + tn(at0[f][:, :n_in].astype(BF), ds_kept[f])
        dnw, dnr = tn(dlw[:, :n_in], ww_ref[0]), tn(dlr[:, :n_in], rw_ref[0])
        add_gain_grad(0, 5, dnw * xh)
        add_gain_grad(0, 0, dnr * xh)
        z0[f, tokens0] = (dz + normalize_back(dnw * gain(10) + dnr * gain(0), xh, rs0[f, :n_in])).astype(BF)

    for c in own_frames():
        c.start()
    loads = [[c for b in range(BLOCKS) for c in weight_copies(l, b, l, w_sem)] for l in range(LAYERS)]
    for c in loads[1] + loads[0]:
        c.start()
    row = lax.broadcasted_iota(jnp.int32, (HEADS * READ, width), 0) // READ
    col = lax.broadcasted_iota(jnp.int32, (HEADS * READ, width), 1) // HEAD
    mask_ref[...] = jnp.where(row == col, 1.0, 0.0).astype(BF)
    dsm_ref[...] = jnp.zeros_like(dsm_ref)
    for l in range(LAYERS):
        gains[l:l + 1] = rg_ref[...].astype(F32)[l:l + 1]
        gains[10 + l:11 + l] = wg_ref[...].astype(F32)[l:l + 1]
        for b in range(BLOCKS):
            lb = l * BLOCKS + b
            gains[2 + lb:3 + lb] = na_ref[l].astype(F32)[b:b + 1]
            gains[6 + lb:7 + lb] = nm_ref[l].astype(F32)[b:b + 1]
        spread = jnp.broadcast_to(decay_ref[l:l + 1], (MEM, MEM))
        diagonal = lax.broadcasted_iota(jnp.int32, (MEM, MEM), 0) == lax.broadcasted_iota(jnp.int32, (MEM, MEM), 1)
        dec_col[l] = jnp.sum(jnp.where(diagonal, spread, 0.0), axis=1, keepdims=True)

    pl.semaphore_wait(barrier, len(partners))
    for c in frame_copies():
        c.start()

    def together(*chains):
        chains = list(chains)
        while chains:
            for c in list(chains):
                try:
                    next(c)
                except StopIteration:
                    chains.remove(c)

    def keep(ref):
        def store(f, v):
            ref[f] = v

        return store

    kept0 = (z0, xh0, rs0, at0, bt0)
    kept1 = (z1, xh1, rs1, at1, bt1)

    for c in loads[1]:
        c.wait()
    lax.fori_loop(0, BLOCKS, transpose_block, 0)
    for c in loads[0]:
        c.wait()
    for c in own_frames():
        c.wait()
    for c in frame_copies():
        c.wait_recv()
    mem0[...] = jnp.zeros_like(mem0)
    mem1[...] = jnp.zeros_like(mem1)

    def chain0(f):
        return layer_forward(0, f, *kept0, mem0, lambda f: None, keep(dout))

    def chain1(f):
        return layer_forward(1, f, *kept1, mem1, lambda f: dout[f], keep(res_v))

    def send_forward(l, f):
        for b in range(BLOCKS):
            start_forward(l * BLOCKS + b, f)

    def forward(f, carry):
        together(chain0(f), chain1(f - 1))
        send_forward(0, f)
        send_forward(1, f - 1)
        return carry

    together(chain0(0))
    send_forward(0, 0)
    lax.fori_loop(1, frames, forward, 0)
    for c in transposed_copies():
        c.start()
    together(chain1(frames - 1))
    send_forward(1, frames - 1)
    again = [c for b in range(BLOCKS) for c in weight_copies(0, b, 1, x_sem)]
    for c in again:
        c.start()
    for c in transposed_copies():
        c.wait()
    start_output(*results)
    dmem0[...] = jnp.zeros_like(dmem0)
    dmem1[...] = jnp.zeros_like(dmem1)

    def back0(f, middle=None):
        return layer_backward(0, f, *kept0, dmem0, lambda f: dout[f].astype(F32), lambda f, v: None, middle)

    def back1(f):
        return layer_backward(1, f, *kept1, dmem1, lambda f: cot_v[f].astype(F32), keep(dout))

    def send_backward(l, f):
        for b in range(BLOCKS - 1, -1, -1):
            start_backward(l * BLOCKS + b, f)

    def backward(i, carry):
        f = frames - 1 - i
        together(back1(f), back0(f + 1))
        send_backward(1, f)
        send_backward(0, f + 1)
        return carry

    together(back1(frames - 1))
    send_backward(1, frames - 1)
    for c in again:
        c.wait()
    lax.fori_loop(0, BLOCKS, transpose_here, 0)
    lax.fori_loop(1, frames, backward, 0)

    def beside():
        start_small(1)
        yield
        for f in range(frames - 1, 0, -1):
            yield
            frame_backward(f)
            yield

    together(back0(0, lambda: start_backward(1, 0)), beside())
    start_backward(0, 0)
    frame_backward(0)
    start_small(0)
    for u in (3, 2):
        wait_factors(u)
        form(u)
    halve_small(1, -1)
    halve_small(1, 0)
    for u in (3, 2):
        for p in range(PIECES):
            halve(u, 0, p)
    for u in (1, 0):
        wait_factors(u)
        form(u)
    halve_small(0, -1)
    for p in range(PIECES):
        halve(1, 0, p)
    halve_small(0, 0)
    for p in range(PIECES):
        halve(0, 0, p)
    start_output(*frame_grads)
    halve_small(1, 1)
    halve(3, 1, 0)
    halve(2, 1, 0)
    halve(3, 1, 1)
    halve(2, 1, 1)
    halve(3, 2, 0)
    halve(2, 2, 0)
    halve(3, 1, 2)
    halve(2, 1, 2)
    halve_small(0, 1)
    halve(3, 2, 1)
    halve(2, 2, 1)
    halve_small(1, 2)
    halve(1, 1, 0)
    halve(0, 1, 0)
    halve(3, 2, 2)
    halve(2, 2, 2)
    halve(1, 1, 1)
    halve(0, 1, 1)
    halve(1, 2, 0)
    halve(0, 2, 0)
    halve(1, 1, 2)
    halve(0, 1, 2)
    for p in range(PIECES):
        send_rows(lbs - 1, p)
    halve(1, 2, 1)
    halve(0, 2, 1)
    halve_small(0, 2)
    halve(1, 2, 2)
    halve(0, 2, 2)
    for u in range(lbs - 1, -1, -1):
        finish(u)
    for out in (results, frame_grads):
        copies, own = output_copies(*out)
        for c in copies + [own]:
            c.wait()
    for c in frame_copies():
        c.wait_send()


def run_fused(sections, hi, lo, lengths, decay, gains, small, frames, cot, weights):
    count, _, tok, width = frames.shape
    lbs = LAYERS * BLOCKS
    ff = weights[2].shape[-1]
    cols = (4 * width + ff) // sections
    all_cols = cols + width
    bits = hi.bit_length() - 1
    chunk = sections * TILE
    peers = sections - 1
    vm, anym = pl.BlockSpec(memory_space=pltpu.VMEM), pl.BlockSpec(memory_space=pl.ANY)
    v, dma = pltpu.VMEM, pltpu.SemaphoreType.DMA

    def sds(shape, dtype):
        return jax.ShapeDtypeStruct(shape, dtype)

    def per(c, dtype):
        return v((lbs, count, READ, c), dtype)

    def by_section(c):
        return v((lbs, sections, count, READ, c), BF)

    rows0, rows1 = tok + MEM, READ + MEM
    lead, block = (LAYERS, BLOCKS), (2,) * bits + (width // hi,)
    transposed = [lead + (3,) + block + (width,), lead + block + (width,), lead + block + (ff,), lead + (ff // width,) + block + (width,)]
    weights = [weights[0].reshape(lead + block + (3 * width,))] + [w.reshape(s) for w, s in zip(weights[1:], transposed[1:])]
    scratch = [v(s, BF) for s in transposed]
    scratch += [v((count, READ, width), BF), v((count, READ, width), BF)]
    scratch += [v((count, r + READ, width), BF) for r in (rows0, rows1)]
    scratch += [v((count, r + READ, width), F32) for r in (rows0, rows1)]
    scratch += [v((count, r + READ, 1), F32) for r in (rows0, rows1)]
    scratch += [v((count, READ, r), F32) for r in (rows0, rows1)]
    scratch += [v((count, MEM, r + READ), F32) for r in (rows0, rows1)]
    scratch += [v((MEM, width), F32)] * 4
    scratch += [v((count, MEM, width), BF), v((count, READ, width), BF)]
    scratch += [v((count, MEM, rows0 + READ), BF), v((count, READ, rows0), BF), v((count, READ, width), BF)]
    scratch += [per(width, F32), per(1, F32), per(width, F32), per(1, F32)]
    scratch += [per(ff, BF), per(3 * width, BF), per(HEADS * READ, F32)]
    scratch += [v((HEADS * READ, width), BF), v((12, width), F32), v((LAYERS, MEM, 1), F32)]
    scratch += [v((LAYERS, SMALL, width), F32)]
    sliced = 4 * width // sections + width
    scratch += [by_section(sliced), by_section(3 * width), by_section(sliced)]
    scratch += [v((lbs,) + (2,) * bits + (chunk, all_cols), BF)]
    scratch += [[v((lbs,) + (2,) * (bits - 1 - k) + (chunk, all_cols), BF) for k in range(bits)]]
    scratch += [v((LAYERS, sections) + (2,) * bits + (TILE, SMALL), F32)] * 2
    scratch += [v((LAYERS,) + (2,) * bits + (TILE, SMALL), F32)]
    scratch += [[v((LAYERS,) + (2,) * (bits - 1 - k) + (TILE, SMALL), F32) for k in range(bits)]]
    scratch += [dma((LAYERS, BLOCKS, 6)), dma((LAYERS, BLOCKS, 6)), dma((BLOCKS, 12)), dma((12,))]
    scratch += [dma((peers, 2)), dma((peers, 2)), dma((2,)), dma((peers, 2)), dma((peers, 2)), dma((2,))]
    scratch += [dma((lbs, peers, 2)), dma((lbs, peers, 2)), dma((lbs,)), dma((lbs, bits, PIECES)), dma((lbs, bits, PIECES))]
    scratch += [dma((LAYERS, peers)), dma((LAYERS, peers)), dma((LAYERS, bits)), dma((LAYERS, bits))]
    scratch += [dma((lbs, PIECES, peers)), dma((lbs, PIECES, peers)), dma((lbs, PIECES + 1))]
    return pl.pallas_call(
        functools.partial(fused_kernel, hi, lo),
        out_shape=[
            sds((count, READ, width), BF),
            sds((count, tok, width), BF),
            sds((lbs, sections, TILE, cols), BF),
            sds((lbs, chunk, width), BF),
            sds((LAYERS, TILE, SMALL), F32),
        ]
        + [sds((4 + 2 * (ff // width),) + block + (width,), BF)],
        in_specs=[pl.BlockSpec(memory_space=pltpu.SMEM)] + [vm] * 7 + [anym] * 6,
        out_specs=[vm] * 5 + [anym],
        scratch_shapes=[scratch],
        compiler_params=pltpu.CompilerParams(
            collective_id=0, has_side_effects=True, vmem_limit_bytes=64 * 2**20 - 2**16
        ),
    )(lengths, decay, *gains, *small, frames, cot, *weights)[:5]


def widen_kernel(
    rows_ref, down_ref, small_ref, res_ref, fgrad_ref,
    res_out, fgrad_out, rg_out, rw_out, na_out, qkv_out, out_out, nm_out, up_out, down_out, wg_out, ww_out,
):
    sections, tile = rows_ref.shape[1:3]
    lbs = LAYERS * BLOCKS
    res_out[...] = res_ref[...]
    fgrad_out[...] = fgrad_ref[...]
    cols = [ref.shape[-1] // sections for ref in (qkv_out, out_out, up_out)]
    for u in range(lbs):
        l, b = u // BLOCKS, u % BLOCKS
        runs = 1 << len(free_bits(u))
        run = cols[2] // runs
        for s in range(sections):
            first = 0
            for ref, c in zip((qkv_out, out_out), cols):
                ref[l, b, :, s * c:(s + 1) * c] = rows_ref[u, s, :, first:first + c].astype(F32)
                first += c
            for j in range(runs):
                start = run_start(run, u, j, {bit: (s >> i) & 1 for i, bit in enumerate(GROUP[u])})
                up_out[l, b, :, start:start + run] = rows_ref[u, s, :, first + j * run:first + (j + 1) * run].astype(F32)
        down_out[l, b] = down_ref[u].astype(F32)
    diagonal = lax.broadcasted_iota(jnp.int32, (tile, tile), 0) == lax.broadcasted_iota(jnp.int32, (tile, tile), 1)

    def as_row(l, i):
        column = jnp.broadcast_to(small_ref[l][:, READ + MEM + i:READ + MEM + i + 1], (tile, tile))
        return jnp.sum(jnp.where(diagonal, column, 0.0), axis=0, keepdims=True)

    for l in range(LAYERS):
        rw_out[l] = small_ref[l][:, :READ]
        ww_out[l] = small_ref[l][:, READ:READ + MEM]
        rg_out[l:l + 1] = as_row(l, 0)
        wg_out[l:l + 1] = as_row(l, 1 + 2 * BLOCKS)
        for b in range(BLOCKS):
            na_out[l, b:b + 1] = as_row(l, 1 + b)
            nm_out[l, b:b + 1] = as_row(l, 1 + BLOCKS + b)


def widen(rows, down, sm, res, fgrad):
    sections, tile, cols = rows.shape[1:]
    width = down.shape[-1]
    vm = pl.BlockSpec(memory_space=pltpu.VMEM)

    def f32(*shape):
        return jax.ShapeDtypeStruct((LAYERS,) + shape, F32)

    out_shape = [jax.ShapeDtypeStruct(a.shape, a.dtype) for a in (res, fgrad)] + [
        f32(tile), f32(tile, READ), f32(BLOCKS, tile), f32(BLOCKS, tile, 3 * width), f32(BLOCKS, tile, width),
        f32(BLOCKS, tile), f32(BLOCKS, tile, sections * cols - 4 * width), f32(BLOCKS, *down.shape[1:]),
        f32(tile), f32(tile, MEM),
    ]
    return pl.pallas_call(
        widen_kernel, out_shape=out_shape, in_specs=[vm] * 5, out_specs=[vm] * len(out_shape)
    )(rows, down, sm, res, fgrad)


def local(
    frames, lengths, decay, read_gain, read_weight, norm_attn, w_qkv, w_out, norm_mlp, w_up, w_down,
    write_gain, write_weight, cotangent,
):
    sections, dp = lax.axis_size("section"), lax.axis_size("dp")
    clip_dev, span, tok, width = frames.shape
    hi = width // (sections * TILE)
    lo = dp // hi
    assert clip_dev == sections and span == 1 and hi * lo == dp
    res, fgrad, rows, down, sm = run_fused(
        sections, hi, lo, lengths, decay, (read_gain, norm_attn, norm_mlp, write_gain),
        [jnp.swapaxes(w, 1, 2) for w in (read_weight, write_weight)], frames, cotangent, (w_qkv, w_out, w_up, w_down),
    )
    if lo > 1:
        groups = [[h * lo + k for k in range(lo)] for h in range(hi)]

        def over_rest(v, axis):
            return lax.psum_scatter(
                v.astype(F32), "dp", scatter_dimension=axis, axis_index_groups=groups, tiled=True
            )

        rows, down, sm = over_rest(rows, 2), over_rest(down, 1), over_rest(sm, 1)
    res, fgrad, *grads = widen(rows, down, sm, res, fgrad)
    return (res[:, None], fgrad[:, None], *grads)


def solution(mesh):
    both = ("section", "dp")
    split = P("dp", "section", None, None)
    return jax.shard_map(
        local,
        mesh=mesh,
        in_specs=(split, P("dp")) + (P(),) * 11 + (split,),
        out_specs=(
            split, split, P(None, both), P(None, both, None), P(None, None, both), P(None, None, both, None),
            P(None, None, both, None), P(None, None, both), P(None, None, both, None),
            P(None, None, both, None), P(None, both), P(None, both, None),
        ),
        check_vma=False,
    )
```
